32 devices in a mesh: dp: 8 (over z, y), fsdp: 4 (over x, core).
Axes of the slice: x: 2, y: 2, z: 4, core: 2. Of those that a mesh axis runs over, the one named last changes fastest.
Arguments:
- tokens: bfloat16 [96, 256, 768], P(('dp', 'fsdp')), may hold values from -6 to 6
- qkv_weight: bfloat16 [768, 2304], P('dp', 'fsdp'), may hold values from -0.21875 to 0.21875
- out_weight: bfloat16 [768, 768], P('dp', 'fsdp'), may hold values from -0.875 to 0.875
- up_weight: bfloat16 [768, 3072], P('dp', 'fsdp'), may hold values from -0.21875 to 0.21875
- up_bias: bfloat16 [3072], P(('dp', 'fsdp')), may hold values from -1.75 to 1.75
- down_weight: bfloat16 [3072, 768], P('dp', 'fsdp'), may hold values from -0.109375 to 0.109375
- vectors: bfloat16 [8, 768], P('fsdp', 'dp'), may hold values from -1.2 to 2.2
- lengths: int32 [96], P(('dp', 'fsdp')), may hold values from 32 to 256, as said below
- exit_depth: int32 [96], P(('dp', 'fsdp')), may hold values from 0 to 1
- prefix_widths: int32 [5], replicated, may hold values from 64 to 768, as said below
- cotangent: bfloat16 [96, 256, 768], P(('dp', 'fsdp')), may hold values from -12 to 12
Outputs:
- layer_out: bfloat16 [96, 256, 768], P(('dp', 'fsdp'))
- pooled: float32 [96, 5, 768], P(('dp', 'fsdp'))
- grad_tokens: bfloat16 [96, 256, 768], P(('dp', 'fsdp'))
- grad_qkv_weight: float32 [768, 2304], P('dp', 'fsdp')
- grad_out_weight: float32 [768, 768], P('dp', 'fsdp')
- grad_up_weight: float32 [768, 3072], P('dp', 'fsdp')
- grad_up_bias: float32 [3072], P(('dp', 'fsdp'))
- grad_down_weight: float32 [3072, 768], P('dp', 'fsdp')
- grad_vectors: float32 [8, 768], P('fsdp', 'dp')
The draws below stay inside these ranges and needn't reach their ends.
Inputs may be any that keep to these rules, and one draw needn't show every extreme that they name: `lengths`: at least one sentence has all 256 slots valid and one has 32. `prefix_widths`: an order of 768, 512, 256, 128, 64.
All inputs are finite; a program needn't handle non-finite values.
Results may differ from the reference program's by a relative error of at most 0.019.
Values may be sent and summed in bfloat16 or wider, within the bound.
No kernel may reach another device: no remote copies, remote signals or barrier semaphores. Data moves between devices by JAX's collectives and lax.ppermute only.
A program may use at most 192 MiB of HBM per device.

```python
import math
import jax
import jax.numpy as jnp
from jax import lax

D = 768
HEAD_DIM = 64
FF = 3072
SEQ = 256
NPREF = 5
SENTS = 96


def draw_vectors(key, part):
    key = jax.random.fold_in(key, 2)
    base = jnp.clip(jax.random.normal(key, (8, D), jnp.float32), -4.0, 4.0) * 0.3
    gain_rows = jnp.array([0.0, 0.0, 0.0, 1.0, 0.0, 0.0, 1.0, 0.0], jnp.float32)[:, None]
    return (base + gain_rows).astype(jnp.bfloat16)


def draw_lengths(key, part):
    key = jax.random.fold_in(key, 1)
    key_len, key_pick = jax.random.split(key)
    drawn = jax.random.randint(key_len, (SENTS,), SEQ // 8, SEQ + 1, jnp.int32)
    picked = jax.random.permutation(key_pick, SENTS)
    drawn = drawn.at[picked[0]].set(SEQ)
    drawn = drawn.at[picked[1]].set(SEQ // 8)
    return drawn


def draw_prefix_widths(key, part):
    key = jax.random.fold_in(key, 3)
    table = jnp.array([D, 2 * D // 3, D // 3, D // 6, D // 12], jnp.int32)
    order = jax.random.permutation(key, NPREF)
    return table[order]


def set_ends(values, stream_key, low, high):
    longest = values.shape.index(max(values.shape))
    spots = []
    for shift in (0, 1):
        where = [jax.random.randint(jax.random.fold_in(stream_key, axis), (), 0, length) for axis, length in enumerate(values.shape)]
        where[longest] = (where[longest] + shift) % values.shape[longest]
        spots.append(tuple(where))
    return values.at[spots[0]].set(low).at[spots[1]].set(high)


def with_spikes(values, rng, source, target, blocks, factor):
    owner, partner = [(jnp.arange(values.shape[dim]) // (values.shape[dim] // blocks)).reshape([-1 if axis == dim else 1 for axis in range(values.ndim)]) for dim in (source, target)]
    chosen = jax.random.permutation(rng, blocks)[partner]
    strong = (owner == chosen) | (owner == (partner + blocks // 2) % blocks)
    return jnp.where(strong, factor * values, values)


def block_levels(key, shape, cuts, low, high):
    loudness, own = 1.0, jax.random.fold_in(key, 6)
    for axis_at, shards_of in cuts:
        steps = jnp.exp(jax.random.uniform(jax.random.fold_in(own, axis_at), (shards_of,), jnp.float32, low / len(cuts), high / len(cuts)))
        loudness = loudness * jnp.repeat(steps, shape[axis_at] // shards_of).reshape([-1 if axis == axis_at else 1 for axis in range(len(shape))])
    return loudness


def scatter_about(own_key, shape, deviation, most, pieces=(), kind=jnp.bfloat16):
    values = deviation * jax.random.normal(own_key, shape, jnp.float32)
    if pieces:
        values = values * block_levels(own_key, shape, pieces, -0.22, 0.18)
    return jnp.clip(values, -most, most).astype(kind)


def noise_with(stream_key, extent, scale, most, cuts, heavy, kind=jnp.bfloat16):
    values = scale * jax.random.normal(stream_key, extent, jnp.float32)
    if cuts:
        values = values * block_levels(stream_key, extent, cuts, -0.22, 0.18)
    return jnp.clip(with_spikes(values, jax.random.fold_in(stream_key, 3), *heavy), -most, most).astype(kind)


def setup_inputs(seed: int = 0) -> dict:
    splits = jax.random.split(jax.random.key(seed), 12)
    return {
        "tokens": scatter_about(splits[0], (SENTS, SEQ, D), 1.0, 6.0, ((0, 32),)),
        "qkv_weight": scatter_about(splits[1], (D, 3 * D), D ** -0.5, 0.21875, ((0, 8), (1, 4))),
        "out_weight": scatter_about(splits[2], (D, D), (D // 16) ** -0.5, 0.875, ((0, 8), (1, 4))),
        "up_weight": scatter_about(splits[3], (D, FF), D ** -0.5, 0.21875, ((0, 8), (1, 4))),
        "up_bias": scatter_about(splits[4], (FF,), 0.3, 1.75, ((0, 32),)),
        "down_weight": scatter_about(splits[5], (FF, D), FF ** -0.5, 0.109375, ((0, 8), (1, 4))),
        "vectors": draw_vectors(jax.random.fold_in(splits[11], 71), 0),
        "lengths": draw_lengths(jax.random.fold_in(splits[11], 71), 0),
        "exit_depth": set_ends(jax.random.randint(splits[8], (SENTS,), 0, 2), jax.random.fold_in(splits[8], 1), 0, 1).astype(jnp.int32),
        "prefix_widths": draw_prefix_widths(jax.random.fold_in(splits[11], 71), 0),
        "cotangent": noise_with(splits[10], (SENTS, SEQ, D), 1.0, 12.0, ((0, 32),), (0, 2, 32, 2.75)),
    }


EPS = 1e-05
HIGH = lax.Precision.HIGHEST

@jax.custom_vjp
def low(v):
    return lax.optimization_barrier(v.astype(jnp.bfloat16)).astype(jnp.float32)

@jax.custom_vjp
def low_back(v):
    return v

def low_keep(v):
    return (low(v), None)

def low_pass(kept, grad):
    return (grad,)

def back_keep(v):
    return (v, None)

def back_low(kept, grad):
    return (low(grad),)
low.defvjp(low_keep, low_pass)
low_back.defvjp(back_keep, back_low)

def layer_norm(hidden, norm_gain, norm_shift):
    row_mean = lax.optimization_barrier(jnp.mean(hidden, axis=-1, keepdims=True))
    centered = hidden - row_mean
    spread = lax.optimization_barrier(jnp.mean(centered * centered, axis=-1, keepdims=True))
    return centered * lax.rsqrt(spread + EPS) * norm_gain + norm_shift

def matmul(left, right):
    return jnp.dot(left, right, precision=HIGH)

def forward(inputs, w_qkv, w_out, w_up, b_up, w_down, vec_f, group_lengths):
    sent_count, seq_len, model_width = inputs.shape
    row_count = sent_count * seq_len
    flat = inputs.reshape(row_count, model_width)
    qkv_bias = jnp.concatenate([vec_f[0], jnp.zeros_like(vec_f[0]), vec_f[1]])
    joined_qkv = low_back(low(matmul(flat, w_qkv) + qkv_bias))
    head_count = model_width // HEAD_DIM
    split_parts = joined_qkv.reshape(sent_count, seq_len, 3, head_count, HEAD_DIM)
    queries = split_parts[:, :, 0]
    key_rows = split_parts[:, :, 1]
    values = split_parts[:, :, 2]
    scores = jnp.einsum('sqhd,skhd->shqk', queries, key_rows, precision=HIGH) * HEAD_DIM ** (-0.5)
    positions = lax.broadcasted_iota(jnp.int32, (sent_count, seq_len), 1)
    key_keep = (positions < group_lengths[:, None])[:, None, None, :]
    scores = low_back(jnp.where(key_keep, scores, -1000000000.0))
    row_top = lax.optimization_barrier(jnp.max(scores, axis=-1, keepdims=True))
    exponent = jnp.exp(scores - row_top)
    probs_f = exponent / lax.optimization_barrier(jnp.sum(exponent, axis=-1, keepdims=True))
    attended = jnp.einsum('shqk,skhd->sqhd', low(probs_f), values, precision=HIGH)
    attended = low_back(low(attended.reshape(row_count, model_width)))
    branch_att = low_back(matmul(attended, w_out) + vec_f[2])
    first_norm = low(layer_norm(flat + branch_att, vec_f[3], vec_f[4]))
    pre_act = low_back(matmul(first_norm, w_up) + b_up)
    activated = low(jax.nn.gelu(pre_act, approximate=False))
    branch_ffn = low_back(matmul(activated, w_down) + vec_f[5])
    result = layer_norm(first_norm + branch_ffn, vec_f[6], vec_f[7])
    return result.reshape(sent_count, seq_len, model_width)

def reference(tokens, qkv_weight, out_weight, up_weight, up_bias, down_weight, vectors, lengths, exit_depth, prefix_widths, cotangent):
    weights = tuple((item.astype(jnp.float32) for item in (qkv_weight, out_weight, up_weight, up_bias, down_weight, vectors)))
    group = math.gcd(SENTS, max(1, 4096 // SEQ))
    blocks = SENTS // group
    inputs_all = tokens.astype(jnp.float32)
    tok_groups = inputs_all.reshape(blocks, group, SEQ, D)
    len_groups = lengths.reshape(blocks, group)
    cot_groups = cotangent.astype(jnp.float32).reshape(blocks, group, SEQ, D)
    block_fn = jax.checkpoint(forward)

    def step_fn(running, block_item):
        block_in, group_lengths, block_cot = block_item

        def apply_block(layer_in, *block_weights):
            return block_fn(layer_in, *block_weights, group_lengths)
        outputs, pull = jax.vjp(apply_block, block_in, *weights)
        grads = pull(block_cot)
        summed = tuple((running_sum + new_grad for running_sum, new_grad in zip(running, grads[1:])))
        return (summed, (outputs, grads[0]))
    zeros_init = tuple((jnp.zeros_like(item) for item in weights))
    sums, (outputs_all, grad_in) = lax.scan(step_fn, zeros_init, (tok_groups, len_groups, cot_groups))
    result = outputs_all.reshape(SENTS, SEQ, D)
    grad_in = grad_in.reshape(SENTS, SEQ, D)
    positions = lax.broadcasted_iota(jnp.int32, (SENTS, SEQ), 1)
    valid_mask = (positions < lengths[:, None]).astype(jnp.float32)
    source = jnp.where((exit_depth == 1)[:, None, None], result, inputs_all)
    pooled_mean = lax.optimization_barrier(jnp.sum(valid_mask[:, :, None] * source, axis=1)) / lengths.astype(jnp.float32)[:, None]
    columns = lax.broadcasted_iota(jnp.int32, (NPREF, D), 1)
    prefix = (columns < prefix_widths[:, None]).astype(jnp.float32)
    pooled = pooled_mean[:, None, :] * prefix[None, :, :]
    return (result.astype(jnp.bfloat16), pooled, grad_in.astype(jnp.bfloat16), sums[0], sums[1], sums[2], sums[3], sums[4], sums[5])
```

```python
import itertools
from functools import partial

import jax
import jax.numpy as jnp
from jax import lax
from jax.experimental import pallas as pl
from jax.experimental.pallas import tpu as pltpu
from jax.sharding import PartitionSpec as P

HEAD_DIM = 64
EPS = 1e-05
MASKED = -1000000000.0
F32 = jnp.float32
BF16 = jnp.bfloat16
VMEM_LIMIT = 56 * 1024 * 1024
LANES = 128


class Links:
    def __init__(self, n_dp, n_fsdp):
        self.n_dp, self.n_fsdp = n_dp, n_fsdp
        self.high = n_fsdp // 4
        self.rest = (n_dp // 2) * self.high

    def number(self, rest, y, x, core):
        z, high = divmod(rest, self.high)
        return (z * 2 + y) * self.n_fsdp + (high * 2 + x) * 2 + core

    def pairs(self, step):
        return [
            (self.number(*place), self.number(*step(*place)))
            for place in itertools.product(range(self.rest), range(2), range(2), range(2))
        ]

    def move(self, value, step):
        return lax.ppermute(value, ("dp", "fsdp"), self.pairs(step))

    def core(self, value):
        return self.move(value, lambda q, y, x, c: (q, y, x, 1 - c))

    def along_x(self, value):
        return self.move(value, lambda q, y, x, c: (q, y, 1 - x, c))

    def along_y(self, value):
        return self.move(value, lambda q, y, x, c: (q, 1 - y, x, c))

    def first(self, value):
        return self.move(value, lambda q, y, x, c: (q, 1 - y, x, c) if c else (q, y, 1 - x, c))

    def second(self, value):
        return self.move(value, lambda q, y, x, c: (q, y, 1 - x, c) if c else (q, 1 - y, x, c))

    def ahead(self, value, far):
        return self.move(value, lambda q, y, x, c: ((q + far) % self.rest, y, x, c))

    def place(self):
        dp, fsdp = lax.axis_index("dp"), lax.axis_index("fsdp")
        rest = (dp // 2) * self.high + fsdp // 4
        return rest, dp % 2, (fsdp // 2) % 2, fsdp % 2


def chip_piece(links, shard, core):
    half = shard.shape[0] // 2
    keep = lax.dynamic_slice_in_dim(shard, core * half, half, 0)
    give = lax.dynamic_slice_in_dim(shard, (1 - core) * half, half, 0)
    got = links.core(give)
    return jnp.where(
        core == 0, jnp.concatenate([keep, got], axis=1), jnp.concatenate([got, keep], axis=1)
    )


def spread(links, piece):
    own = jnp.stack([piece] + [links.ahead(piece, far) for far in range(1, links.rest)])
    by_first = links.first(own)
    by_second = links.second(own)
    by_both = links.second(by_first)
    near = [own, by_second, by_first, by_both]
    return near + [links.core(item) for item in near]


def collect(links, keep, give):
    got = links.core(give)
    far_half = (keep[1].astype(F32) + got[1].astype(F32)).astype(BF16)
    by_second = links.second(far_half)

    def near(one):
        return keep[0, one].astype(F32) + got[0, one].astype(F32) + by_second[one].astype(F32)

    by_first = links.first(near(1).astype(BF16))
    blocks = [near(0)[far] + by_first[far].astype(F32) for far in range(links.rest)]
    total = blocks[0]
    for far in range(1, links.rest):
        total = total + links.ahead(blocks[far].astype(BF16), far).astype(F32)
    return total


def owned(links, piece, core):
    width = piece.shape[1] // 2
    keep = lax.dynamic_slice_in_dim(piece, core * width, width, 1)
    give = lax.dynamic_slice_in_dim(piece, (1 - core) * width, width, 1)
    got = links.core(give)
    return jnp.where(
        core == 0, jnp.concatenate([keep, got], axis=0), jnp.concatenate([got, keep], axis=0)
    )


def sum_everywhere(links, value):
    value = value + links.core(value)
    value = value + links.along_x(value)
    value = value + links.along_y(value)
    total = value
    for far in range(1, links.rest):
        total = total + links.ahead(value, far)
    return total


class Blocks:
    def __init__(self, links, where):
        self.links = links
        self.rest, self.y, self.x, self.core = where[0], where[1], where[2], where[3]

    def device(self, other, one, two, far, sign):
        links = self.links
        core = jnp.bitwise_xor(self.core, other)
        flip_x = jnp.where(core == 0, one, two)
        flip_y = jnp.where(core == 0, two, one)
        rest = lax.rem(self.rest + (sign * far + links.rest), links.rest)
        x, y = jnp.bitwise_xor(self.x, flip_x), jnp.bitwise_xor(self.y, flip_y)
        dp = lax.div(rest, links.high) * 2 + y
        return dp, lax.rem(rest, links.high) * 2 + x, core

    def corner(self, rows, cols, *spot):
        dp, wide, core = self.device(*spot)
        return pl.multiple_of((dp * 2 + core) * rows, rows), pl.multiple_of(wide * cols, cols)


def load_weight(links, where, refs, first_col, cols, out, sem):
    if len(refs) == 1:
        copies = [pltpu.make_async_copy(refs[0], out, sem)]
    else:
        blocks = Blocks(links, where)
        rows = refs[0].shape[1]
        copies = []
        for stack, far in itertools.product(range(8), range(links.rest)):
            row, col = blocks.corner(
                rows, cols, stack // 4, (stack // 2) % 2, stack % 2, far, -1
            )
            copies.append(
                pltpu.make_async_copy(
                    refs[stack].at[far, :, pl.ds(first_col, cols)],
                    out.at[pl.ds(row, rows), pl.ds(col, cols)],
                    sem,
                )
            )
    for copy in copies:
        copy.start()
    return copies


def store_grad(links, where, grad, refs, first_col, cols, sem):
    if len(refs) == 1:
        copies = [pltpu.make_async_copy(grad, refs[0], sem)]
    else:
        blocks = Blocks(links, where)
        rows = refs[0].shape[3]
        copies = []
        for other, one, two, far in itertools.product(
            range(2), range(2), range(2), range(links.rest)
        ):
            row, col = blocks.corner(rows, cols, other, one, two, far, 1)
            copies.append(
                pltpu.make_async_copy(
                    grad.at[pl.ds(row, rows), pl.ds(col, cols)],
                    refs[other].at[two, one, far, :, pl.ds(first_col, cols)],
                    sem,
                )
            )
    for copy in copies:
        copy.start()
    return copies


def wait_all(copies):
    for copy in copies:
        copy.wait()


def dot(left, right):
    return lax.dot_general(left, right, (((1,), (0,)), ((), ())), preferred_element_type=F32)


def dot_nt(left, right):
    return lax.dot_general(left, right, (((1,), (1,)), ((), ())), preferred_element_type=F32)


def dot_tn(left, right):
    return lax.dot_general(left, right, (((0,), (0,)), ((), ())), preferred_element_type=F32)


def normalize(hidden):
    centered = hidden - jnp.mean(hidden, axis=-1, keepdims=True)
    factor = lax.rsqrt(jnp.mean(centered * centered, axis=-1, keepdims=True) + EPS)
    return centered * factor, factor


def norm_back(scaled, normed, factor):
    return factor * (
        scaled
        - jnp.mean(scaled, axis=-1, keepdims=True)
        - normed * jnp.mean(scaled * normed, axis=-1, keepdims=True)
    )


def gelu_parts(value):
    size = jnp.abs(value) * 0.7071067811865476
    bell = jnp.exp(-0.5 * value * value)
    part = 1.0 / (1.0 + 0.3275911 * size)
    poly = part * (
        0.127414796
        + part * (-0.142248368 + part * (0.7107068705 + part * (-0.7265760135 + part * 0.5307027145)))
    )
    tail = poly * bell
    weight = jnp.where(value > 0.0, 1.0 - tail, tail)
    return value * weight, weight + value * (bell * 0.3989422804014327)


def small_kernel(links, where, *refs):
    stacks, vec_out, bias_out, held, sem = refs[:8], *refs[8:]
    blocks = Blocks(links, where)
    first_col = stacks[0].shape[2] - LANES
    copies = []
    for stack, far in itertools.product(range(8), range(links.rest)):
        dp, wide, core = blocks.device(stack // 4, (stack // 2) % 2, stack % 2, far, -1)
        copies.append(
            pltpu.make_async_copy(
                stacks[stack].at[far, pl.ds(0, 16), pl.ds(first_col, LANES)],
                held.at[dp * links.n_fsdp + wide * 2 + core],
                sem,
            )
        )
    for copy in copies:
        copy.start()
    wait_all(copies)
    rows, width = 8 // links.n_fsdp, vec_out.shape[1] // links.n_dp
    got = [held[at].astype(F32)[:, :width] for at in range(links.n_dp * links.n_fsdp)]
    for fsdp in range(links.n_fsdp):
        line = jnp.concatenate([got[dp * links.n_fsdp + fsdp] for dp in range(links.n_dp)], axis=1)
        vec_out[pl.ds(rows * fsdp, rows), :] = line[:rows]
    bias_out[...] = jnp.concatenate(got, axis=1)[rows : rows + 1]


def head_half(pair, half):
    lane = lax.broadcasted_iota(jnp.int32, pair.shape, 1)
    keep = (lane < HEAD_DIM) if half == 0 else (lane >= HEAD_DIM)
    return jnp.where(keep, pair, jnp.zeros_like(pair))


def join_halves(low, high):
    lane = lax.broadcasted_iota(jnp.int32, low.shape, 1)
    return jnp.where(lane < HEAD_DIM, low, high)


def attend_kernel(links, n_weight, where, lengths, tokens, vec, *refs):
    weight_refs = refs[:n_weight]
    out_refs = refs[n_weight : 2 * n_weight]
    qkv, attended, first_norm, normed, factor = refs[2 * n_weight : 2 * n_weight + 5]
    w_qkv, w_out, sems = refs[2 * n_weight + 5 :]
    width = tokens.shape[1]
    seq = 256
    sents = tokens.shape[0] // seq
    wide = width * 3 * 2 // links.n_fsdp
    copies = load_weight(links, where, weight_refs, 0, wide, w_qkv, sems.at[0])
    copies_out = load_weight(
        links, where, out_refs, wide, width * 2 // links.n_fsdp, w_out, sems.at[1]
    )
    wait_all(copies)

    def project(tile, carry):
        at = pl.ds(pl.multiple_of(tile * 256, 256), 256)
        product = dot(tokens[...], w_qkv[:, at])
        place = tile * 256
        row = jnp.where(place < width, 0, 1)
        col = pl.multiple_of(lax.rem(place, width), 256)
        bias = vec[pl.ds(row, 1), pl.ds(col, 256)]
        bias = jnp.where((place >= width) & (place < 2 * width), 0.0, bias)
        qkv[:, at] = (product + bias).astype(BF16)
        return carry

    lax.fori_loop(0, 3 * width // 256, project, 0)

    pairs = width // LANES

    def attend(step, carry):
        sent, pair = lax.div(step, pairs), lax.rem(step, pairs)
        rows = pl.ds(pl.multiple_of(sent * seq, seq), seq)
        col = pl.multiple_of(pair * LANES, LANES)
        queries = qkv[rows, pl.ds(col, LANES)]
        keys = qkv[rows, pl.ds(col + width, LANES)]
        values = qkv[rows, pl.ds(col + 2 * width, LANES)]
        queries = queries * jnp.asarray(HEAD_DIM ** (-0.5), BF16)
        keep = lax.broadcasted_iota(jnp.int32, (seq, seq), 1) < lengths[sent]
        outs = []
        for half in range(2):
            scores = jnp.where(keep, dot_nt(head_half(queries, half), keys), MASKED)
            exponent = jnp.exp(scores - jnp.max(scores, axis=-1, keepdims=True))
            scale = 1.0 / jnp.sum(exponent, axis=-1, keepdims=True)
            outs.append(dot((exponent * scale).astype(BF16), values))
        attended[rows, pl.ds(col, LANES)] = join_halves(*outs).astype(BF16)
        return carry

    lax.fori_loop(0, sents * pairs, attend, 0)
    wait_all(copies_out)
    for sent in range(sents):
        rows = pl.ds(sent * seq, seq)
        hidden = tokens[rows, :].astype(F32) + (dot(attended[rows, :], w_out[...]) + vec[2:3, :])
        part, scale = normalize(hidden)
        normed[rows, :] = part
        factor[rows, :] = jnp.broadcast_to(scale, (seq, LANES))
        first_norm[rows, :] = (part * vec[3:4, :] + vec[4:5, :]).astype(BF16)


def up_kernel(links, n_weight, where, first_norm, bias, *refs):
    weight_refs = refs[:n_weight]
    activated, slope = refs[n_weight : n_weight + 2]
    w_up, act_buf, slope_buf, sems, out_sems = refs[n_weight + 2 :]
    width, hidden = w_up.shape
    copies = load_weight(links, where, weight_refs, 0, hidden * 2 // links.n_fsdp, w_up, sems.at[0])
    wait_all(copies)
    tile = 256
    count = hidden // tile

    def out_copies(step):
        at = pl.ds(pl.multiple_of(step * tile, tile), tile)
        slot = lax.rem(step, 2)
        return (
            pltpu.make_async_copy(act_buf.at[slot], activated.at[:, at], out_sems.at[slot, 0]),
            pltpu.make_async_copy(slope_buf.at[slot], slope.at[:, at], out_sems.at[slot, 1]),
        )

    def body(step, carry):
        at = pl.ds(pl.multiple_of(step * tile, tile), tile)
        slot = lax.rem(step, 2)

        @pl.when(step >= 2)
        def _():
            wait_all(out_copies(step - 2))

        for part in range(first_norm.shape[0] // 256):
            rows = pl.ds(part * 256, 256)
            value = dot(first_norm[rows, :], w_up[:, at]) + bias[:, at]
            act, der = gelu_parts(value)
            act_buf[slot, rows, :] = act.astype(BF16)
            slope_buf[slot, rows, :] = der.astype(BF16)
        for copy in out_copies(step):
            copy.start()
        return carry

    lax.fori_loop(0, count, body, 0)
    wait_all(out_copies(count - 2))
    wait_all(out_copies(count - 1))


def down_kernel(links, n_weight, n_grad, where, lengths, depth, prefix, *refs):
    activated, first_norm, tokens, cotangent, vec = refs[:5]
    weight_refs = refs[5 : 5 + n_weight]
    layer_out, pooled, d_second, d_down, sums = refs[5 + n_weight : 10 + n_weight]
    grad_refs = refs[10 + n_weight : 10 + n_weight + n_grad]
    w_down, grad, sems = refs[10 + n_weight + n_grad :]
    hidden, width = w_down.shape
    seq = 256
    sents = tokens.shape[0] // seq
    cols = width * 2 // links.n_fsdp
    wait_all(load_weight(links, where, weight_refs, 0, cols, w_down, sems.at[0]))
    sums[...] = jnp.zeros_like(sums)
    columns = lax.broadcasted_iota(jnp.int32, (1, width), 1)
    for sent in range(sents):
        rows = pl.ds(sent * seq, seq)
        total = first_norm[rows, :].astype(F32) + (dot(activated[rows, :], w_down[...]) + vec[5:6, :])
        normed, factor = normalize(total)
        result = normed * vec[6:7, :] + vec[7:8, :]
        layer_out[rows, :] = result.astype(BF16)
        valid = lax.broadcasted_iota(jnp.int32, (seq, width), 0) < lengths[sent]
        source = jnp.where(depth[sent] == 1, result, tokens[rows, :].astype(F32))
        mean = jnp.sum(jnp.where(valid, source, 0.0), axis=0, keepdims=True)
        mean = mean / lengths[sent].astype(F32)
        for at in range(pooled.shape[1]):
            pooled[sent, pl.ds(at, 1), :] = mean * (columns < prefix[at]).astype(F32)
        grad_in = cotangent[rows, :].astype(F32)
        sums[0:1, :] += jnp.sum(grad_in * normed, axis=0, keepdims=True)
        sums[1:2, :] += jnp.sum(grad_in, axis=0, keepdims=True)
        back = norm_back(grad_in * vec[6:7, :], normed, factor)
        d_second[rows, :] = back
        low = back.astype(BF16)
        d_down[rows, :] = low
        sums[2:3, :] += jnp.sum(low.astype(F32), axis=0, keepdims=True)

    def body(step, carry):
        at = pl.ds(pl.multiple_of(step * 256, 256), 256)
        grad[at, :] = dot_tn(activated[:, at], d_down[...]).astype(BF16)
        return carry

    lax.fori_loop(0, hidden // 256, body, 0)
    wait_all(store_grad(links, where, grad, grad_refs, 0, cols, sems.at[1]))


def up_back_kernel(links, n_weight, n_grad, where, d_down, slope, first_norm, *refs):
    weight_refs = refs[:n_weight]
    d_pre, sums = refs[n_weight : n_weight + 2]
    grad_refs = refs[n_weight + 2 : n_weight + 2 + n_grad]
    w_down, turned, grad, sems = refs[n_weight + 2 + n_grad :]
    hidden, width = w_down.shape
    copies = load_weight(links, where, weight_refs, 0, width * 2 // links.n_fsdp, w_down, sems.at[0])
    turned[...] = first_norm[...].T
    wait_all(copies)

    def body(step, carry):
        at = pl.ds(pl.multiple_of(step * 256, 256), 256)
        d_act = dot_nt(d_down[...], w_down[at, :])
        low = (d_act * slope[:, at].astype(F32)).astype(BF16)
        d_pre[:, at] = low
        sums[:, at] = jnp.sum(low.astype(F32), axis=0, keepdims=True)
        grad[:, at] = dot(turned[...], low).astype(BF16)
        return carry

    lax.fori_loop(0, hidden // 256, body, 0)
    wait_all(store_grad(links, where, grad, grad_refs, 0, hidden * 2 // links.n_fsdp, sems.at[1]))


def out_back_kernel(links, n_weight, where, *refs):
    d_pre, d_second, normed, factor, attended, vec = refs[:6]
    up_refs = refs[6 : 6 + n_weight]
    out_refs = refs[6 + n_weight : 6 + 2 * n_weight]
    d_resid, d_att, grad_out, sums = refs[6 + 2 * n_weight : 10 + 2 * n_weight]
    w_up, w_out, d_attn, sems = refs[10 + 2 * n_weight :]
    width, hidden = w_up.shape
    seq = 256
    wide = width * 3 * 2 // links.n_fsdp
    copies = load_weight(links, where, up_refs, 0, hidden * 2 // links.n_fsdp, w_up, sems.at[0])
    copies_out = load_weight(
        links, where, out_refs, wide, width * 2 // links.n_fsdp, w_out, sems.at[1]
    )
    wait_all(copies)
    sums[...] = jnp.zeros_like(sums)
    for part in range(d_pre.shape[0] // seq):
        rows = pl.ds(part * seq, seq)
        d_first = dot_nt(d_pre[rows, :], w_up[...]) + d_second[rows, :]
        unit = normed[rows, :]
        sums[0:1, :] += jnp.sum(d_first * unit, axis=0, keepdims=True)
        sums[1:2, :] += jnp.sum(d_first, axis=0, keepdims=True)
        back = norm_back(d_first * vec[3:4, :], unit, factor[rows, 0:1])
        d_resid[rows, :] = back
        low = back.astype(BF16)
        d_attn[rows, :] = low
        sums[2:3, :] += jnp.sum(low.astype(F32), axis=0, keepdims=True)
    wait_all(copies_out)
    d_att[...] = dot_nt(d_attn[...], w_out[...]).astype(BF16)
    grad_out[...] = dot_tn(attended[...], d_attn[...]).astype(BF16)


def attend_back_kernel(links, n_grad, where, lengths, qkv, d_att, tokens, grad_out, *refs):
    d_qkv, sums = refs[:2]
    grad_refs = refs[2 : 2 + n_grad]
    turned, grad, sems = refs[2 + n_grad :]
    width = tokens.shape[1]
    seq = 256
    sents = tokens.shape[0] // seq
    pairs = width // LANES
    wide = width * 3 * 2 // links.n_fsdp
    if n_grad == 2:
        copies = store_grad(
            links, where, grad_out, grad_refs, wide, width * 2 // links.n_fsdp, sems.at[0]
        )
    else:
        copies = []
    turned[...] = tokens[...].T
    sums[...] = jnp.zeros_like(sums)
    key_scale = jnp.asarray(HEAD_DIM ** (-0.5), BF16)

    def body(step, carry):
        sent, pair = lax.div(step, pairs), lax.rem(step, pairs)
        rows = pl.ds(pl.multiple_of(sent * seq, seq), seq)
        col = pl.multiple_of(pair * LANES, LANES)
        queries = qkv[rows, pl.ds(col, LANES)] * key_scale
        keys = qkv[rows, pl.ds(col + width, LANES)]
        values = qkv[rows, pl.ds(col + 2 * width, LANES)]
        d_out = d_att[rows, pl.ds(col, LANES)]
        keep = lax.broadcasted_iota(jnp.int32, (seq, seq), 0) < lengths[sent]
        d_queries, d_keys, d_values = [], [], []
        for half in range(2):
            scores = jnp.where(keep, dot_nt(keys, head_half(queries, half)), MASKED)
            exponent = jnp.exp(scores - jnp.max(scores, axis=0, keepdims=True))
            probs = exponent * (1.0 / jnp.sum(exponent, axis=0, keepdims=True))
            d_values.append(dot(probs.astype(BF16), d_out))
            d_probs = dot_nt(values, head_half(d_out, half))
            row_dot = jnp.sum(d_probs * probs, axis=0, keepdims=True)
            d_scores = (probs * (d_probs - row_dot)).astype(BF16)
            d_keys.append(dot(d_scores, queries))
            d_queries.append(dot_tn(d_scores, keys))
        d_query = (join_halves(*d_queries) * (HEAD_DIM ** (-0.5))).astype(BF16)
        d_value = join_halves(*d_values).astype(BF16)
        d_qkv[rows, pl.ds(col, LANES)] = d_query
        d_qkv[rows, pl.ds(col + width, LANES)] = join_halves(*d_keys).astype(BF16)
        d_qkv[rows, pl.ds(col + 2 * width, LANES)] = d_value
        sums[0:1, pl.ds(col, LANES)] += jnp.sum(d_query.astype(F32), axis=0, keepdims=True)
        sums[1:2, pl.ds(col, LANES)] += jnp.sum(d_value.astype(F32), axis=0, keepdims=True)
        return carry

    lax.fori_loop(0, sents * pairs, body, 0)

    def grads(step, carry):
        at = pl.ds(pl.multiple_of(step * 256, 256), 256)
        grad[:, at] = dot(turned[...], d_qkv[:, at]).astype(BF16)
        return carry

    lax.fori_loop(0, 3 * width // 256, grads, 0)
    wait_all(copies)
    wait_all(store_grad(links, where, grad, grad_refs, 0, wide, sems.at[1]))


def inputs_kernel(links, n_weight, where, d_qkv, d_resid, *refs):
    weight_refs = refs[:n_weight]
    grad_tokens, w_qkv, sem = refs[n_weight:]
    width = d_resid.shape[1]
    wait_all(load_weight(links, where, weight_refs, 0, width * 3 * 2 // links.n_fsdp, w_qkv, sem))
    for part in range(d_qkv.shape[0] // 256):
        rows = pl.ds(part * 256, 256)
        grad_tokens[rows, :] = (dot_nt(d_qkv[rows, :], w_qkv[...]) + d_resid[rows, :]).astype(BF16)


SMEM_SPEC = pl.BlockSpec(memory_space=pltpu.SMEM)
VMEM_SPEC = pl.BlockSpec(memory_space=pltpu.VMEM)
ANY_SPEC = pl.BlockSpec(memory_space=pl.ANY)


def call(body, name, outs, scratch, args, flops):
    spec = {"s": SMEM_SPEC, "v": VMEM_SPEC, "a": ANY_SPEC}
    size = sum(v.size * v.dtype.itemsize for _, v in list(args) + list(outs))
    return pl.pallas_call(
        body,
        name=name,
        out_shape=[jax.ShapeDtypeStruct(v.shape, v.dtype) for _, v in outs],
        in_specs=[spec[place] for place, _ in args],
        out_specs=[spec[place] for place, _ in outs],
        scratch_shapes=scratch,
        compiler_params=pltpu.CompilerParams(vmem_limit_bytes=VMEM_LIMIT),
        cost_estimate=pl.CostEstimate(flops=flops, bytes_accessed=size, transcendentals=0),
    )(*[value for _, value in args])


def shaped(*shape, dtype=BF16):
    return jax.ShapeDtypeStruct(shape, dtype)


def local(
    n_dp,
    n_fsdp,
    tokens,
    qkv_weight,
    out_weight,
    up_weight,
    up_bias,
    down_weight,
    vectors,
    lengths,
    exit_depth,
    prefix_widths,
    cotangent,
):
    sent_count, seq_len, width = tokens.shape
    rows = sent_count * seq_len
    hidden = up_weight.shape[1] * n_fsdp
    links = Links(n_dp, n_fsdp)
    where = jnp.stack(links.place()).astype(jnp.int32)
    core = where[3]
    inputs = tokens.reshape(rows, width)
    grad_in = cotangent.reshape(rows, width)
    blocked = qkv_weight.shape[0] % 32 == 0 and out_weight.shape[1] % 64 == 0

    if blocked:
        small = jnp.concatenate([vectors, up_bias.reshape(1, -1)], axis=0)
        half = qkv_weight.shape[0] // 2
        small = jnp.pad(small, ((0, half - small.shape[0]), (0, LANES - small.shape[1])))
        piece = jnp.concatenate(
            [chip_piece(links, qkv_weight, core), chip_piece(links, out_weight, core), small], axis=1
        )
        stacks_in = spread(links, piece)
        stacks_up = spread(links, chip_piece(links, up_weight, core))
        stacks_down = spread(links, chip_piece(links, down_weight, core))
        any_in = [("a", item) for item in stacks_in]
        any_out = any_in
        any_up = [("a", item) for item in stacks_up]
        any_down = [("a", item) for item in stacks_down]
        vec, bias = call(
            partial(small_kernel, links),
            "small_values",
            [("v", shaped(8, width, dtype=F32)), ("v", shaped(1, hidden, dtype=F32))],
            [pltpu.VMEM((n_dp * n_fsdp, 16, LANES), BF16), pltpu.SemaphoreType.DMA],
            [("s", where)] + any_in,
            1000,
        )
    else:

        def whole(shard):
            part = lax.all_gather(shard, "fsdp", axis=1, tiled=True)
            return lax.all_gather(part, "dp", axis=0, tiled=True)

        any_in, any_out, any_up, any_down = (
            [("a", whole(shard))] for shard in (qkv_weight, out_weight, up_weight, down_weight)
        )
        vec = lax.all_gather(vectors, "fsdp", axis=0, tiled=True)
        vec = lax.all_gather(vec, "dp", axis=1, tiled=True).astype(F32)
        bias = lax.all_gather(up_bias, ("dp", "fsdp"), axis=0, tiled=True)
        bias = bias.astype(F32).reshape(1, hidden)
    n_weight = len(any_in)
    n_grad = 2 if blocked else 1

    def grad_outs(shard, extra=0):
        if not blocked:
            return [("a", shaped(shard.shape[0] * n_dp, shard.shape[1] * n_fsdp))]
        shape = (2, 2, links.rest, shard.shape[0] // 2, shard.shape[1] * 2 + extra)
        return [("a", shaped(*shape))] * 2

    one, two = pltpu.SemaphoreType.DMA, pltpu.SemaphoreType.DMA((2,))
    flat = shaped(rows, width)
    flat32 = shaped(rows, width, dtype=F32)
    lined = ("s", where)

    qkv, attended, first_norm, normed, factor = call(
        partial(attend_kernel, links, n_weight),
        "attend",
        [
            ("v", shaped(rows, 3 * width)),
            ("v", flat),
            ("v", flat),
            ("v", flat32),
            ("v", shaped(rows, LANES, dtype=F32)),
        ],
        [pltpu.VMEM((width, 3 * width), BF16), pltpu.VMEM((width, width), BF16), two],
        [lined, ("s", lengths), ("v", inputs), ("v", vec)] + any_in + any_out,
        8 * rows * width * width + 4 * rows * seq_len * width,
    )
    activated, slope = call(
        partial(up_kernel, links, n_weight),
        "up",
        [("a", shaped(rows, hidden)), ("a", shaped(rows, hidden))],
        [
            pltpu.VMEM((width, hidden), BF16),
            pltpu.VMEM((2, rows, 256), BF16),
            pltpu.VMEM((2, rows, 256), BF16),
            two,
            pltpu.SemaphoreType.DMA((2, 2)),
        ],
        [lined, ("v", first_norm), ("v", bias)] + any_up,
        2 * rows * width * hidden,
    )
    down = call(
        partial(down_kernel, links, n_weight, n_grad),
        "down",
        [
            ("v", flat),
            ("v", shaped(sent_count, prefix_widths.shape[0], width, dtype=F32)),
            ("v", flat32),
            ("v", flat),
            ("v", shaped(8, width, dtype=F32)),
        ]
        + grad_outs(down_weight),
        [pltpu.VMEM((hidden, width), BF16), pltpu.VMEM((hidden, width), BF16), two],
        [lined, ("s", lengths), ("s", exit_depth), ("s", prefix_widths)]
        + [("v", activated), ("v", first_norm), ("v", inputs), ("v", grad_in), ("v", vec)]
        + any_down,
        4 * rows * width * hidden,
    )
    layer_out, pooled, d_second, d_down, sums_down = down[:5]
    grad_down = down[5:]

    up_back = call(
        partial(up_back_kernel, links, n_weight, n_grad),
        "up_back",
        [("v", shaped(rows, hidden)), ("v", shaped(1, hidden, dtype=F32))] + grad_outs(up_weight),
        [
            pltpu.VMEM((hidden, width), BF16),
            pltpu.VMEM((width, rows), BF16),
            pltpu.VMEM((width, hidden), BF16),
            two,
        ],
        [lined, ("v", d_down), ("v", slope), ("v", first_norm)] + any_down,
        4 * rows * width * hidden,
    )
    d_pre, sums_up = up_back[:2]
    grad_up = up_back[2:]
    d_resid, d_att, grad_out, sums_out = call(
        partial(out_back_kernel, links, n_weight),
        "out_back",
        [("v", flat32), ("v", flat), ("v", shaped(width, width)), ("v", shaped(8, width, dtype=F32))],
        [
            pltpu.VMEM((width, hidden), BF16),
            pltpu.VMEM((width, width), BF16),
            pltpu.VMEM((rows, width), BF16),
            two,
        ],
        [lined]
        + [("v", item) for item in (d_pre, d_second, normed, factor, attended, vec)]
        + any_up
        + any_out,
        2 * rows * width * hidden + 4 * rows * width * width,
    )
    attend_back = call(
        partial(attend_back_kernel, links, n_grad),
        "attend_back",
        [("v", shaped(rows, 3 * width)), ("v", shaped(8, width, dtype=F32))]
        + grad_outs(qkv_weight, 2 * out_weight.shape[1]),
        [pltpu.VMEM((width, rows), BF16), pltpu.VMEM((width, 3 * width), BF16), two],
        [lined, ("s", lengths), ("v", qkv), ("v", d_att), ("v", inputs), ("v", grad_out)],
        6 * rows * width * width + 10 * rows * seq_len * width,
    )
    d_qkv, sums_in = attend_back[:2]
    grad_in_blocks = attend_back[2:]
    (grad_tokens,) = call(
        partial(inputs_kernel, links, n_weight),
        "inputs",
        [("v", flat)],
        [pltpu.VMEM((width, 3 * width), BF16), one],
        [lined, ("v", d_qkv), ("v", d_resid)] + any_in,
        6 * rows * width * width,
    )

    grad_vec = jnp.concatenate(
        [sums_in[:2], sums_out[2:3], sums_out[:2], sums_down[2:3], sums_down[:2]], axis=0
    )
    if blocked:
        own_down = owned(links, collect(links, *grad_down), core)
        own_up = owned(links, collect(links, *grad_up), core)
        last = collect(links, *grad_in_blocks)
        split = 2 * qkv_weight.shape[1]
        own_qkv = owned(links, last[:, :split], core)
        own_out = owned(links, last[:, split:], core)
    else:

        def scattered(grad):
            part = lax.psum_scatter(grad, "dp", scatter_dimension=0, tiled=True)
            part = lax.psum_scatter(part, "fsdp", scatter_dimension=1, tiled=True)
            return part.astype(F32)

        own_down, own_up, own_out, own_qkv = (
            scattered(item) for item in (grad_down[0], grad_up[0], grad_out, grad_in_blocks[0])
        )
    every = jnp.concatenate([grad_vec, sums_up.reshape(-1, width)], axis=0)
    every = sum_everywhere(links, every)
    dp, fsdp = lax.axis_index("dp"), lax.axis_index("fsdp")
    own_vec = lax.dynamic_slice(
        every, (fsdp * vectors.shape[0], dp * vectors.shape[1]), vectors.shape
    )
    own_bias = lax.dynamic_slice_in_dim(
        every[8:].reshape(-1), (dp * n_fsdp + fsdp) * up_bias.shape[0], up_bias.shape[0], 0
    )
    return (
        layer_out.reshape(tokens.shape),
        pooled,
        grad_tokens.reshape(tokens.shape),
        own_qkv,
        own_out,
        own_up,
        own_bias,
        own_down,
        own_vec,
    )


def solution(mesh):
    placed = (
        P(("dp", "fsdp"), None, None),
        P("dp", "fsdp"),
        P("dp", "fsdp"),
        P("dp", "fsdp"),
        P(("dp", "fsdp")),
        P("dp", "fsdp"),
        P("fsdp", "dp"),
        P(("dp", "fsdp")),
        P(("dp", "fsdp")),
        P(),
        P(("dp", "fsdp"), None, None),
    )
    return jax.shard_map(
        partial(local, mesh.shape["dp"], mesh.shape["fsdp"]),
        mesh=mesh,
        in_specs=placed,
        out_specs=(
            P(("dp", "fsdp"), None, None),
            P(("dp", "fsdp"), None, None),
            P(("dp", "fsdp"), None, None),
            P("dp", "fsdp"),
            P("dp", "fsdp"),
            P("dp", "fsdp"),
            P(("dp", "fsdp")),
            P("dp", "fsdp"),
            P("fsdp", "dp"),
        ),
        check_vma=False,
    )
```

```python
import itertools
from functools import partial

import jax
import jax.numpy as jnp
from jax import lax
from jax.experimental import pallas as pl
from jax.experimental.pallas import tpu as pltpu
from jax.sharding import PartitionSpec as P

HEAD_DIM = 64
EPS = 1e-05
MASKED = -1000000000.0
F32 = jnp.float32
BF16 = jnp.bfloat16
MIB = 1024 * 1024
LANES = 128
GROUP = 3


class Links:
    def __init__(self, n_dp, n_fsdp):
        self.n_dp, self.n_fsdp = n_dp, n_fsdp
        self.high = n_fsdp // 4
        self.rest = (n_dp // 2) * self.high

    def number(self, rest, y, x, core):
        z, high = divmod(rest, self.high)
        return (z * 2 + y) * self.n_fsdp + (high * 2 + x) * 2 + core

    def pairs(self, step):
        return [
            (self.number(*place), self.number(*step(*place)))
            for place in itertools.product(range(self.rest), range(2), range(2), range(2))
        ]

    def move(self, value, step):
        return lax.ppermute(value, ("dp", "fsdp"), self.pairs(step))

    def core(self, value):
        return self.move(value, lambda q, y, x, c: (q, y, x, 1 - c))

    def along_x(self, value):
        return self.move(value, lambda q, y, x, c: (q, y, 1 - x, c))

    def along_y(self, value):
        return self.move(value, lambda q, y, x, c: (q, 1 - y, x, c))

    def across(self, value):
        return self.move(value, lambda q, y, x, c: (q, 1 - y, 1 - x, c))

    def first(self, value):
        return self.move(value, lambda q, y, x, c: (q, 1 - y, x, c) if c else (q, y, 1 - x, c))

    def second(self, value):
        return self.move(value, lambda q, y, x, c: (q, y, 1 - x, c) if c else (q, 1 - y, x, c))

    def flip(self, value, bit):
        return self.move(value, lambda q, y, x, c: (q ^ bit, y, x, c))

    def ahead(self, value, far):
        return self.move(value, lambda q, y, x, c: ((q + far) % self.rest, y, x, c))

    def place(self):
        dp, fsdp = lax.axis_index("dp"), lax.axis_index("fsdp")
        rest = (dp // 2) * self.high + fsdp // 4
        return rest, dp % 2, (fsdp // 2) % 2, fsdp % 2


def stack_rest(links, piece):
    return jnp.stack([piece] + [links.ahead(piece, far) for far in range(1, links.rest)])


def double_rest(links, stack):
    while stack.shape[0] < links.rest:
        stack = jnp.concatenate([stack, links.ahead(stack, stack.shape[0])], axis=0)
    return stack


def spread_cores(links, near):
    return list(near) + [links.core(item) for item in near]


class Collect:
    def __init__(self, links, keep, give):
        self.links, self.keep = links, keep
        self.got = links.core(give)

    def add_cores(self):
        def half(y, x):
            return (self.keep[y, x].astype(F32) + self.got[y, x].astype(F32)).astype(BF16)

        links = self.links
        self.halves = [half(0, 1), half(1, 0), half(1, 1)]
        self.near = [
            links.along_x(self.halves[0]),
            links.along_y(self.halves[1]),
            links.across(self.halves[2]),
        ]

    def add_chips(self):
        total = self.keep[0, 0].astype(F32) + self.got[0, 0].astype(F32)
        for item in self.near:
            total = total + item.astype(F32)
        self.total = total

    def direct(self):
        self.blocks = [self.total[far].astype(BF16) for far in range(1, self.links.rest)]
        self.ahead = [self.links.ahead(item, at + 1) for at, item in enumerate(self.blocks)]

    def halve(self):
        half = self.total.shape[0] // 2
        self.far = self.total[half:].astype(BF16)
        self.total = self.total[:half]
        self.back = self.links.ahead(self.far, half)

    def add_half(self):
        self.total = self.total + self.back.astype(F32)


class Blocks:
    def __init__(self, links, where):
        self.links = links
        self.rest, self.y, self.x, self.core = where[0], where[1], where[2], where[3]

    def device(self, other, flip_y, flip_x, far, sign):
        links = self.links
        core = jnp.bitwise_xor(self.core, other)
        rest = lax.rem(self.rest + (sign * far + links.rest), links.rest)
        x, y = jnp.bitwise_xor(self.x, flip_x), jnp.bitwise_xor(self.y, flip_y)
        dp = lax.div(rest, links.high) * 2 + y
        return dp, lax.rem(rest, links.high) * 2 + x, core

    def corner(self, rows, cols, *spot):
        dp, wide, core = self.device(*spot)
        return pl.multiple_of((dp * 2 + core) * rows, rows), pl.multiple_of(wide * cols, cols)


def load_weight(links, where, refs, first_col, cols, out, sem, steps=True):
    if len(refs) == 1:
        copies = [pltpu.make_async_copy(refs[0], out, sem)]
    else:
        blocks = Blocks(links, where)
        rows = refs[0].shape[1]
        copies = []
        for stack, far in itertools.product(range(8), range(links.rest)):
            other, high, low = stack // 4, (stack // 2) % 2, stack % 2
            if steps:
                core = jnp.bitwise_xor(blocks.core, other)
                high, low = jnp.where(core == 0, high, low), jnp.where(core == 0, low, high)
            row, col = blocks.corner(rows, cols, other, high, low, far, -1)
            copies.append(
                pltpu.make_async_copy(
                    refs[stack].at[far, :, pl.ds(first_col, cols)],
                    out.at[pl.ds(row, rows), pl.ds(col, cols)],
                    sem,
                )
            )
    for copy in copies:
        copy.start()
    return copies


def store_grad(links, where, grad, refs, first_col, cols, sem):
    if len(refs) == 1:
        copies = [pltpu.make_async_copy(grad, refs[0], sem)]
    else:
        blocks = Blocks(links, where)
        rows = refs[0].shape[3]
        copies = []
        for other, y, x, far in itertools.product(range(2), range(2), range(2), range(links.rest)):
            row, col = blocks.corner(rows, cols, other, y, x, far, 1)
            out = refs[other].at[y, x, far]
            copies.append(
                pltpu.make_async_copy(
                    grad.at[pl.ds(row, rows), pl.ds(col, cols)],
                    out.at[:, pl.ds(first_col, cols)],
                    sem,
                )
            )
    for copy in copies:
        copy.start()
    return copies


def store_small(links, where, small, refs, first_col, sem):
    blocks = Blocks(links, where)
    copies = []
    for other, y, x, far in itertools.product(range(2), range(2), range(2), range(links.rest)):
        dp, wide, core = blocks.device(other, y, x, far, 1)
        target = refs[other].at[y, x, far, pl.ds(0, 16), pl.ds(first_col, LANES)]
        source = small.at[dp * links.n_fsdp + wide * 2 + core]
        copies.append(pltpu.make_async_copy(source, target, sem))
    for copy in copies:
        copy.start()
    return copies


def wait_all(copies):
    for copy in copies:
        copy.wait()


def dot(left, right):
    return lax.dot_general(left, right, (((1,), (0,)), ((), ())), preferred_element_type=F32)


def dot_nt(left, right):
    return lax.dot_general(left, right, (((1,), (1,)), ((), ())), preferred_element_type=F32)


def dot_tn(left, right):
    return lax.dot_general(left, right, (((0,), (0,)), ((), ())), preferred_element_type=F32)


def normalize(hidden):
    centered = hidden - jnp.mean(hidden, axis=-1, keepdims=True)
    factor = lax.rsqrt(jnp.mean(centered * centered, axis=-1, keepdims=True) + EPS)
    return centered * factor, factor


def norm_back(scaled, normed, factor):
    return factor * (
        scaled
        - jnp.mean(scaled, axis=-1, keepdims=True)
        - normed * jnp.mean(scaled * normed, axis=-1, keepdims=True)
    )


def gelu_parts(value):
    bell = jnp.exp(-0.5 * value * value)
    weight = 0.5 + 0.5 * lax.erf(value * 0.7071067811865476)
    return value * weight, weight + value * (bell * 0.3989422804014327)


def halves_kernel(n_shards, where, *refs):
    shards, outs = refs[:n_shards], refs[n_shards:]
    half = shards[0].shape[0] // 2
    for part in range(2):
        first = jnp.bitwise_xor(where[3], part) * half
        lines = []
        for shard in shards:
            times = shard.shape[0] // 2 // half
            for at in range(times):
                row = pl.multiple_of(first * times + at * half, half)
                lines.append(shard[pl.ds(row, half), :])
        outs[part][...] = jnp.concatenate(lines, axis=1)


def pieces_kernel(widths, where, keep, got, *refs):
    *extra, piece = refs
    mine = where[3] == 0
    low, high = jnp.where(mine, keep[...], got[...]), jnp.where(mine, got[...], keep[...])
    lines, at = [], 0
    for wide in widths:
        lines += [low[:, at : at + wide], high[:, at : at + wide]]
        at += wide
    if extra:
        line = jnp.concatenate([item[...].astype(F32) for item in extra], axis=0)
        below = jnp.zeros((low.shape[0] - line.shape[0], line.shape[1]), F32)
        line = jnp.concatenate([line, below], axis=0)
        beside = jnp.zeros((line.shape[0], LANES - line.shape[1]), F32)
        lines.append(jnp.concatenate([line, beside], axis=1).astype(BF16))
    piece[...] = jnp.concatenate(lines, axis=1)


def small_kernel(links, where, *refs):
    stacks, vec_out, bias_out, held, sem = refs[:8], *refs[8:]
    blocks = Blocks(links, where)
    first_col = stacks[0].shape[2] - LANES
    copies = []
    for stack, far in itertools.product(range(8), range(links.rest)):
        dp, wide, core = blocks.device(stack // 4, (stack // 2) % 2, stack % 2, far, -1)
        copies.append(
            pltpu.make_async_copy(
                stacks[stack].at[far, pl.ds(0, 16), pl.ds(first_col, LANES)],
                held.at[dp * links.n_fsdp + wide * 2 + core],
                sem,
            )
        )
    for copy in copies:
        copy.start()
    wait_all(copies)
    rows, width = 8 // links.n_fsdp, vec_out.shape[1] // links.n_dp
    got = [held[at].astype(F32)[:, :width] for at in range(links.n_dp * links.n_fsdp)]
    for fsdp in range(links.n_fsdp):
        line = jnp.concatenate([got[dp * links.n_fsdp + fsdp] for dp in range(links.n_dp)], axis=1)
        vec_out[pl.ds(rows * fsdp, rows), :] = line[:rows]
    bias_out[...] = jnp.concatenate(got, axis=1)[rows : rows + 1]


def head_half(pair, half):
    lane = lax.broadcasted_iota(jnp.int32, pair.shape, 1)
    keep = (lane < HEAD_DIM) if half == 0 else (lane >= HEAD_DIM)
    return jnp.where(keep, pair, jnp.zeros_like(pair))


def group_spots(step, pairs, seq):
    spots = []
    for at in range(GROUP):
        number = step * GROUP + at
        sent, pair = lax.div(number, pairs), lax.rem(number, pairs)
        rows = pl.ds(pl.multiple_of(sent * seq, seq), seq)
        spots.append((sent, rows, pl.multiple_of(pair * LANES, LANES)))
    return spots


def join_halves(low, high):
    lane = lax.broadcasted_iota(jnp.int32, low.shape, 1)
    return jnp.where(lane < HEAD_DIM, low, high)


def attend_kernel(links, n_weight, where, lengths, tokens, vec, *refs):
    weight_refs = refs[:n_weight]
    qkv, attended, w_qkv, sem = refs[n_weight:]
    width = tokens.shape[1]
    seq = 256
    sents = tokens.shape[0] // seq
    wide = width * 3 * 2 // links.n_fsdp
    wait_all(load_weight(links, where, weight_refs, 0, wide, w_qkv, sem, steps=False))
    for tile in range(3 * width // 256):
        at = pl.ds(tile * 256, 256)
        product = dot(tokens[...], w_qkv[:, at])
        if tile * 256 < width:
            product = product + vec[0:1, at]
        elif tile * 256 >= 2 * width:
            product = product + vec[1:2, pl.ds(tile * 256 - 2 * width, 256)]
        qkv[:, at] = product.astype(BF16)

    pairs = width // LANES

    def attend(step, carry):
        spots = group_spots(step, pairs, seq)
        scores = []
        for sent, rows, col in spots:
            queries = qkv[rows, pl.ds(col, LANES)] * jnp.asarray(HEAD_DIM ** (-0.5), BF16)
            keys = qkv[rows, pl.ds(col + width, LANES)]
            keep = lax.broadcasted_iota(jnp.int32, (seq, seq), 1) < lengths[sent]
            for half in range(2):
                scores.append(jnp.where(keep, dot_nt(head_half(queries, half), keys), MASKED))
        tops = [jnp.max(item, axis=-1, keepdims=True) for item in scores]
        exponents = [jnp.exp(item - top) for item, top in zip(scores, tops)]
        scales = [1.0 / jnp.sum(item, axis=-1, keepdims=True) for item in exponents]
        probs = [(item * scale).astype(BF16) for item, scale in zip(exponents, scales)]
        for at, (sent, rows, col) in enumerate(spots):
            values = qkv[rows, pl.ds(col + 2 * width, LANES)]
            low, high = (dot(probs[2 * at + half], values) for half in range(2))
            attended[rows, pl.ds(col, LANES)] = join_halves(low, high).astype(BF16)
        return carry

    lax.fori_loop(0, sents * pairs // GROUP, attend, 0)


def up_kernel(links, n_weight, where, attended, tokens, vec, bias, *refs):
    up_refs = refs[:n_weight]
    out_refs = refs[n_weight : 2 * n_weight]
    activated, slope, first_norm, normed, factor = refs[2 * n_weight : 2 * n_weight + 5]
    w_up, w_out, even, odd, sems = refs[2 * n_weight + 5 :]
    width, hidden = w_up.shape
    tile = even.shape[1]
    count = hidden // tile
    wide = hidden * 2 // links.n_fsdp
    copies_out = load_weight(
        links, where, out_refs, wide, width * 2 // links.n_fsdp, w_out, sems.at[1]
    )
    copies = load_weight(links, where, up_refs, 0, wide, w_up, sems.at[0])
    wait_all(copies_out)
    for part in range(tokens.shape[0] // 256):
        rows = pl.ds(part * 256, 256)
        total = tokens[rows, :].astype(F32) + (dot(attended[rows, :], w_out[...]) + vec[2:3, :])
        unit, scale = normalize(total)
        normed[rows, :] = unit
        factor[rows, :] = jnp.broadcast_to(scale, (256, LANES))
        first_norm[rows, :] = (unit * vec[3:4, :] + vec[4:5, :]).astype(BF16)
    wait_all(copies)

    def place(step):
        return pl.ds(pl.multiple_of(step * tile, tile), tile)

    def fill(held, step):
        held[...] = dot(first_norm[...], w_up[:, place(step)])

    def drain(held, step):
        at = place(step)
        act, der = gelu_parts(held[...] + bias[:, at])
        activated[:, at] = act.astype(BF16)
        slope[:, at] = der.astype(BF16)

    fill(even, 0)

    def body(step, carry):
        fill(odd, 2 * step + 1)
        drain(even, 2 * step)
        fill(even, lax.rem(2 * step + 2, count))
        drain(odd, 2 * step + 1)
        return carry

    lax.fori_loop(0, count // 2, body, 0)


def down_kernel(links, n_weight, n_grad, where, lengths, depth, prefix, *refs):
    activated, first_norm, tokens, cotangent, vec = refs[:5]
    weight_refs = refs[5 : 5 + n_weight]
    layer_out, pooled, d_second, d_down, sums = refs[5 + n_weight : 10 + n_weight]
    grad_refs = refs[10 + n_weight : 10 + n_weight + n_grad]
    w_down, grad, sems = refs[10 + n_weight + n_grad :]
    hidden, width = w_down.shape
    seq = 256
    sents = tokens.shape[0] // seq
    cols = width * 2 // links.n_fsdp
    wait_all(load_weight(links, where, weight_refs, 0, cols, w_down, sems.at[0]))
    sums[...] = jnp.zeros_like(sums)
    columns = lax.broadcasted_iota(jnp.int32, (1, width), 1)
    for sent in range(sents):
        rows = pl.ds(sent * seq, seq)
        total = first_norm[rows, :].astype(F32) + (dot(activated[rows, :], w_down[...]) + vec[5:6, :])
        normed, factor = normalize(total)
        result = normed * vec[6:7, :] + vec[7:8, :]
        layer_out[rows, :] = result.astype(BF16)
        valid = lax.broadcasted_iota(jnp.int32, (seq, width), 0) < lengths[sent]
        source = jnp.where(depth[sent] == 1, result, tokens[rows, :].astype(F32))
        mean = jnp.sum(jnp.where(valid, source, 0.0), axis=0, keepdims=True)
        mean = mean / lengths[sent].astype(F32)
        for at in range(pooled.shape[1]):
            pooled[sent, pl.ds(at, 1), :] = mean * (columns < prefix[at]).astype(F32)
        grad_in = cotangent[rows, :].astype(F32)
        sums[6:7, :] += jnp.sum(grad_in * normed, axis=0, keepdims=True)
        sums[7:8, :] += jnp.sum(grad_in, axis=0, keepdims=True)
        back = norm_back(grad_in * vec[6:7, :], normed, factor)
        d_second[rows, :] = back
        low = back.astype(BF16)
        d_down[rows, :] = low
        sums[5:6, :] += jnp.sum(low.astype(F32), axis=0, keepdims=True)

    for step in range(hidden // 768):
        at = pl.ds(step * 768, 768)
        grad[at, :] = dot_tn(activated[:, at], d_down[...]).astype(BF16)
    wait_all(store_grad(links, where, grad, grad_refs, 0, cols, sems.at[1]))


def up_back_kernel(links, n_weight, where, d_down, slope, first_norm, sums_in, *refs):
    weight_refs = refs[:n_weight]
    d_pre, sums, grad, w_down, turned, sem = refs[n_weight:]
    hidden, width = w_down.shape
    copies = load_weight(links, where, weight_refs, 0, width * 2 // links.n_fsdp, w_down, sem)
    sums[...] = sums_in[...]
    turned[...] = first_norm[...].T
    wait_all(copies)

    for step in range(hidden // 512):
        at = pl.ds(step * 512, 512)
        d_act = dot_nt(d_down[...], w_down[at, :])
        low = (d_act * slope[:, at].astype(F32)).astype(BF16)
        d_pre[:, at] = low
        line = jnp.sum(low.astype(F32), axis=0, keepdims=True)
        for part in range(2):
            row, col = divmod(step * 512 + part * 256, width)
            sums[pl.ds(8 + row, 1), pl.ds(col, 256)] = line[:, part * 256 : part * 256 + 256]
        grad[:, at] = dot(turned[...], low).astype(BF16)


def out_back_kernel(links, n_weight, n_grad, where, *refs):
    d_pre, d_second, normed, factor, attended, vec, sums_in, grad_up = refs[:8]
    up_refs = refs[8 : 8 + n_weight]
    out_refs = refs[8 + n_weight : 8 + 2 * n_weight]
    d_resid, d_att, sums = refs[8 + 2 * n_weight : 11 + 2 * n_weight]
    grad_refs = refs[11 + 2 * n_weight : 11 + 2 * n_weight + n_grad]
    w_up, w_out, d_attn, grad_out, sems = refs[11 + 2 * n_weight + n_grad :]
    width, hidden = w_up.shape
    seq = 256
    wide = hidden * 2 // links.n_fsdp
    copies = load_weight(links, where, up_refs, 0, wide, w_up, sems.at[0])
    copies_out = load_weight(
        links, where, out_refs, wide, width * 2 // links.n_fsdp, w_out, sems.at[1]
    )
    if n_grad > 1:
        copies_up = store_grad(links, where, grad_up, grad_refs, 0, wide, sems.at[3])
    wait_all(copies)
    sums[...] = sums_in[...]
    for part in range(d_pre.shape[0] // seq):
        rows = pl.ds(part * seq, seq)
        d_first = dot_nt(d_pre[rows, :], w_up[...]) + d_second[rows, :]
        unit = normed[rows, :]
        sums[3:4, :] += jnp.sum(d_first * unit, axis=0, keepdims=True)
        sums[4:5, :] += jnp.sum(d_first, axis=0, keepdims=True)
        back = norm_back(d_first * vec[3:4, :], unit, factor[rows, 0:1])
        d_resid[rows, :] = back
        low = back.astype(BF16)
        d_attn[rows, :] = low
        sums[2:3, :] += jnp.sum(low.astype(F32), axis=0, keepdims=True)
    wait_all(copies_out)
    grad_out[...] = dot_tn(attended[...], d_attn[...]).astype(BF16)
    first = wide if n_grad > 1 else 0
    copies = store_grad(
        links, where, grad_out, grad_refs, first, width * 2 // links.n_fsdp, sems.at[2]
    )
    if n_grad > 1:
        copies += copies_up
    d_att[...] = dot_nt(d_attn[...], w_out[...]).astype(BF16)
    wait_all(copies)


def attend_back_kernel(links, n_grad, where, lengths, qkv, d_att, tokens, sums_in, *refs):
    d_qkv, sums = refs[:2]
    grad_refs = refs[2 : 2 + n_grad]
    turned, grad, held, small, sems = refs[2 + n_grad :]
    width = tokens.shape[1]
    seq = 256
    sents = tokens.shape[0] // seq
    pairs = width // LANES
    wide = width * 3 * 2 // links.n_fsdp
    turned[...] = tokens[...].T
    sums[...] = sums_in[...]
    key_scale = jnp.asarray(HEAD_DIM ** (-0.5), BF16)

    def body(step, carry):
        spots = group_spots(step, pairs, seq)
        loaded, scores, d_probs = [], [], []
        for sent, rows, col in spots:
            queries = qkv[rows, pl.ds(col, LANES)] * key_scale
            keys = qkv[rows, pl.ds(col + width, LANES)]
            values = qkv[rows, pl.ds(col + 2 * width, LANES)]
            d_out = d_att[rows, pl.ds(col, LANES)]
            loaded.append((queries, keys, d_out))
            keep = lax.broadcasted_iota(jnp.int32, (seq, seq), 0) < lengths[sent]
            for half in range(2):
                scores.append(jnp.where(keep, dot_nt(keys, head_half(queries, half)), MASKED))
                d_probs.append(dot_nt(values, head_half(d_out, half)))
        tops = [jnp.max(item, axis=0, keepdims=True) for item in scores]
        exponents = [jnp.exp(item - top) for item, top in zip(scores, tops)]
        scales = [1.0 / jnp.sum(item, axis=0, keepdims=True) for item in exponents]
        probs = [item * scale for item, scale in zip(exponents, scales)]
        row_dots = [jnp.sum(back * prob, axis=0, keepdims=True) for back, prob in zip(d_probs, probs)]
        d_scores = [
            (prob * (back - row_dot)).astype(BF16)
            for prob, back, row_dot in zip(probs, d_probs, row_dots)
        ]
        for at, (sent, rows, col) in enumerate(spots):
            queries, keys, d_out = loaded[at]
            mine = (2 * at, 2 * at + 1)
            d_value = join_halves(*(dot(probs[one].astype(BF16), d_out) for one in mine))
            d_key = join_halves(*(dot(d_scores[one], queries) for one in mine))
            d_query = join_halves(*(dot_tn(d_scores[one], keys) for one in mine))
            d_query = (d_query * (HEAD_DIM ** (-0.5))).astype(BF16)
            d_value = d_value.astype(BF16)
            d_qkv[rows, pl.ds(col, LANES)] = d_query
            d_qkv[rows, pl.ds(col + width, LANES)] = d_key.astype(BF16)
            d_qkv[rows, pl.ds(col + 2 * width, LANES)] = d_value
            sums[0:1, pl.ds(col, LANES)] += jnp.sum(d_query.astype(F32), axis=0, keepdims=True)
            sums[1:2, pl.ds(col, LANES)] += jnp.sum(d_value.astype(F32), axis=0, keepdims=True)
        return carry

    lax.fori_loop(0, sents * pairs // GROUP, body, 0)
    copies = []
    if n_grad > 1:
        held[...] = jnp.zeros_like(held)
        per_device = 8 // links.n_fsdp
        line_rows, line_cols = sums.shape[0] - 8, width // links.n_dp
        for dp, fsdp in itertools.product(range(links.n_dp), range(links.n_fsdp)):
            at = dp * links.n_fsdp + fsdp
            rows = pl.ds(fsdp * per_device, per_device)
            held[at, :per_device, :line_cols] = sums[rows, pl.ds(dp * line_cols, line_cols)]
            first = at * line_cols
            row, col = 8 + first // width, first % width
            held[at, per_device : per_device + 1, :line_cols] = sums[pl.ds(row, 1), pl.ds(col, line_cols)]
        small[...] = held[...].astype(BF16)
        copies = store_small(links, where, small, grad_refs, wide, sems.at[1])
    for step in range(3 * width // 256):
        at = pl.ds(step * 256, 256)
        grad[:, at] = dot(turned[...], d_qkv[:, at]).astype(BF16)
    wait_all(copies + store_grad(links, where, grad, grad_refs, 0, wide, sems.at[0]))


def inputs_kernel(links, n_weight, where, d_qkv, d_resid, *refs):
    weight_refs = refs[:n_weight]
    grad_tokens, w_qkv, sem = refs[n_weight:]
    width = d_resid.shape[1]
    wide = width * 3 * 2 // links.n_fsdp
    wait_all(load_weight(links, where, weight_refs, 0, wide, w_qkv, sem, steps=False))
    for part in range(d_qkv.shape[0] // 256):
        rows = pl.ds(part * 256, 256)
        grad_tokens[rows, :] = (dot_nt(d_qkv[rows, :], w_qkv[...]) + d_resid[rows, :]).astype(BF16)


def columns_kernel(spans, extra, where, *refs):
    n_outs = 2 * len(spans) + (1 if extra else 0)
    parts, outs = refs[:-n_outs], refs[-n_outs:]
    total = parts[0][...]
    for part in parts[1:]:
        total = total + part[...].astype(F32)
    mine = where[3] == 0
    for at, (first, last) in enumerate(spans):
        middle = (first + last) // 2
        low, high = total[:, first:middle], total[:, middle:last]
        outs[2 * at][...] = jnp.where(mine, low, high)
        outs[2 * at + 1][...] = jnp.where(mine, high, low)
    if extra:
        outs[-1][...] = total[:8, -extra:]


def rows_kernel(where, *refs):
    count = len(refs) // 3
    mine = where[3] == 0
    for at in range(count):
        keep, got, out = refs[at], refs[count + at], refs[2 * count + at]
        half = keep.shape[0]
        out[:half, :] = jnp.where(mine, keep[...], got[...])
        out[half:, :] = jnp.where(mine, got[...], keep[...])


SMEM_SPEC = pl.BlockSpec(memory_space=pltpu.SMEM)
VMEM_SPEC = pl.BlockSpec(memory_space=pltpu.VMEM)
ANY_SPEC = pl.BlockSpec(memory_space=pl.ANY)


def call(body, name, outs, scratch, args, vmem, after=(), through=()):
    spec = {"s": SMEM_SPEC, "v": VMEM_SPEC, "a": ANY_SPEC}
    extra = [("a", v) for v in list(through) + list(after)]
    handed = [("a", v) for v in through]
    n_args, n_outs = len(args), len(outs)

    def run(*refs):
        rest = refs[n_args + len(extra) :]
        body(*refs[:n_args], *rest[:n_outs], *rest[n_outs + len(handed) :])

    return list(
        pl.pallas_call(
            run,
            name=name,
            out_shape=[jax.ShapeDtypeStruct(v.shape, v.dtype) for _, v in list(outs) + handed],
            in_specs=[spec[place] for place, _ in list(args) + extra],
            out_specs=[spec[place] for place, _ in list(outs) + handed],
            scratch_shapes=scratch,
            input_output_aliases={n_args + at: n_outs + at for at in range(len(handed))},
            compiler_params=pltpu.CompilerParams(vmem_limit_bytes=vmem * MIB),
            cost_estimate=pl.CostEstimate(flops=1, bytes_accessed=1, transcendentals=0),
        )(*[value for _, value in list(args) + extra])
    )


def hold(arrays, after):
    return call(lambda: None, "hold", [], [], [], 1, after=after, through=arrays)


def owned(links, where, parts, spans, extra=0):
    rows = parts[0].shape[0]
    halves = [("v", shaped(rows, (last - first) // 2, dtype=F32)) for first, last in spans]
    pieces = call(
        partial(columns_kernel, spans, extra),
        "columns",
        [item for half in halves for item in (half, half)]
        + ([("v", shaped(8, extra, dtype=F32))] if extra else []),
        [],
        [("s", where)] + [("v", item) for item in parts],
        4,
    )
    count = 2 * len(spans)
    keep, give, last = pieces[:count:2], pieces[1:count:2], pieces[count:]
    got = [links.core(item) for item in give]
    rows_out = call(
        rows_kernel,
        "rows",
        [("v", shaped(2 * rows, half.shape[1], dtype=F32)) for _, half in halves],
        [],
        [("s", where)] + [("v", item) for item in keep + got],
        4,
    )
    return rows_out + last


def shaped(*shape, dtype=BF16):
    return jax.ShapeDtypeStruct(shape, dtype)


def local(
    n_dp,
    n_fsdp,
    tokens,
    qkv_weight,
    out_weight,
    up_weight,
    up_bias,
    down_weight,
    vectors,
    lengths,
    exit_depth,
    prefix_widths,
    cotangent,
):
    sent_count, seq_len, width = tokens.shape
    rows = sent_count * seq_len
    hidden = up_weight.shape[1] * n_fsdp
    links = Links(n_dp, n_fsdp)
    where = jnp.stack(links.place()).astype(jnp.int32)
    inputs = tokens.reshape(rows, width)
    grad_in = cotangent.reshape(rows, width)
    blocked = qkv_weight.shape[0] % 32 == 0 and out_weight.shape[1] % 64 == 0

    if blocked:
        half = qkv_weight.shape[0] // 2
        parts = down_weight.shape[0] // 2 // half
        widths = [up_weight.shape[1], out_weight.shape[1]] + parts * [down_weight.shape[1]]

        def chip_piece(name, wides, shards, extra=(), after=()):
            line = ("v", shaped(half, sum(wides)))
            keep, give = call(
                partial(halves_kernel, len(shards)),
                name + "_halves",
                [line, line],
                [],
                [("s", where)] + [("v", item) for item in shards],
                3,
                after=after,
            )
            wide = 2 * sum(wides) + (LANES if extra else 0)
            return call(
                partial(pieces_kernel, wides),
                name + "_piece",
                [("v", shaped(half, wide))],
                [],
                [("s", where)] + [("v", item) for item in (keep, links.core(give), *extra)],
                3,
            )[0]

        piece_in = chip_piece(
            "in", [qkv_weight.shape[1]], [qkv_weight], [vectors, up_bias.reshape(1, -1)]
        )
        piece_up = chip_piece(
            "up", widths, [up_weight, out_weight, down_weight], after=[piece_in]
        )
        own_in = stack_rest(links, piece_in)
        pair = jnp.stack([piece_up, links.ahead(piece_up, 1)])
        split = 2 * (up_weight.shape[1] + out_weight.shape[1])
        up_pair = pair[:, :, :split]
        down_pair = jnp.concatenate(jnp.split(pair[:, :, split:], parts, axis=2), axis=1)
        (own_in,) = hold([own_in], [up_pair, down_pair])
        own_up_stack = double_rest(links, up_pair)
        near_in = [own_in, links.along_x(own_in), links.along_y(own_in), links.across(own_in)]
        (down_pair,) = hold([down_pair], [own_up_stack])
        down_far = links.ahead(down_pair, 2)
        near_in = hold(near_in, [own_up_stack])
        up_first, up_second = links.first(own_up_stack), links.second(own_up_stack)
        any_in = [("a", item) for item in spread_cores(links, near_in)]
        vec, bias = call(
            partial(small_kernel, links),
            "small_values",
            [("v", shaped(8, width, dtype=F32)), ("v", shaped(1, hidden, dtype=F32))],
            [pltpu.VMEM((n_dp * n_fsdp, 16, LANES), BF16), pltpu.SemaphoreType.DMA],
            [("s", where)] + any_in,
            3,
        )
    else:

        def whole(shard):
            part = lax.all_gather(shard, "fsdp", axis=1, tiled=True)
            return lax.all_gather(part, "dp", axis=0, tiled=True)

        any_in, any_out, any_up, any_down = (
            [("a", whole(shard))] for shard in (qkv_weight, out_weight, up_weight, down_weight)
        )
        vec = lax.all_gather(vectors, "fsdp", axis=0, tiled=True)
        vec = lax.all_gather(vec, "dp", axis=1, tiled=True).astype(F32)
        bias = lax.all_gather(up_bias, ("dp", "fsdp"), axis=0, tiled=True)
        bias = bias.astype(F32).reshape(1, hidden)
    n_weight = len(any_in)
    n_grad = 2 if blocked else 1

    def grad_outs(shard, *more, extra=0):
        if not blocked:
            return [("a", shaped(shard.shape[0] * n_dp, shard.shape[1] * n_fsdp))]
        cols = shard.shape[1] + sum(item.shape[1] for item in more)
        shape = (links.rest, shard.shape[0] // 2, 2 * cols + extra)
        return 2 * [("a", shaped(2, 2, *shape))]

    small = shaped(8 + -(-hidden // width // 8) * 8, width, dtype=F32)
    one, two = pltpu.SemaphoreType.DMA, pltpu.SemaphoreType.DMA((2,))
    flat = shaped(rows, width)
    flat32 = shaped(rows, width, dtype=F32)
    lined = ("s", where)

    def room(mib):
        return mib if blocked else 2 * mib

    qkv, attended = call(
        partial(attend_kernel, links, n_weight),
        "attend",
        [("v", shaped(rows, 3 * width)), ("v", flat)],
        [pltpu.VMEM((width, 3 * width), BF16), one],
        [lined, ("s", lengths), ("v", inputs), ("v", vec)] + any_in,
        room(13),
    )
    if blocked:
        up_first, up_second, down_far = hold([up_first, up_second, down_far], [attended])
        own_down_stack = double_rest(links, jnp.concatenate([down_pair, down_far], axis=0))
        up_both = links.second(up_first)
        down_first, down_second = links.first(own_down_stack), links.second(own_down_stack)
        near_up = [own_up_stack, up_first, up_second, up_both]
        any_up = [("a", item) for item in spread_cores(links, near_up)]
        any_out = any_up
    activated, slope, first_norm, normed, factor = call(
        partial(up_kernel, links, n_weight),
        "up",
        [
            ("v", shaped(rows, hidden)),
            ("v", shaped(rows, hidden)),
            ("v", flat),
            ("v", flat32),
            ("v", shaped(rows, LANES, dtype=F32)),
        ],
        [pltpu.VMEM((width, hidden), BF16), pltpu.VMEM((width, width), BF16)]
        + [pltpu.VMEM((rows, 512), F32)] * 2
        + [two],
        [lined, ("v", attended), ("v", inputs), ("v", vec), ("v", bias)] + any_up + any_out,
        room(17),
        after=[down_first] if blocked else [],
    )
    if blocked:
        down_both = links.second(down_first)
        down_second, down_both = hold([down_second, down_both], [activated])
        near_down = [own_down_stack, down_first, down_second, down_both]
        any_down = [("a", item) for item in spread_cores(links, near_down)]
    down = call(
        partial(down_kernel, links, n_weight, n_grad),
        "down",
        [
            ("v", flat),
            ("v", shaped(sent_count, prefix_widths.shape[0], width, dtype=F32)),
            ("v", flat32),
            ("v", flat),
            ("v", small),
        ]
        + grad_outs(down_weight),
        [pltpu.VMEM((hidden, width), BF16), pltpu.VMEM((hidden, width), BF16), two],
        [lined, ("s", lengths), ("s", exit_depth), ("s", prefix_widths)]
        + [("v", activated), ("v", first_norm), ("v", inputs), ("v", grad_in), ("v", vec)]
        + any_down,
        room(19),
    )
    layer_out, pooled, d_second, d_down, sums_down = down[:5]
    grad_down = down[5:]
    if blocked:
        sum_down = Collect(links, *grad_down)
        sum_down.add_cores()

    d_pre, sums_up, grad_up = call(
        partial(up_back_kernel, links, n_weight),
        "up_back",
        [("v", shaped(rows, hidden)), ("v", small), ("v", shaped(width, hidden))],
        [pltpu.VMEM((hidden, width), BF16), pltpu.VMEM((width, rows), BF16), one],
        [lined, ("v", d_down), ("v", slope), ("v", first_norm), ("v", sums_down)] + any_down,
        room(16),
        after=sum_down.halves if blocked else [],
    )
    d_resid, d_att, sums_out, *grad_out = call(
        partial(out_back_kernel, links, n_weight, n_grad),
        "out_back",
        [("v", flat32), ("v", flat), ("v", small)]
        + (grad_outs(up_weight, out_weight) if blocked else grad_outs(out_weight)),
        [
            pltpu.VMEM((width, hidden), BF16),
            pltpu.VMEM((width, width), BF16),
            pltpu.VMEM((rows, width), BF16),
            pltpu.VMEM((width, width), BF16),
            pltpu.SemaphoreType.DMA((4,)),
        ],
        [lined]
        + [("v", item) for item in (d_pre, d_second, normed, factor, attended, vec, sums_up, grad_up)]
        + any_up
        + any_out,
        room(17),
    )
    if blocked:
        sum_up = Collect(links, grad_out[0], *hold(grad_out[1:], sum_down.near))
        sum_up.add_cores()
        sum_down.add_chips()
        sum_down.halve()
    attend_back = call(
        partial(attend_back_kernel, links, n_grad),
        "attend_back",
        [("v", shaped(rows, 3 * width)), ("v", small)]
        + grad_outs(qkv_weight, extra=LANES),
        [
            pltpu.VMEM((width, rows), BF16),
            pltpu.VMEM((width, 3 * width), BF16),
            pltpu.VMEM((n_dp * n_fsdp, 16, LANES), F32),
            pltpu.VMEM((n_dp * n_fsdp, 16, LANES), BF16),
            two,
        ],
        [lined, ("s", lengths), ("v", qkv), ("v", d_att), ("v", inputs), ("v", sums_out)],
        room(17),
        after=sum_up.halves + [sum_down.far] if blocked else [],
    )
    d_qkv, sums_in = attend_back[:2]
    grad_in_blocks = attend_back[2:]
    (grad_tokens,) = call(
        partial(inputs_kernel, links, n_weight),
        "inputs",
        [("v", flat)],
        [pltpu.VMEM((width, 3 * width), BF16), one],
        [lined, ("v", d_qkv), ("v", d_resid)] + any_in,
        room(10),
    )

    if blocked:
        passed = hold([grad_in_blocks[1], sum_down.back] + sum_up.near, [grad_tokens])
        give, sum_down.back, *sum_up.near = passed
        sum_in = Collect(links, grad_in_blocks[0], give)
        sum_in.add_cores()
        sum_up.near = hold(sum_up.near, sum_in.halves)
        sum_up.add_chips()
        sum_up.halve()
        sum_down.add_half()
        sum_down.halve()
        passed = hold(sum_in.near + [sum_up.back, sum_down.back], [])
        sum_in.near, waiting = passed[:3], passed[3:]
        sum_in.add_chips()
        sum_in.direct()
        sum_up.back, sum_down.back = hold(waiting, sum_in.blocks)
        for item in (sum_up, sum_down):
            item.add_half()
            while item.total.shape[0] > 1:
                item.halve()
                item.add_half()
        wide = 2 * qkv_weight.shape[1]
        own_qkv, last = owned(links, where, [sum_in.total[0]] + sum_in.ahead, [(0, wide)], LANES)
        own_vec = last[: vectors.shape[0], : vectors.shape[1]]
        own_bias = last[vectors.shape[0], : up_bias.shape[0]]
        wide = 2 * down_weight.shape[1]
        (own_down,) = owned(links, where, [sum_down.total[0]], [(0, wide)])
        split, wide = 2 * up_weight.shape[1], 2 * (up_weight.shape[1] + out_weight.shape[1])
        own_up, own_out = owned(links, where, [sum_up.total[0]], [(0, split), (split, wide)])
    else:

        def scattered(grad):
            part = lax.psum_scatter(grad, "dp", scatter_dimension=0, tiled=True)
            part = lax.psum_scatter(part, "fsdp", scatter_dimension=1, tiled=True)
            return part.astype(F32)

        own_down, own_up, own_out, own_qkv = (
            scattered(item) for item in (grad_down[0], grad_up, grad_out[0], grad_in_blocks[0])
        )
        every = lax.psum(sums_in, ("dp", "fsdp"))
        dp, fsdp = lax.axis_index("dp"), lax.axis_index("fsdp")
        own_vec = lax.dynamic_slice(
            every, (fsdp * vectors.shape[0], dp * vectors.shape[1]), vectors.shape
        )
        own_bias = lax.dynamic_slice_in_dim(
            every[8:].reshape(-1), (dp * n_fsdp + fsdp) * up_bias.shape[0], up_bias.shape[0], 0
        )
    return (
        layer_out.reshape(tokens.shape),
        pooled,
        grad_tokens.reshape(tokens.shape),
        own_qkv,
        own_out,
        own_up,
        own_bias,
        own_down,
        own_vec,
    )


def solution(mesh):
    placed = (
        P(("dp", "fsdp"), None, None),
        P("dp", "fsdp"),
        P("dp", "fsdp"),
        P("dp", "fsdp"),
        P(("dp", "fsdp")),
        P("dp", "fsdp"),
        P("fsdp", "dp"),
        P(("dp", "fsdp")),
        P(("dp", "fsdp")),
        P(),
        P(("dp", "fsdp"), None, None),
    )
    return jax.shard_map(
        partial(local, mesh.shape["dp"], mesh.shape["fsdp"]),
        mesh=mesh,
        in_specs=placed,
        out_specs=(
            P(("dp", "fsdp"), None, None),
            P(("dp", "fsdp"), None, None),
            P(("dp", "fsdp"), None, None),
            P("dp", "fsdp"),
            P("dp", "fsdp"),
            P("dp", "fsdp"),
            P(("dp", "fsdp")),
            P("dp", "fsdp"),
            P("fsdp", "dp"),
        ),
        check_vma=False,
    )
```

```python
import itertools
from functools import partial

import jax
import jax.numpy as jnp
from jax import lax
from jax.experimental import pallas as pl
from jax.experimental.pallas import tpu as pltpu
from jax.sharding import PartitionSpec as P

HEAD_DIM = 64
EPS = 1e-05
MASKED = -1000000000.0
F32 = jnp.float32
BF16 = jnp.bfloat16
MIB = 1024 * 1024
LANES = 128
GROUP = 3


class Links:
    def __init__(self, n_dp, n_fsdp):
        self.n_dp, self.n_fsdp = n_dp, n_fsdp
        self.high = n_fsdp // 4
        self.rest = (n_dp // 2) * self.high

    def number(self, rest, y, x, core):
        z, high = divmod(rest, self.high)
        return (z * 2 + y) * self.n_fsdp + (high * 2 + x) * 2 + core

    def pairs(self, step):
        return [
            (self.number(*place), self.number(*step(*place)))
            for place in itertools.product(range(self.rest), range(2), range(2), range(2))
        ]

    def move(self, value, step):
        return lax.ppermute(value, ("dp", "fsdp"), self.pairs(step))

    def core(self, value):
        return self.move(value, lambda q, y, x, c: (q, y, x, 1 - c))

    def along_x(self, value):
        return self.move(value, lambda q, y, x, c: (q, y, 1 - x, c))

    def along_y(self, value):
        return self.move(value, lambda q, y, x, c: (q, 1 - y, x, c))

    def across(self, value):
        return self.move(value, lambda q, y, x, c: (q, 1 - y, 1 - x, c))

    def first(self, value):
        return self.move(value, lambda q, y, x, c: (q, 1 - y, x, c) if c else (q, y, 1 - x, c))

    def second(self, value):
        return self.move(value, lambda q, y, x, c: (q, y, 1 - x, c) if c else (q, 1 - y, x, c))

    def flip(self, value, bit):
        return self.move(value, lambda q, y, x, c: (q ^ bit, y, x, c))

    def ahead(self, value, far):
        return self.move(value, lambda q, y, x, c: ((q + far) % self.rest, y, x, c))

    def place(self):
        dp, fsdp = lax.axis_index("dp"), lax.axis_index("fsdp")
        rest = (dp // 2) * self.high + fsdp // 4
        return rest, dp % 2, (fsdp // 2) % 2, fsdp % 2


def double_rest(links, stack):
    while stack.shape[0] < links.rest:
        stack = jnp.concatenate([stack, links.ahead(stack, stack.shape[0])], axis=0)
    return stack


def spread_cores(links, near):
    return list(near) + [links.core(item) for item in near]


class Collect:
    def __init__(self, links, keep, give):
        self.links, self.keep = links, keep
        self.got = links.core(give)

    def add_cores(self):
        def half(y, x):
            return (self.keep[y, x].astype(F32) + self.got[y, x].astype(F32)).astype(BF16)

        links = self.links
        self.halves = [half(0, 1), half(1, 0), half(1, 1)]
        self.near = [
            links.along_x(self.halves[0]),
            links.along_y(self.halves[1]),
            links.across(self.halves[2]),
        ]

    def add_chips(self):
        total = self.keep[0, 0].astype(F32) + self.got[0, 0].astype(F32)
        for item in self.near:
            total = total + item.astype(F32)
        self.total = total

    def direct(self):
        self.blocks = [self.total[far].astype(BF16) for far in range(1, self.links.rest)]
        self.ahead = [self.links.ahead(item, at + 1) for at, item in enumerate(self.blocks)]

    def halve(self):
        half = self.total.shape[0] // 2
        self.far = self.total[half:].astype(BF16)
        self.total = self.total[:half]
        self.back = self.links.ahead(self.far, half)

    def add_half(self):
        self.total = self.total + self.back.astype(F32)


class Blocks:
    def __init__(self, links, where):
        self.links = links
        self.rest, self.y, self.x, self.core = where[0], where[1], where[2], where[3]

    def device(self, other, flip_y, flip_x, far, sign):
        links = self.links
        core = jnp.bitwise_xor(self.core, other)
        rest = lax.rem(self.rest + (sign * far + links.rest), links.rest)
        x, y = jnp.bitwise_xor(self.x, flip_x), jnp.bitwise_xor(self.y, flip_y)
        dp = lax.div(rest, links.high) * 2 + y
        return dp, lax.rem(rest, links.high) * 2 + x, core

    def corner(self, rows, cols, *spot):
        dp, wide, core = self.device(*spot)
        return pl.multiple_of((dp * 2 + core) * rows, rows), pl.multiple_of(wide * cols, cols)


def load_weight(links, where, refs, first_col, cols, out, sem, steps=True):
    if len(refs) == 1:
        copies = [pltpu.make_async_copy(refs[0], out, sem)]
    else:
        blocks = Blocks(links, where)
        rows = refs[0].shape[1]
        copies = []
        for stack, far in itertools.product(range(8), range(links.rest)):
            other, high, low = stack // 4, (stack // 2) % 2, stack % 2
            if steps:
                core = jnp.bitwise_xor(blocks.core, other)
                high, low = jnp.where(core == 0, high, low), jnp.where(core == 0, low, high)
            row, col = blocks.corner(rows, cols, other, high, low, far, -1)
            copies.append(
                pltpu.make_async_copy(
                    refs[stack].at[far, :, pl.ds(first_col, cols)],
                    out.at[pl.ds(row, rows), pl.ds(col, cols)],
                    sem,
                )
            )
    for copy in copies:
        copy.start()
    return copies


def store_grad(links, where, grad, refs, first_col, cols, sem):
    if len(refs) == 1:
        copies = [pltpu.make_async_copy(grad, refs[0], sem)]
    else:
        blocks = Blocks(links, where)
        rows = refs[0].shape[3]
        copies = []
        for other, y, x, far in itertools.product(range(2), range(2), range(2), range(links.rest)):
            row, col = blocks.corner(rows, cols, other, y, x, far, 1)
            out = refs[other].at[y, x, far]
            copies.append(
                pltpu.make_async_copy(
                    grad.at[pl.ds(row, rows), pl.ds(col, cols)],
                    out.at[:, pl.ds(first_col, cols)],
                    sem,
                )
            )
    for copy in copies:
        copy.start()
    return copies


def store_small(links, where, small, refs, first_col, sem):
    blocks = Blocks(links, where)
    copies = []
    for other, y, x, far in itertools.product(range(2), range(2), range(2), range(links.rest)):
        dp, wide, core = blocks.device(other, y, x, far, 1)
        target = refs[other].at[y, x, far, pl.ds(0, 16), pl.ds(first_col, LANES)]
        source = small.at[dp * links.n_fsdp + wide * 2 + core]
        copies.append(pltpu.make_async_copy(source, target, sem))
    for copy in copies:
        copy.start()
    return copies


def wait_all(copies):
    for copy in copies:
        copy.wait()


def dot(left, right):
    return lax.dot_general(left, right, (((1,), (0,)), ((), ())), preferred_element_type=F32)


def dot_nt(left, right):
    return lax.dot_general(left, right, (((1,), (1,)), ((), ())), preferred_element_type=F32)


def dot_tn(left, right):
    return lax.dot_general(left, right, (((0,), (0,)), ((), ())), preferred_element_type=F32)


def normalize(hidden):
    centered = hidden - jnp.mean(hidden, axis=-1, keepdims=True)
    factor = lax.rsqrt(jnp.mean(centered * centered, axis=-1, keepdims=True) + EPS)
    return centered * factor, factor


def norm_back(scaled, normed, factor):
    return factor * (
        scaled
        - jnp.mean(scaled, axis=-1, keepdims=True)
        - normed * jnp.mean(scaled * normed, axis=-1, keepdims=True)
    )


def gelu_parts(value):
    bell = jnp.exp(-0.5 * value * value)
    weight = 0.5 + 0.5 * lax.erf(value * 0.7071067811865476)
    return value * weight, weight + value * (bell * 0.3989422804014327)


def piece_kernel(n_shards, where, *refs):
    mine, theirs = refs[:n_shards], refs[n_shards : 2 * n_shards]
    *extra, piece = refs[2 * n_shards :]
    core = where[3]
    half = mine[0].shape[0] // 2
    lines = []
    for keep, got in zip(mine, theirs):
        times = keep.shape[0] // 2 // half
        for at in range(times):
            row = pl.multiple_of(core * half * times + at * half, half)
            low, high = keep[pl.ds(row, half), :], got[pl.ds(row, half), :]
            lines += [jnp.where(core == 0, low, high), jnp.where(core == 0, high, low)]
    if extra:
        line = jnp.concatenate([item[...].astype(F32) for item in extra], axis=0)
        below = jnp.zeros((half - line.shape[0], line.shape[1]), F32)
        line = jnp.concatenate([line, below], axis=0)
        beside = jnp.zeros((line.shape[0], LANES - line.shape[1]), F32)
        lines.append(jnp.concatenate([line, beside], axis=1).astype(BF16))
    piece[...] = jnp.concatenate(lines, axis=1)


def small_kernel(links, where, *refs):
    stacks, vec_out, bias_out, held, sem = refs[:8], *refs[8:]
    blocks = Blocks(links, where)
    first_col = stacks[0].shape[2] - LANES
    copies = []
    for stack, far in itertools.product(range(8), range(links.rest)):
        dp, wide, core = blocks.device(stack // 4, (stack // 2) % 2, stack % 2, far, -1)
        copies.append(
            pltpu.make_async_copy(
                stacks[stack].at[far, pl.ds(0, 16), pl.ds(first_col, LANES)],
                held.at[dp * links.n_fsdp + wide * 2 + core],
                sem,
            )
        )
    for copy in copies:
        copy.start()
    wait_all(copies)
    rows, width = 8 // links.n_fsdp, vec_out.shape[1] // links.n_dp
    got = [held[at].astype(F32)[:, :width] for at in range(links.n_dp * links.n_fsdp)]
    for fsdp in range(links.n_fsdp):
        line = jnp.concatenate([got[dp * links.n_fsdp + fsdp] for dp in range(links.n_dp)], axis=1)
        vec_out[pl.ds(rows * fsdp, rows), :] = line[:rows]
    bias_out[...] = jnp.concatenate(got, axis=1)[rows : rows + 1]


def head_half(pair, half):
    lane = lax.broadcasted_iota(jnp.int32, pair.shape, 1)
    keep = (lane < HEAD_DIM) if half == 0 else (lane >= HEAD_DIM)
    return jnp.where(keep, pair, jnp.zeros_like(pair))


def group_spots(step, pairs, seq):
    spots = []
    for at in range(GROUP):
        number = step * GROUP + at
        sent, pair = lax.div(number, pairs), lax.rem(number, pairs)
        rows = pl.ds(pl.multiple_of(sent * seq, seq), seq)
        spots.append((sent, rows, pl.multiple_of(pair * LANES, LANES)))
    return spots


def join_halves(low, high):
    lane = lax.broadcasted_iota(jnp.int32, low.shape, 1)
    return jnp.where(lane < HEAD_DIM, low, high)


def attend_kernel(links, n_weight, where, lengths, tokens, vec, *refs):
    weight_refs = refs[:n_weight]
    qkv, attended, w_qkv, sem = refs[n_weight:]
    width = tokens.shape[1]
    seq = 256
    sents = tokens.shape[0] // seq
    wide = width * 3 * 2 // links.n_fsdp
    wait_all(load_weight(links, where, weight_refs, 0, wide, w_qkv, sem, steps=False))
    for tile in range(3 * width // 256):
        at = pl.ds(tile * 256, 256)
        product = dot(tokens[...], w_qkv[:, at])
        if tile * 256 < width:
            product = product + vec[0:1, at]
        elif tile * 256 >= 2 * width:
            product = product + vec[1:2, pl.ds(tile * 256 - 2 * width, 256)]
        qkv[:, at] = product.astype(BF16)

    pairs = width // LANES

    def attend(step, carry):
        spots = group_spots(step, pairs, seq)
        scores = []
        for sent, rows, col in spots:
            queries = qkv[rows, pl.ds(col, LANES)] * jnp.asarray(HEAD_DIM ** (-0.5), BF16)
            keys = qkv[rows, pl.ds(col + width, LANES)]
            keep = lax.broadcasted_iota(jnp.int32, (seq, seq), 1) < lengths[sent]
            for half in range(2):
                scores.append(jnp.where(keep, dot_nt(head_half(queries, half), keys), MASKED))
        tops = [jnp.max(item, axis=-1, keepdims=True) for item in scores]
        exponents = [jnp.exp(item - top) for item, top in zip(scores, tops)]
        scales = [1.0 / jnp.sum(item, axis=-1, keepdims=True) for item in exponents]
        probs = [(item * scale).astype(BF16) for item, scale in zip(exponents, scales)]
        for at, (sent, rows, col) in enumerate(spots):
            values = qkv[rows, pl.ds(col + 2 * width, LANES)]
            low, high = (dot(probs[2 * at + half], values) for half in range(2))
            attended[rows, pl.ds(col, LANES)] = join_halves(low, high).astype(BF16)
        return carry

    lax.fori_loop(0, sents * pairs // GROUP, attend, 0)


def up_kernel(links, n_weight, where, attended, tokens, vec, bias, *refs):
    up_refs = refs[:n_weight]
    out_refs = refs[n_weight : 2 * n_weight]
    activated, slope, first_norm, normed, factor = refs[2 * n_weight : 2 * n_weight + 5]
    w_up, w_out, even, odd, sems = refs[2 * n_weight + 5 :]
    width, hidden = w_up.shape
    tile = even.shape[1]
    count = hidden // tile
    wide = hidden * 2 // links.n_fsdp
    copies_out = load_weight(
        links, where, out_refs, wide, width * 2 // links.n_fsdp, w_out, sems.at[1]
    )
    copies = load_weight(links, where, up_refs, 0, wide, w_up, sems.at[0])
    wait_all(copies_out)
    for part in range(tokens.shape[0] // 256):
        rows = pl.ds(part * 256, 256)
        total = tokens[rows, :].astype(F32) + (dot(attended[rows, :], w_out[...]) + vec[2:3, :])
        unit, scale = normalize(total)
        normed[rows, :] = unit.astype(BF16)
        factor[rows, :] = jnp.broadcast_to(scale, (256, LANES))
        first_norm[rows, :] = (unit * vec[3:4, :] + vec[4:5, :]).astype(BF16)
    wait_all(copies)

    def place(step):
        return pl.ds(pl.multiple_of(step * tile, tile), tile)

    def fill(held, step):
        held[...] = dot(first_norm[...], w_up[:, place(step)])

    def drain(held, step):
        at = place(step)
        act, der = gelu_parts(held[...] + bias[:, at])
        activated[:, at] = act.astype(BF16)
        slope[:, at] = der.astype(BF16)

    fill(even, 0)

    def body(step, carry):
        fill(odd, 2 * step + 1)
        drain(even, 2 * step)
        fill(even, lax.rem(2 * step + 2, count))
        drain(odd, 2 * step + 1)
        return carry

    lax.fori_loop(0, count // 2, body, 0)


def down_kernel(links, n_weight, n_grad, where, lengths, depth, prefix, *refs):
    activated, first_norm, tokens, cotangent, vec = refs[:5]
    weight_refs = refs[5 : 5 + n_weight]
    layer_out, pooled, d_down, sums = refs[5 + n_weight : 9 + n_weight]
    grad_refs = refs[9 + n_weight : 9 + n_weight + n_grad]
    w_down, grad, sems = refs[9 + n_weight + n_grad :]
    hidden, width = w_down.shape
    seq = 256
    sents = tokens.shape[0] // seq
    cols = width * 2 // links.n_fsdp
    wait_all(load_weight(links, where, weight_refs, 0, cols, w_down, sems.at[0]))
    sums[...] = jnp.zeros_like(sums)
    columns = lax.broadcasted_iota(jnp.int32, (1, width), 1)
    for sent in range(sents):
        rows = pl.ds(sent * seq, seq)
        total = first_norm[rows, :].astype(F32) + (dot(activated[rows, :], w_down[...]) + vec[5:6, :])
        normed, factor = normalize(total)
        result = normed * vec[6:7, :] + vec[7:8, :]
        layer_out[rows, :] = result.astype(BF16)
        valid = lax.broadcasted_iota(jnp.int32, (seq, width), 0) < lengths[sent]
        source = jnp.where(depth[sent] == 1, result, tokens[rows, :].astype(F32))
        mean = jnp.sum(jnp.where(valid, source, 0.0), axis=0, keepdims=True)
        mean = mean / lengths[sent].astype(F32)
        for at in range(pooled.shape[1]):
            pooled[sent, pl.ds(at, 1), :] = mean * (columns < prefix[at]).astype(F32)
        grad_in = cotangent[rows, :].astype(F32)
        sums[6:7, :] += jnp.sum(grad_in * normed, axis=0, keepdims=True)
        sums[7:8, :] += jnp.sum(grad_in, axis=0, keepdims=True)
        back = norm_back(grad_in * vec[6:7, :], normed, factor)
        low = back.astype(BF16)
        d_down[rows, :] = low
        sums[5:6, :] += jnp.sum(low.astype(F32), axis=0, keepdims=True)

    for step in range(hidden // 768):
        at = pl.ds(step * 768, 768)
        grad[at, :] = dot_tn(activated[:, at], d_down[...]).astype(BF16)
    wait_all(store_grad(links, where, grad, grad_refs, 0, cols, sems.at[1]))


def up_back_kernel(links, n_weight, where, d_down, slope, first_norm, sums_in, *refs):
    weight_refs = refs[:n_weight]
    d_pre, sums, grad, w_down, turned, sem = refs[n_weight:]
    hidden, width = w_down.shape
    copies = load_weight(links, where, weight_refs, 0, width * 2 // links.n_fsdp, w_down, sem)
    sums[...] = sums_in[...]
    turned[...] = first_norm[...].T
    wait_all(copies)

    for step in range(hidden // 512):
        at = pl.ds(step * 512, 512)
        d_act = dot_nt(d_down[...], w_down[at, :])
        low = (d_act * slope[:, at].astype(F32)).astype(BF16)
        d_pre[:, at] = low
        line = jnp.sum(low.astype(F32), axis=0, keepdims=True)
        for part in range(2):
            row, col = divmod(step * 512 + part * 256, width)
            sums[pl.ds(8 + row, 1), pl.ds(col, 256)] = line[:, part * 256 : part * 256 + 256]
        grad[:, at] = dot(turned[...], low).astype(BF16)


def out_back_kernel(links, n_weight, n_grad, where, *refs):
    d_pre, d_down, normed, factor, attended, vec, sums_in, grad_up = refs[:8]
    up_refs = refs[8 : 8 + n_weight]
    out_refs = refs[8 + n_weight : 8 + 2 * n_weight]
    d_attn, d_att, sums = refs[8 + 2 * n_weight : 11 + 2 * n_weight]
    grad_refs = refs[11 + 2 * n_weight : 11 + 2 * n_weight + n_grad]
    w_up, w_out, grad_out, sems = refs[11 + 2 * n_weight + n_grad :]
    width, hidden = w_up.shape
    seq = 256
    wide = hidden * 2 // links.n_fsdp
    copies = load_weight(links, where, up_refs, 0, wide, w_up, sems.at[0])
    copies_out = load_weight(
        links, where, out_refs, wide, width * 2 // links.n_fsdp, w_out, sems.at[1]
    )
    if n_grad > 1:
        copies_up = store_grad(links, where, grad_up, grad_refs, 0, wide, sems.at[3])
    wait_all(copies)
    sums[...] = sums_in[...]
    for part in range(d_pre.shape[0] // seq):
        rows = pl.ds(part * seq, seq)
        d_first = dot_nt(d_pre[rows, :], w_up[...]) + d_down[rows, :].astype(F32)
        unit = normed[rows, :].astype(F32)
        sums[3:4, :] += jnp.sum(d_first * unit, axis=0, keepdims=True)
        sums[4:5, :] += jnp.sum(d_first, axis=0, keepdims=True)
        back = norm_back(d_first * vec[3:4, :], unit, factor[rows, 0:1])
        low = back.astype(BF16)
        d_attn[rows, :] = low
        sums[2:3, :] += jnp.sum(low.astype(F32), axis=0, keepdims=True)
    wait_all(copies_out)
    grad_out[...] = dot_tn(attended[...], d_attn[...]).astype(BF16)
    first = wide if n_grad > 1 else 0
    copies = store_grad(
        links, where, grad_out, grad_refs, first, width * 2 // links.n_fsdp, sems.at[2]
    )
    if n_grad > 1:
        copies += copies_up
    d_att[...] = dot_nt(d_attn[...], w_out[...]).astype(BF16)
    wait_all(copies)


def attend_back_kernel(links, n_grad, where, lengths, qkv, d_att, tokens, sums_in, *refs):
    d_qkv, sums = refs[:2]
    grad_refs = refs[2 : 2 + n_grad]
    turned, grad, held, small, sems = refs[2 + n_grad :]
    width = tokens.shape[1]
    seq = 256
    sents = tokens.shape[0] // seq
    pairs = width // LANES
    wide = width * 3 * 2 // links.n_fsdp
    turned[...] = tokens[...].T
    sums[...] = sums_in[...]
    key_scale = jnp.asarray(HEAD_DIM ** (-0.5), BF16)

    def body(step, carry):
        spots = group_spots(step, pairs, seq)
        loaded, scores, d_probs = [], [], []
        for sent, rows, col in spots:
            queries = qkv[rows, pl.ds(col, LANES)] * key_scale
            keys = qkv[rows, pl.ds(col + width, LANES)]
            values = qkv[rows, pl.ds(col + 2 * width, LANES)]
            d_out = d_att[rows, pl.ds(col, LANES)]
            loaded.append((queries, keys, d_out))
            keep = lax.broadcasted_iota(jnp.int32, (seq, seq), 0) < lengths[sent]
            for half in range(2):
                scores.append(jnp.where(keep, dot_nt(keys, head_half(queries, half)), MASKED))
                d_probs.append(dot_nt(values, head_half(d_out, half)))
        tops = [jnp.max(item, axis=0, keepdims=True) for item in scores]
        exponents = [jnp.exp(item - top) for item, top in zip(scores, tops)]
        scales = [1.0 / jnp.sum(item, axis=0, keepdims=True) for item in exponents]
        probs = [item * scale for item, scale in zip(exponents, scales)]
        row_dots = [jnp.sum(back * prob, axis=0, keepdims=True) for back, prob in zip(d_probs, probs)]
        d_scores = [
            (prob * (back - row_dot)).astype(BF16)
            for prob, back, row_dot in zip(probs, d_probs, row_dots)
        ]
        for at, (sent, rows, col) in enumerate(spots):
            queries, keys, d_out = loaded[at]
            mine = (2 * at, 2 * at + 1)
            d_value = join_halves(*(dot(probs[one].astype(BF16), d_out) for one in mine))
            d_key = join_halves(*(dot(d_scores[one], queries) for one in mine))
            d_query = join_halves(*(dot_tn(d_scores[one], keys) for one in mine))
            d_query = (d_query * (HEAD_DIM ** (-0.5))).astype(BF16)
            d_value = d_value.astype(BF16)
            d_qkv[rows, pl.ds(col, LANES)] = d_query
            d_qkv[rows, pl.ds(col + width, LANES)] = d_key.astype(BF16)
            d_qkv[rows, pl.ds(col + 2 * width, LANES)] = d_value
            sums[0:1, pl.ds(col, LANES)] += jnp.sum(d_query.astype(F32), axis=0, keepdims=True)
            sums[1:2, pl.ds(col, LANES)] += jnp.sum(d_value.astype(F32), axis=0, keepdims=True)
        return carry

    lax.fori_loop(0, sents * pairs // GROUP, body, 0)
    copies = []
    if n_grad > 1:
        held[...] = jnp.zeros_like(held)
        per_device = 8 // links.n_fsdp
        line_rows, line_cols = sums.shape[0] - 8, width // links.n_dp
        for dp, fsdp in itertools.product(range(links.n_dp), range(links.n_fsdp)):
            at = dp * links.n_fsdp + fsdp
            rows = pl.ds(fsdp * per_device, per_device)
            held[at, :per_device, :line_cols] = sums[rows, pl.ds(dp * line_cols, line_cols)]
            first = at * line_cols
            row, col = 8 + first // width, first % width
            held[at, per_device : per_device + 1, :line_cols] = sums[pl.ds(row, 1), pl.ds(col, line_cols)]
        small[...] = held[...].astype(BF16)
        copies = store_small(links, where, small, grad_refs, wide, sems.at[1])
    for step in range(3 * width // 256):
        at = pl.ds(step * 256, 256)
        grad[:, at] = dot(turned[...], d_qkv[:, at]).astype(BF16)
    wait_all(copies + store_grad(links, where, grad, grad_refs, 0, wide, sems.at[0]))


def inputs_kernel(links, n_weight, where, d_qkv, d_attn, *refs):
    weight_refs = refs[:n_weight]
    grad_tokens, w_qkv, sem = refs[n_weight:]
    width = d_attn.shape[1]
    wide = width * 3 * 2 // links.n_fsdp
    wait_all(load_weight(links, where, weight_refs, 0, wide, w_qkv, sem, steps=False))
    for part in range(d_qkv.shape[0] // 256):
        rows = pl.ds(part * 256, 256)
        grad_tokens[rows, :] = (
            dot_nt(d_qkv[rows, :], w_qkv[...]) + d_attn[rows, :].astype(F32)
        ).astype(BF16)


def columns_kernel(plan, where, *refs):
    refs = list(refs)
    mine = where[3] == 0
    sums = []
    for n_parts, spans, extra in plan:
        total = refs.pop(0)[...]
        for _ in range(n_parts - 1):
            total = total + refs.pop(0)[...].astype(F32)
        sums.append(total)
    for total, (_, spans, extra) in zip(sums, plan):
        for first, last in spans:
            middle = (first + last) // 2
            low, high = total[:, first:middle], total[:, middle:last]
            refs.pop(0)[...] = jnp.where(mine, low, high)
            refs.pop(0)[...] = jnp.where(mine, high, low)
        if extra:
            refs.pop(0)[...] = total[:8, -extra:]


def rows_kernel(where, *refs):
    count = len(refs) // 3
    mine = where[3] == 0
    for at in range(count):
        keep, got, out = refs[at], refs[count + at], refs[2 * count + at]
        half = keep.shape[0]
        out[:half, :] = jnp.where(mine, keep[...], got[...])
        out[half:, :] = jnp.where(mine, got[...], keep[...])


SMEM_SPEC = pl.BlockSpec(memory_space=pltpu.SMEM)
VMEM_SPEC = pl.BlockSpec(memory_space=pltpu.VMEM)
ANY_SPEC = pl.BlockSpec(memory_space=pl.ANY)


def call(body, name, outs, scratch, args, vmem, after=(), through=()):
    spec = {"s": SMEM_SPEC, "v": VMEM_SPEC, "a": ANY_SPEC}
    extra = [("a", v) for v in list(through) + list(after)]
    handed = [("a", v) for v in through]
    n_args, n_outs = len(args), len(outs)

    def run(*refs):
        rest = refs[n_args + len(extra) :]
        body(*refs[:n_args], *rest[:n_outs], *rest[n_outs + len(handed) :])

    return list(
        pl.pallas_call(
            run,
            name=name,
            out_shape=[jax.ShapeDtypeStruct(v.shape, v.dtype) for _, v in list(outs) + handed],
            in_specs=[spec[place] for place, _ in list(args) + extra],
            out_specs=[spec[place] for place, _ in list(outs) + handed],
            scratch_shapes=scratch,
            input_output_aliases={n_args + at: n_outs + at for at in range(len(handed))},
            compiler_params=pltpu.CompilerParams(vmem_limit_bytes=vmem * MIB),
            cost_estimate=pl.CostEstimate(flops=1, bytes_accessed=1, transcendentals=0),
        )(*[value for _, value in list(args) + extra])
    )


def hold(arrays, after):
    return call(lambda: None, "hold", [], [], [], 1, after=after, through=arrays)


def owned(links, where, items):
    outs, pairs = [], []
    for parts, spans, extra in items:
        rows = parts[0].shape[0]
        for first, last in spans:
            pairs.append(len(outs))
            outs += 2 * [("v", shaped(rows, (last - first) // 2, dtype=F32))]
        if extra:
            outs.append(("v", shaped(8, extra, dtype=F32)))
    pieces = call(
        partial(columns_kernel, [(len(parts), spans, extra) for parts, spans, extra in items]),
        "columns",
        outs,
        [],
        [("s", where)] + [("v", part) for parts, _, _ in items for part in parts],
        5,
    )
    keep = [pieces[at] for at in pairs]
    got = [links.core(pieces[at + 1]) for at in pairs]
    rows_out = call(
        rows_kernel,
        "rows",
        [("v", shaped(2 * item.shape[0], item.shape[1], dtype=F32)) for item in keep],
        [],
        [("s", where)] + [("v", item) for item in keep + got],
        4,
    )
    return rows_out + [item for at, item in enumerate(pieces) if at not in pairs and at - 1 not in pairs]


def shaped(*shape, dtype=BF16):
    return jax.ShapeDtypeStruct(shape, dtype)


def local(
    n_dp,
    n_fsdp,
    tokens,
    qkv_weight,
    out_weight,
    up_weight,
    up_bias,
    down_weight,
    vectors,
    lengths,
    exit_depth,
    prefix_widths,
    cotangent,
):
    sent_count, seq_len, width = tokens.shape
    rows = sent_count * seq_len
    hidden = up_weight.shape[1] * n_fsdp
    links = Links(n_dp, n_fsdp)
    where = jnp.stack(links.place()).astype(jnp.int32)
    inputs = tokens.reshape(rows, width)
    grad_in = cotangent.reshape(rows, width)
    blocked = qkv_weight.shape[0] % 32 == 0 and out_weight.shape[1] % 64 == 0

    if blocked:
        half = qkv_weight.shape[0] // 2
        parts = down_weight.shape[0] // 2 // half

        def chip_piece(name, shards, extra=(), after=()):
            wide = 2 * sum(item.size for item in shards) // (2 * half)
            theirs = [links.core(item) for item in shards]
            return call(
                partial(piece_kernel, len(shards)),
                name,
                [("v", shaped(half, wide + (LANES if extra else 0)))],
                [],
                [("s", where)] + [("v", item) for item in (*shards, *theirs, *extra)],
                3,
                after=after,
            )[0]

        piece_in = chip_piece("in_piece", [qkv_weight], [vectors, up_bias.reshape(1, -1)])
        far_in = [links.ahead(piece_in, far) for far in range(1, links.rest)]
        own_in = jnp.stack([piece_in] + far_in)
        piece_up = chip_piece(
            "up_piece", [up_weight, out_weight, down_weight], after=far_in[:1]
        )
        pair = jnp.stack([piece_up, links.ahead(piece_up, 1)])
        split = 2 * (up_weight.shape[1] + out_weight.shape[1])
        up_pair = pair[:, :, :split]
        down_pair = jnp.concatenate(jnp.split(pair[:, :, split:], parts, axis=2), axis=1)
        own_up_stack = double_rest(links, up_pair)
        near_in = [own_in, links.along_x(own_in), links.along_y(own_in), links.across(own_in)]
        (down_pair,) = hold([down_pair], [own_up_stack])
        down_far = links.ahead(down_pair, 2)
        up_first, up_second = links.first(own_up_stack), links.second(own_up_stack)
        any_in = [("a", item) for item in spread_cores(links, near_in)]
        vec, bias = call(
            partial(small_kernel, links),
            "small_values",
            [("v", shaped(8, width, dtype=F32)), ("v", shaped(1, hidden, dtype=F32))],
            [pltpu.VMEM((n_dp * n_fsdp, 16, LANES), BF16), pltpu.SemaphoreType.DMA],
            [("s", where)] + any_in,
            3,
            after=[own_up_stack],
        )
    else:

        def whole(shard):
            part = lax.all_gather(shard, "fsdp", axis=1, tiled=True)
            return lax.all_gather(part, "dp", axis=0, tiled=True)

        any_in, any_out, any_up, any_down = (
            [("a", whole(shard))] for shard in (qkv_weight, out_weight, up_weight, down_weight)
        )
        vec = lax.all_gather(vectors, "fsdp", axis=0, tiled=True)
        vec = lax.all_gather(vec, "dp", axis=1, tiled=True).astype(F32)
        bias = lax.all_gather(up_bias, ("dp", "fsdp"), axis=0, tiled=True)
        bias = bias.astype(F32).reshape(1, hidden)
    n_weight = len(any_in)
    n_grad = 2 if blocked else 1

    def grad_outs(shard, *more, extra=0):
        if not blocked:
            return [("a", shaped(shard.shape[0] * n_dp, shard.shape[1] * n_fsdp))]
        cols = shard.shape[1] + sum(item.shape[1] for item in more)
        shape = (links.rest, shard.shape[0] // 2, 2 * cols + extra)
        return 2 * [("a", shaped(2, 2, *shape))]

    small = shaped(8 + -(-hidden // width // 8) * 8, width, dtype=F32)
    one, two = pltpu.SemaphoreType.DMA, pltpu.SemaphoreType.DMA((2,))
    flat = shaped(rows, width)
    lined = ("s", where)

    def room(mib):
        return mib if blocked else 2 * mib

    qkv, attended = call(
        partial(attend_kernel, links, n_weight),
        "attend",
        [("v", shaped(rows, 3 * width)), ("v", flat)],
        [pltpu.VMEM((width, 3 * width), BF16), one],
        [lined, ("s", lengths), ("v", inputs), ("v", vec)] + any_in,
        room(13),
    )
    if blocked:
        up_first, up_second, down_far = hold([up_first, up_second, down_far], [attended])
        own_down_stack = double_rest(links, jnp.concatenate([down_pair, down_far], axis=0))
        up_both = links.second(up_first)
        down_first, down_second = links.first(own_down_stack), links.second(own_down_stack)
        near_up = [own_up_stack, up_first, up_second, up_both]
        any_up = [("a", item) for item in spread_cores(links, near_up)]
        any_out = any_up
    activated, slope, first_norm, normed, factor = call(
        partial(up_kernel, links, n_weight),
        "up",
        [
            ("v", shaped(rows, hidden)),
            ("v", shaped(rows, hidden)),
            ("v", flat),
            ("v", flat),
            ("v", shaped(rows, LANES, dtype=F32)),
        ],
        [pltpu.VMEM((width, hidden), BF16), pltpu.VMEM((width, width), BF16)]
        + [pltpu.VMEM((rows, 512), F32)] * 2
        + [two],
        [lined, ("v", attended), ("v", inputs), ("v", vec), ("v", bias)] + any_up + any_out,
        room(17),
        after=[down_first] if blocked else [],
    )
    if blocked:
        down_both = links.second(down_first)
        down_second, down_both = hold([down_second, down_both], [activated])
        near_down = [own_down_stack, down_first, down_second, down_both]
        any_down = [("a", item) for item in spread_cores(links, near_down)]
    down = call(
        partial(down_kernel, links, n_weight, n_grad),
        "down",
        [
            ("v", flat),
            ("v", shaped(sent_count, prefix_widths.shape[0], width, dtype=F32)),
            ("v", flat),
            ("v", small),
        ]
        + grad_outs(down_weight),
        [pltpu.VMEM((hidden, width), BF16), pltpu.VMEM((hidden, width), BF16), two],
        [lined, ("s", lengths), ("s", exit_depth), ("s", prefix_widths)]
        + [("v", activated), ("v", first_norm), ("v", inputs), ("v", grad_in), ("v", vec)]
        + any_down,
        room(19),
    )
    layer_out, pooled, d_down, sums_down = down[:4]
    grad_down = down[4:]
    if blocked:
        sum_down = Collect(links, *grad_down)
        sum_down.add_cores()

    d_pre, sums_up, grad_up = call(
        partial(up_back_kernel, links, n_weight),
        "up_back",
        [("v", shaped(rows, hidden)), ("v", small), ("v", shaped(width, hidden))],
        [pltpu.VMEM((hidden, width), BF16), pltpu.VMEM((width, rows), BF16), one],
        [lined, ("v", d_down), ("v", slope), ("v", first_norm), ("v", sums_down)] + any_down,
        room(16),
        after=sum_down.halves if blocked else [],
    )
    d_attn, d_att, sums_out, *grad_out = call(
        partial(out_back_kernel, links, n_weight, n_grad),
        "out_back",
        [("v", flat), ("v", flat), ("v", small)]
        + (grad_outs(up_weight, out_weight) if blocked else grad_outs(out_weight)),
        [
            pltpu.VMEM((width, hidden), BF16),
            pltpu.VMEM((width, width), BF16),
            pltpu.VMEM((width, width), BF16),
            pltpu.SemaphoreType.DMA((4,)),
        ],
        [lined]
        + [("v", item) for item in (d_pre, d_down, normed, factor, attended, vec, sums_up, grad_up)]
        + any_up
        + any_out,
        room(17),
    )
    if blocked:
        sum_up = Collect(links, grad_out[0], *hold(grad_out[1:], sum_down.near))
        sum_up.add_cores()
        sum_down.add_chips()
        sum_down.halve()
    attend_back = call(
        partial(attend_back_kernel, links, n_grad),
        "attend_back",
        [("v", shaped(rows, 3 * width)), ("v", small)]
        + grad_outs(qkv_weight, extra=LANES),
        [
            pltpu.VMEM((width, rows), BF16),
            pltpu.VMEM((width, 3 * width), BF16),
            pltpu.VMEM((n_dp * n_fsdp, 16, LANES), F32),
            pltpu.VMEM((n_dp * n_fsdp, 16, LANES), BF16),
            two,
        ],
        [lined, ("s", lengths), ("v", qkv), ("v", d_att), ("v", inputs), ("v", sums_out)],
        room(17),
        after=sum_up.halves + [sum_down.far] if blocked else [],
    )
    d_qkv, sums_in = attend_back[:2]
    grad_in_blocks = attend_back[2:]
    if blocked:
        (sum_down.back,) = hold([sum_down.back], [sums_in])
        sum_down.add_half()
        sum_down.halve()
    (grad_tokens,) = call(
        partial(inputs_kernel, links, n_weight),
        "inputs",
        [("v", flat)],
        [pltpu.VMEM((width, 3 * width), BF16), one],
        [lined, ("v", d_qkv), ("v", d_attn)] + any_in,
        room(10),
        after=[sum_down.far] if blocked else [],
    )

    if blocked:
        passed = hold([grad_in_blocks[1], sum_down.back] + sum_up.near, [grad_tokens])
        give, sum_down.back, *sum_up.near = passed
        sum_in = Collect(links, grad_in_blocks[0], give)
        sum_in.add_cores()
        sum_up.near = hold(sum_up.near, sum_in.halves)
        sum_up.add_chips()
        sum_up.halve()
        *sum_in.near, sum_up.back = hold(sum_in.near + [sum_up.back], [])
        sum_in.add_chips()
        sum_in.direct()
        sum_up.back, sum_down.back = hold([sum_up.back, sum_down.back], sum_in.blocks)
        for item in (sum_up, sum_down):
            item.add_half()
            while item.total.shape[0] > 1:
                item.halve()
                item.add_half()
        wide = 2 * qkv_weight.shape[1]
        split, total = 2 * up_weight.shape[1], 2 * (up_weight.shape[1] + out_weight.shape[1])
        own_qkv, own_up, own_out, own_down, last = owned(
            links,
            where,
            [
                ([sum_in.total[0]] + sum_in.ahead, [(0, wide)], LANES),
                ([sum_up.total[0]], [(0, split), (split, total)], 0),
                ([sum_down.total[0]], [(0, 2 * down_weight.shape[1])], 0),
            ],
        )
        own_vec = last[: vectors.shape[0], : vectors.shape[1]]
        own_bias = last[vectors.shape[0], : up_bias.shape[0]]
    else:

        def scattered(grad):
            part = lax.psum_scatter(grad, "dp", scatter_dimension=0, tiled=True)
            part = lax.psum_scatter(part, "fsdp", scatter_dimension=1, tiled=True)
            return part.astype(F32)

        own_down, own_up, own_out, own_qkv = (
            scattered(item) for item in (grad_down[0], grad_up, grad_out[0], grad_in_blocks[0])
        )
        every = lax.psum(sums_in, ("dp", "fsdp"))
        dp, fsdp = lax.axis_index("dp"), lax.axis_index("fsdp")
        own_vec = lax.dynamic_slice(
            every, (fsdp * vectors.shape[0], dp * vectors.shape[1]), vectors.shape
        )
        own_bias = lax.dynamic_slice_in_dim(
            every[8:].reshape(-1), (dp * n_fsdp + fsdp) * up_bias.shape[0], up_bias.shape[0], 0
        )
    return (
        layer_out.reshape(tokens.shape),
        pooled,
        grad_tokens.reshape(tokens.shape),
        own_qkv,
        own_out,
        own_up,
        own_bias,
        own_down,
        own_vec,
    )


def solution(mesh):
    placed = (
        P(("dp", "fsdp"), None, None),
        P("dp", "fsdp"),
        P("dp", "fsdp"),
        P("dp", "fsdp"),
        P(("dp", "fsdp")),
        P("dp", "fsdp"),
        P("fsdp", "dp"),
        P(("dp", "fsdp")),
        P(("dp", "fsdp")),
        P(),
        P(("dp", "fsdp"), None, None),
    )
    return jax.shard_map(
        partial(local, mesh.shape["dp"], mesh.shape["fsdp"]),
        mesh=mesh,
        in_specs=placed,
        out_specs=(
            P(("dp", "fsdp"), None, None),
            P(("dp", "fsdp"), None, None),
            P(("dp", "fsdp"), None, None),
            P("dp", "fsdp"),
            P("dp", "fsdp"),
            P("dp", "fsdp"),
            P(("dp", "fsdp")),
            P("dp", "fsdp"),
            P("fsdp", "dp"),
        ),
        check_vma=False,
    )
```

```python
import itertools
from functools import partial

import jax
import jax.numpy as jnp
from jax import lax
from jax.experimental import pallas as pl
from jax.experimental.pallas import tpu as pltpu
from jax.sharding import PartitionSpec as P

HEAD_DIM = 64
EPS = 1e-05
MASKED = -1000000000.0
F32 = jnp.float32
BF16 = jnp.bfloat16
MIB = 1024 * 1024
LANES = 128
GROUP = 3


class Links:
    def __init__(self, n_dp, n_fsdp):
        self.n_dp, self.n_fsdp = n_dp, n_fsdp
        self.high = n_fsdp // 4
        self.rest = (n_dp // 2) * self.high

    def number(self, rest, y, x, core):
        z, high = divmod(rest, self.high)
        return (z * 2 + y) * self.n_fsdp + (high * 2 + x) * 2 + core

    def pairs(self, step):
        return [
            (self.number(*place), self.number(*step(*place)))
            for place in itertools.product(range(self.rest), range(2), range(2), range(2))
        ]

    def move(self, value, step):
        return lax.ppermute(value, ("dp", "fsdp"), self.pairs(step))

    def core(self, value):
        return self.move(value, lambda q, y, x, c: (q, y, x, 1 - c))

    def along_x(self, value):
        return self.move(value, lambda q, y, x, c: (q, y, 1 - x, c))

    def along_y(self, value):
        return self.move(value, lambda q, y, x, c: (q, 1 - y, x, c))

    def across(self, value):
        return self.move(value, lambda q, y, x, c: (q, 1 - y, 1 - x, c))

    def first(self, value):
        return self.move(value, lambda q, y, x, c: (q, 1 - y, x, c) if c else (q, y, 1 - x, c))

    def second(self, value):
        return self.move(value, lambda q, y, x, c: (q, y, 1 - x, c) if c else (q, 1 - y, x, c))

    def flip(self, value, bit):
        return self.move(value, lambda q, y, x, c: (q ^ bit, y, x, c))

    def ahead(self, value, far):
        return self.move(value, lambda q, y, x, c: ((q + far) % self.rest, y, x, c))

    def place(self):
        dp, fsdp = lax.axis_index("dp"), lax.axis_index("fsdp")
        rest = (dp // 2) * self.high + fsdp // 4
        return rest, dp % 2, (fsdp // 2) % 2, fsdp % 2


def double_rest(links, stack):
    while stack.shape[0] < links.rest:
        stack = jnp.concatenate([stack, links.ahead(stack, stack.shape[0])], axis=0)
    return stack


def spread_cores(links, near):
    return list(near) + [links.core(item) for item in near]


class Collect:
    def __init__(self, links, keep, give):
        self.links, self.keep = links, keep
        self.got = [links.core(item) for item in give]

    def add_cores(self):
        halves = [
            (keep.astype(F32) + got.astype(F32)).astype(BF16)
            for keep, got in zip(self.keep[1:], self.got[1:])
        ]
        self.halves = halves
        links = self.links
        self.near = [
            links.along_x(halves[0]),
            links.along_y(halves[1]),
            links.across(halves[2]),
        ]

    def add_chips(self):
        total = self.keep[0].astype(F32) + self.got[0].astype(F32)
        for item in self.near:
            total = total + item.astype(F32)
        self.total = total

    def direct(self):
        self.blocks = [self.total[far].astype(BF16) for far in range(1, self.links.rest)]
        self.ahead = [self.links.ahead(item, at + 1) for at, item in enumerate(self.blocks)]

    def halve(self):
        half = self.total.shape[0] // 2
        self.far = self.total[half:].astype(BF16)
        self.total = self.total[:half]
        self.back = self.links.ahead(self.far, half)

    def add_half(self):
        self.total = self.total + self.back.astype(F32)


class Blocks:
    def __init__(self, links, where):
        self.links = links
        self.rest, self.y, self.x, self.core = where[0], where[1], where[2], where[3]

    def device(self, other, flip_y, flip_x, far, sign):
        links = self.links
        core = jnp.bitwise_xor(self.core, other)
        rest = lax.rem(self.rest + (sign * far + links.rest), links.rest)
        x, y = jnp.bitwise_xor(self.x, flip_x), jnp.bitwise_xor(self.y, flip_y)
        dp = lax.div(rest, links.high) * 2 + y
        return dp, lax.rem(rest, links.high) * 2 + x, core

    def corner(self, rows, cols, *spot):
        dp, wide, core = self.device(*spot)
        return pl.multiple_of((dp * 2 + core) * rows, rows), pl.multiple_of(wide * cols, cols)


def load_weight(links, where, refs, first_col, cols, out, sem, steps=True):
    if len(refs) == 1:
        copies = [pltpu.make_async_copy(refs[0], out, sem)]
    else:
        blocks = Blocks(links, where)
        rows = refs[0].shape[1]
        copies = []
        for stack, far in itertools.product(range(8), range(links.rest)):
            other, high, low = stack // 4, (stack // 2) % 2, stack % 2
            if not steps:
                high, low = 1 - high, 1 - low
            else:
                core = jnp.bitwise_xor(blocks.core, other)
                high, low = jnp.where(core == 0, high, low), jnp.where(core == 0, low, high)
            row, col = blocks.corner(rows, cols, other, high, low, far, -1)
            copies.append(
                pltpu.make_async_copy(
                    refs[stack].at[far, :, pl.ds(first_col, cols)],
                    out.at[pl.ds(row, rows), pl.ds(col, cols)],
                    sem,
                )
            )
    for copy in copies:
        copy.start()
    return copies


def store_grad(links, where, grad, refs, first_col, cols, sem):
    if len(refs) == 1:
        copies = [pltpu.make_async_copy(grad, refs[0], sem)]
    else:
        blocks = Blocks(links, where)
        rows = refs[0].shape[1]
        copies = []
        for other, y, x, far in itertools.product(range(2), range(2), range(2), range(links.rest)):
            row, col = blocks.corner(rows, cols, other, y, x, far, 1)
            out = refs[4 * other + 2 * y + x].at[far]
            copies.append(
                pltpu.make_async_copy(
                    grad.at[pl.ds(row, rows), pl.ds(col, cols)],
                    out.at[:, pl.ds(first_col, cols)],
                    sem,
                )
            )
    for copy in copies:
        copy.start()
    return copies


def store_small(links, where, small, refs, first_col, sem):
    blocks = Blocks(links, where)
    copies = []
    for other, y, x, far in itertools.product(range(2), range(2), range(2), range(links.rest)):
        dp, wide, core = blocks.device(other, y, x, far, 1)
        target = refs[4 * other + 2 * y + x].at[far, pl.ds(0, 16), pl.ds(first_col, LANES)]
        source = small.at[dp * links.n_fsdp + wide * 2 + core]
        copies.append(pltpu.make_async_copy(source, target, sem))
    for copy in copies:
        copy.start()
    return copies


def wait_all(copies):
    for copy in copies:
        copy.wait()


def dot(left, right):
    return lax.dot_general(left, right, (((1,), (0,)), ((), ())), preferred_element_type=F32)


def dot_nt(left, right):
    return lax.dot_general(left, right, (((1,), (1,)), ((), ())), preferred_element_type=F32)


def dot_tn(left, right):
    return lax.dot_general(left, right, (((0,), (0,)), ((), ())), preferred_element_type=F32)


def normalize(hidden):
    centered = hidden - jnp.mean(hidden, axis=-1, keepdims=True)
    factor = lax.rsqrt(jnp.mean(centered * centered, axis=-1, keepdims=True) + EPS)
    return centered * factor, factor


def norm_back(scaled, normed, factor):
    return factor * (
        scaled
        - jnp.mean(scaled, axis=-1, keepdims=True)
        - normed * jnp.mean(scaled * normed, axis=-1, keepdims=True)
    )


def gelu_parts(value):
    bell = jnp.exp(-0.5 * value * value)
    weight = 0.5 + 0.5 * lax.erf(value * 0.7071067811865476)
    return value * weight, weight + value * (bell * 0.3989422804014327)


def piece_kernel(n_shards, where, *refs):
    mine, theirs = refs[:n_shards], refs[n_shards : 2 * n_shards]
    *extra, piece = refs[2 * n_shards :]
    core = where[3]
    half = mine[0].shape[0] // 2
    lines = []
    for keep, got in zip(mine, theirs):
        times = keep.shape[0] // 2 // half
        for at in range(times):
            row = pl.multiple_of(core * half * times + at * half, half)
            low, high = keep[pl.ds(row, half), :], got[pl.ds(row, half), :]
            lines += [jnp.where(core == 0, low, high), jnp.where(core == 0, high, low)]
    if extra:
        line = jnp.concatenate([item[...].astype(F32) for item in extra], axis=0)
        below = jnp.zeros((half - line.shape[0], line.shape[1]), F32)
        line = jnp.concatenate([line, below], axis=0)
        beside = jnp.zeros((line.shape[0], LANES - line.shape[1]), F32)
        lines.append(jnp.concatenate([line, beside], axis=1).astype(BF16))
    piece[...] = jnp.concatenate(lines, axis=1)


def small_kernel(links, where, *refs):
    stacks, vec_out, bias_out, held, sem = refs[:8], *refs[8:]
    blocks = Blocks(links, where)
    first_col = stacks[0].shape[2] - LANES
    copies = []
    for stack, far in itertools.product(range(8), range(links.rest)):
        dp, wide, core = blocks.device(stack // 4, 1 - (stack // 2) % 2, 1 - stack % 2, far, -1)
        copies.append(
            pltpu.make_async_copy(
                stacks[stack].at[far, pl.ds(0, 16), pl.ds(first_col, LANES)],
                held.at[dp * links.n_fsdp + wide * 2 + core],
                sem,
            )
        )
    for copy in copies:
        copy.start()
    wait_all(copies)
    rows, width = 8 // links.n_fsdp, vec_out.shape[1] // links.n_dp
    got = [held[at].astype(F32)[:, :width] for at in range(links.n_dp * links.n_fsdp)]
    for fsdp in range(links.n_fsdp):
        line = jnp.concatenate([got[dp * links.n_fsdp + fsdp] for dp in range(links.n_dp)], axis=1)
        vec_out[pl.ds(rows * fsdp, rows), :] = line[:rows]
    bias_out[...] = jnp.concatenate(got, axis=1)[rows : rows + 1]


def head_half(pair, half):
    lane = lax.broadcasted_iota(jnp.int32, pair.shape, 1)
    keep = (lane < HEAD_DIM) if half == 0 else (lane >= HEAD_DIM)
    return jnp.where(keep, pair, jnp.zeros_like(pair))


def group_spots(step, pairs, seq):
    spots = []
    for at in range(GROUP):
        number = step * GROUP + at
        sent, pair = lax.div(number, pairs), lax.rem(number, pairs)
        rows = pl.ds(pl.multiple_of(sent * seq, seq), seq)
        spots.append((sent, rows, pl.multiple_of(pair * LANES, LANES)))
    return spots


def join_halves(low, high):
    lane = lax.broadcasted_iota(jnp.int32, low.shape, 1)
    return jnp.where(lane < HEAD_DIM, low, high)


def attend_kernel(links, n_weight, where, lengths, tokens, vec, *refs):
    weight_refs = refs[:n_weight]
    qkv, attended, w_qkv, sem = refs[n_weight:]
    width = tokens.shape[1]
    seq = 256
    sents = tokens.shape[0] // seq
    wide = width * 3 * 2 // links.n_fsdp
    wait_all(load_weight(links, where, weight_refs, 0, wide, w_qkv, sem, steps=False))
    for tile in range(3 * width // 256):
        at = pl.ds(tile * 256, 256)
        product = dot(tokens[...], w_qkv[:, at])
        if tile * 256 < width:
            product = product + vec[0:1, at]
        elif tile * 256 >= 2 * width:
            product = product + vec[1:2, pl.ds(tile * 256 - 2 * width, 256)]
        qkv[:, at] = product.astype(BF16)

    pairs = width // LANES

    def attend(step, carry):
        spots = group_spots(step, pairs, seq)
        scores = []
        for sent, rows, col in spots:
            queries = qkv[rows, pl.ds(col, LANES)] * jnp.asarray(HEAD_DIM ** (-0.5), BF16)
            keys = qkv[rows, pl.ds(col + width, LANES)]
            keep = lax.broadcasted_iota(jnp.int32, (seq, seq), 1) < lengths[sent]
            for half in range(2):
                scores.append(jnp.where(keep, dot_nt(head_half(queries, half), keys), MASKED))
        tops = [jnp.max(item, axis=-1, keepdims=True) for item in scores]
        exponents = [jnp.exp(item - top) for item, top in zip(scores, tops)]
        scales = [1.0 / jnp.sum(item, axis=-1, keepdims=True) for item in exponents]
        probs = [(item * scale).astype(BF16) for item, scale in zip(exponents, scales)]
        for at, (sent, rows, col) in enumerate(spots):
            values = qkv[rows, pl.ds(col + 2 * width, LANES)]
            low, high = (dot(probs[2 * at + half], values) for half in range(2))
            attended[rows, pl.ds(col, LANES)] = join_halves(low, high).astype(BF16)
        return carry

    lax.fori_loop(0, sents * pairs // GROUP, attend, 0)


def up_kernel(links, n_weight, where, attended, tokens, vec, bias, *refs):
    up_refs = refs[:n_weight]
    out_refs = refs[n_weight : 2 * n_weight]
    activated, slope, first_norm, normed, factor = refs[2 * n_weight : 2 * n_weight + 5]
    w_up, w_out, even, odd, sems = refs[2 * n_weight + 5 :]
    width, hidden = w_up.shape
    tile = even.shape[1]
    count = hidden // tile
    wide = hidden * 2 // links.n_fsdp
    copies_out = load_weight(
        links, where, out_refs, wide, width * 2 // links.n_fsdp, w_out, sems.at[1]
    )
    copies = load_weight(links, where, up_refs, 0, wide, w_up, sems.at[0])
    wait_all(copies_out)
    for part in range(tokens.shape[0] // 256):
        rows = pl.ds(part * 256, 256)
        total = tokens[rows, :].astype(F32) + (dot(attended[rows, :], w_out[...]) + vec[2:3, :])
        unit, scale = normalize(total)
        normed[rows, :] = unit.astype(BF16)
        factor[rows, :] = jnp.broadcast_to(scale, (256, LANES))
        first_norm[rows, :] = (unit * vec[3:4, :] + vec[4:5, :]).astype(BF16)
    wait_all(copies)

    def place(step):
        return pl.ds(pl.multiple_of(step * tile, tile), tile)

    def fill(held, step):
        held[...] = dot(first_norm[...], w_up[:, place(step)])

    def drain(held, step):
        at = place(step)
        act, der = gelu_parts(held[...] + bias[:, at])
        activated[:, at] = act.astype(BF16)
        slope[:, at] = der.astype(BF16)

    fill(even, 0)

    def body(step, carry):
        fill(odd, 2 * step + 1)
        drain(even, 2 * step)
        fill(even, lax.rem(2 * step + 2, count))
        drain(odd, 2 * step + 1)
        return carry

    lax.fori_loop(0, count // 2, body, 0)


def down_kernel(links, n_weight, n_grad, where, lengths, depth, prefix, *refs):
    activated, first_norm, tokens, cotangent, vec = refs[:5]
    weight_refs = refs[5 : 5 + n_weight]
    layer_out, pooled, d_down, sums = refs[5 + n_weight : 9 + n_weight]
    grad_refs = refs[9 + n_weight : 9 + n_weight + n_grad]
    w_down, grad, sems = refs[9 + n_weight + n_grad :]
    hidden, width = w_down.shape
    seq = 256
    sents = tokens.shape[0] // seq
    cols = width * 2 // links.n_fsdp
    wait_all(load_weight(links, where, weight_refs, 0, cols, w_down, sems.at[0]))
    sums[...] = jnp.zeros_like(sums)
    columns = lax.broadcasted_iota(jnp.int32, (1, width), 1)
    for sent in range(sents):
        rows = pl.ds(sent * seq, seq)
        total = first_norm[rows, :].astype(F32) + (dot(activated[rows, :], w_down[...]) + vec[5:6, :])
        normed, factor = normalize(total)
        result = normed * vec[6:7, :] + vec[7:8, :]
        layer_out[rows, :] = result.astype(BF16)
        valid = lax.broadcasted_iota(jnp.int32, (seq, width), 0) < lengths[sent]
        source = jnp.where(depth[sent] == 1, result, tokens[rows, :].astype(F32))
        mean = jnp.sum(jnp.where(valid, source, 0.0), axis=0, keepdims=True)
        mean = mean / lengths[sent].astype(F32)
        for at in range(pooled.shape[1]):
            pooled[sent, pl.ds(at, 1), :] = mean * (columns < prefix[at]).astype(F32)
        grad_in = cotangent[rows, :].astype(F32)
        sums[6:7, :] += jnp.sum(grad_in * normed, axis=0, keepdims=True)
        sums[7:8, :] += jnp.sum(grad_in, axis=0, keepdims=True)
        back = norm_back(grad_in * vec[6:7, :], normed, factor)
        low = back.astype(BF16)
        d_down[rows, :] = low
        sums[5:6, :] += jnp.sum(low.astype(F32), axis=0, keepdims=True)

    for step in range(hidden // 768):
        at = pl.ds(step * 768, 768)
        grad[at, :] = dot_tn(activated[:, at], d_down[...]).astype(BF16)
    wait_all(store_grad(links, where, grad, grad_refs, 0, cols, sems.at[1]))


def up_back_kernel(links, n_weight, where, d_down, slope, first_norm, sums_in, *refs):
    weight_refs = refs[:n_weight]
    d_pre, sums, grad, w_down, turned, sem = refs[n_weight:]
    hidden, width = w_down.shape
    copies = load_weight(links, where, weight_refs, 0, width * 2 // links.n_fsdp, w_down, sem)
    sums[...] = sums_in[...]
    turned[...] = first_norm[...].T
    wait_all(copies)

    for step in range(hidden // 512):
        at = pl.ds(step * 512, 512)
        d_act = dot_nt(d_down[...], w_down[at, :])
        low = (d_act * slope[:, at].astype(F32)).astype(BF16)
        d_pre[:, at] = low
        line = jnp.sum(low.astype(F32), axis=0, keepdims=True)
        for part in range(2):
            row, col = divmod(step * 512 + part * 256, width)
            sums[pl.ds(8 + row, 1), pl.ds(col, 256)] = line[:, part * 256 : part * 256 + 256]
        grad[:, at] = dot(turned[...], low).astype(BF16)


def out_back_kernel(links, n_weight, n_grad, where, *refs):
    d_pre, d_down, normed, factor, attended, vec, sums_in, grad_up = refs[:8]
    up_refs = refs[8 : 8 + n_weight]
    out_refs = refs[8 + n_weight : 8 + 2 * n_weight]
    d_attn, d_att, sums = refs[8 + 2 * n_weight : 11 + 2 * n_weight]
    grad_refs = refs[11 + 2 * n_weight : 11 + 2 * n_weight + n_grad]
    w_up, w_out, grad_out, sems = refs[11 + 2 * n_weight + n_grad :]
    width, hidden = w_up.shape
    seq = 256
    wide = hidden * 2 // links.n_fsdp
    copies = load_weight(links, where, up_refs, 0, wide, w_up, sems.at[0])
    copies_out = load_weight(
        links, where, out_refs, wide, width * 2 // links.n_fsdp, w_out, sems.at[1]
    )
    if n_grad > 1:
        copies_up = store_grad(links, where, grad_up, grad_refs, 0, wide, sems.at[3])
    wait_all(copies)
    sums[...] = sums_in[...]
    for part in range(d_pre.shape[0] // seq):
        rows = pl.ds(part * seq, seq)
        d_first = dot_nt(d_pre[rows, :], w_up[...]) + d_down[rows, :].astype(F32)
        unit = normed[rows, :].astype(F32)
        sums[3:4, :] += jnp.sum(d_first * unit, axis=0, keepdims=True)
        sums[4:5, :] += jnp.sum(d_first, axis=0, keepdims=True)
        back = norm_back(d_first * vec[3:4, :], unit, factor[rows, 0:1])
        low = back.astype(BF16)
        d_attn[rows, :] = low
        sums[2:3, :] += jnp.sum(low.astype(F32), axis=0, keepdims=True)
    wait_all(copies_out)
    grad_out[...] = dot_tn(attended[...], d_attn[...]).astype(BF16)
    first = wide if n_grad > 1 else 0
    copies = store_grad(
        links, where, grad_out, grad_refs, first, width * 2 // links.n_fsdp, sems.at[2]
    )
    if n_grad > 1:
        copies += copies_up
    d_att[...] = dot_nt(d_attn[...], w_out[...]).astype(BF16)
    wait_all(copies)


def attend_back_kernel(links, n_grad, where, lengths, qkv, d_att, tokens, sums_in, *refs):
    d_qkv, sums = refs[:2]
    grad_refs = refs[2 : 2 + n_grad]
    turned, grad, held, small, sems = refs[2 + n_grad :]
    width = tokens.shape[1]
    seq = 256
    sents = tokens.shape[0] // seq
    pairs = width // LANES
    wide = width * 3 * 2 // links.n_fsdp
    turned[...] = tokens[...].T
    sums[...] = sums_in[...]
    key_scale = jnp.asarray(HEAD_DIM ** (-0.5), BF16)

    def body(step, carry):
        spots = group_spots(step, pairs, seq)
        loaded, scores, d_probs = [], [], []
        for sent, rows, col in spots:
            queries = qkv[rows, pl.ds(col, LANES)] * key_scale
            keys = qkv[rows, pl.ds(col + width, LANES)]
            values = qkv[rows, pl.ds(col + 2 * width, LANES)]
            d_out = d_att[rows, pl.ds(col, LANES)]
            loaded.append((queries, keys, d_out))
            keep = lax.broadcasted_iota(jnp.int32, (seq, seq), 0) < lengths[sent]
            for half in range(2):
                scores.append(jnp.where(keep, dot_nt(keys, head_half(queries, half)), MASKED))
                d_probs.append(dot_nt(values, head_half(d_out, half)))
        tops = [jnp.max(item, axis=0, keepdims=True) for item in scores]
        exponents = [jnp.exp(item - top) for item, top in zip(scores, tops)]
        scales = [1.0 / jnp.sum(item, axis=0, keepdims=True) for item in exponents]
        probs = [item * scale for item, scale in zip(exponents, scales)]
        row_dots = [jnp.sum(back * prob, axis=0, keepdims=True) for back, prob in zip(d_probs, probs)]
        d_scores = [
            (prob * (back - row_dot)).astype(BF16)
            for prob, back, row_dot in zip(probs, d_probs, row_dots)
        ]
        for at, (sent, rows, col) in enumerate(spots):
            queries, keys, d_out = loaded[at]
            mine = (2 * at, 2 * at + 1)
            d_value = join_halves(*(dot(probs[one].astype(BF16), d_out) for one in mine))
            d_key = join_halves(*(dot(d_scores[one], queries) for one in mine))
            d_query = join_halves(*(dot_tn(d_scores[one], keys) for one in mine))
            d_query = (d_query * (HEAD_DIM ** (-0.5))).astype(BF16)
            d_value = d_value.astype(BF16)
            d_qkv[rows, pl.ds(col, LANES)] = d_query
            d_qkv[rows, pl.ds(col + width, LANES)] = d_key.astype(BF16)
            d_qkv[rows, pl.ds(col + 2 * width, LANES)] = d_value
            sums[0:1, pl.ds(col, LANES)] += jnp.sum(d_query.astype(F32), axis=0, keepdims=True)
            sums[1:2, pl.ds(col, LANES)] += jnp.sum(d_value.astype(F32), axis=0, keepdims=True)
        return carry

    lax.fori_loop(0, sents * pairs // GROUP, body, 0)
    copies = []
    if n_grad > 1:
        held[...] = jnp.zeros_like(held)
        per_device = 8 // links.n_fsdp
        line_rows, line_cols = sums.shape[0] - 8, width // links.n_dp
        for dp, fsdp in itertools.product(range(links.n_dp), range(links.n_fsdp)):
            at = dp * links.n_fsdp + fsdp
            rows = pl.ds(fsdp * per_device, per_device)
            held[at, :per_device, :line_cols] = sums[rows, pl.ds(dp * line_cols, line_cols)]
            first = at * line_cols
            row, col = 8 + first // width, first % width
            held[at, per_device : per_device + 1, :line_cols] = sums[pl.ds(row, 1), pl.ds(col, line_cols)]
        small[...] = held[...].astype(BF16)
        copies = store_small(links, where, small, grad_refs, wide, sems.at[1])
    for step in range(3 * width // 256):
        at = pl.ds(step * 256, 256)
        grad[:, at] = dot(turned[...], d_qkv[:, at]).astype(BF16)
    wait_all(copies + store_grad(links, where, grad, grad_refs, 0, wide, sems.at[0]))


def inputs_kernel(links, n_weight, where, d_qkv, d_attn, *refs):
    weight_refs = refs[:n_weight]
    grad_tokens, w_qkv, sem = refs[n_weight:]
    width = d_attn.shape[1]
    wide = width * 3 * 2 // links.n_fsdp
    wait_all(load_weight(links, where, weight_refs, 0, wide, w_qkv, sem, steps=False))
    for part in range(d_qkv.shape[0] // 256):
        rows = pl.ds(part * 256, 256)
        grad_tokens[rows, :] = (
            dot_nt(d_qkv[rows, :], w_qkv[...]) + d_attn[rows, :].astype(F32)
        ).astype(BF16)


def columns_kernel(plan, where, *refs):
    refs = list(refs)
    mine = where[3] == 0
    sums = []
    for n_parts, spans, extra in plan:
        total = refs.pop(0)[...]
        for _ in range(n_parts - 1):
            total = total + refs.pop(0)[...].astype(F32)
        sums.append(total)
    for total, (_, spans, extra) in zip(sums, plan):
        for first, last in spans:
            middle = (first + last) // 2
            low, high = total[:, first:middle], total[:, middle:last]
            refs.pop(0)[...] = jnp.where(mine, low, high)
            refs.pop(0)[...] = jnp.where(mine, high, low)
        if extra:
            refs.pop(0)[...] = total[:8, -extra:]


def rows_kernel(where, *refs):
    count = len(refs) // 3
    mine = where[3] == 0
    for at in range(count):
        keep, got, out = refs[at], refs[count + at], refs[2 * count + at]
        half = keep.shape[0]
        out[:half, :] = jnp.where(mine, keep[...], got[...])
        out[half:, :] = jnp.where(mine, got[...], keep[...])


SMEM_SPEC = pl.BlockSpec(memory_space=pltpu.SMEM)
VMEM_SPEC = pl.BlockSpec(memory_space=pltpu.VMEM)
ANY_SPEC = pl.BlockSpec(memory_space=pl.ANY)


def call(body, name, outs, scratch, args, vmem, after=(), through=()):
    spec = {"s": SMEM_SPEC, "v": VMEM_SPEC, "a": ANY_SPEC}
    extra = [("a", v) for v in list(through) + list(after)]
    handed = [("a", v) for v in through]
    n_args, n_outs = len(args), len(outs)

    def run(*refs):
        rest = refs[n_args + len(extra) :]
        body(*refs[:n_args], *rest[:n_outs], *rest[n_outs + len(handed) :])

    return list(
        pl.pallas_call(
            run,
            name=name,
            out_shape=[jax.ShapeDtypeStruct(v.shape, v.dtype) for _, v in list(outs) + handed],
            in_specs=[spec[place] for place, _ in list(args) + extra],
            out_specs=[spec[place] for place, _ in list(outs) + handed],
            scratch_shapes=scratch,
            input_output_aliases={n_args + at: n_outs + at for at in range(len(handed))},
            compiler_params=pltpu.CompilerParams(vmem_limit_bytes=vmem * MIB),
            cost_estimate=pl.CostEstimate(flops=1, bytes_accessed=1, transcendentals=0),
        )(*[value for _, value in list(args) + extra])
    )


def hold(arrays, after):
    return call(lambda: None, "hold", [], [], [], 1, after=after, through=arrays)


def owned(links, where, items):
    outs, pairs = [], []
    for parts, spans, extra in items:
        rows = parts[0].shape[0]
        for first, last in spans:
            pairs.append(len(outs))
            outs += 2 * [("v", shaped(rows, (last - first) // 2, dtype=F32))]
        if extra:
            outs.append(("v", shaped(8, extra, dtype=F32)))
    pieces = call(
        partial(columns_kernel, [(len(parts), spans, extra) for parts, spans, extra in items]),
        "columns",
        outs,
        [],
        [("s", where)] + [("v", part) for parts, _, _ in items for part in parts],
        5,
    )
    keep = [pieces[at] for at in pairs]
    got = [links.core(pieces[at + 1]) for at in pairs]
    rows_out = call(
        rows_kernel,
        "rows",
        [("v", shaped(2 * item.shape[0], item.shape[1], dtype=F32)) for item in keep],
        [],
        [("s", where)] + [("v", item) for item in keep + got],
        4,
    )
    return rows_out + [item for at, item in enumerate(pieces) if at not in pairs and at - 1 not in pairs]


def shaped(*shape, dtype=BF16):
    return jax.ShapeDtypeStruct(shape, dtype)


def local(
    n_dp,
    n_fsdp,
    tokens,
    qkv_weight,
    out_weight,
    up_weight,
    up_bias,
    down_weight,
    vectors,
    lengths,
    exit_depth,
    prefix_widths,
    cotangent,
):
    sent_count, seq_len, width = tokens.shape
    rows = sent_count * seq_len
    hidden = up_weight.shape[1] * n_fsdp
    links = Links(n_dp, n_fsdp)
    where = jnp.stack(links.place()).astype(jnp.int32)
    inputs = tokens.reshape(rows, width)
    grad_in = cotangent.reshape(rows, width)
    blocked = qkv_weight.shape[0] % 32 == 0 and out_weight.shape[1] % 64 == 0

    if blocked:
        half = qkv_weight.shape[0] // 2
        parts = down_weight.shape[0] // 2 // half

        def chip_piece(name, shards, extra=(), after=()):
            wide = 2 * sum(item.size for item in shards) // (2 * half)
            theirs = [links.core(item) for item in shards]
            return call(
                partial(piece_kernel, len(shards)),
                name,
                [("v", shaped(half, wide + (LANES if extra else 0)))],
                [],
                [("s", where)] + [("v", item) for item in (*shards, *theirs, *extra)],
                3,
                after=after,
            )[0]

        piece_in = chip_piece("in_piece", [qkv_weight], [vectors, up_bias.reshape(1, -1)])
        far_in = [links.ahead(piece_in, far) for far in range(1, links.rest)]
        own_in = jnp.stack([piece_in] + far_in)
        piece_up = chip_piece(
            "up_piece", [up_weight, out_weight, down_weight], after=far_in[:1]
        )
        (piece_up,) = hold([piece_up], [own_in])
        pair = jnp.stack([piece_up, links.ahead(piece_up, 1)])
        split = 2 * (up_weight.shape[1] + out_weight.shape[1])
        up_pair = pair[:, :, :split]
        down_pair = jnp.concatenate(jnp.split(pair[:, :, split:], parts, axis=2), axis=1)
        own_up_stack = double_rest(links, up_pair)
        near_in = [links.across(own_in), links.along_y(own_in), links.along_x(own_in), own_in]
        (down_pair,) = hold([down_pair], [own_up_stack])
        down_far = links.ahead(down_pair, 2)
        up_first, up_second = links.first(own_up_stack), links.second(own_up_stack)
        any_in = [("a", item) for item in spread_cores(links, near_in)]
        vec, bias = call(
            partial(small_kernel, links),
            "small_values",
            [("v", shaped(8, width, dtype=F32)), ("v", shaped(1, hidden, dtype=F32))],
            [pltpu.VMEM((n_dp * n_fsdp, 16, LANES), BF16), pltpu.SemaphoreType.DMA],
            [("s", where)] + any_in,
            3,
            after=[own_up_stack],
        )
    else:

        def whole(shard):
            part = lax.all_gather(shard, "fsdp", axis=1, tiled=True)
            return lax.all_gather(part, "dp", axis=0, tiled=True)

        any_in, any_out, any_up, any_down = (
            [("a", whole(shard))] for shard in (qkv_weight, out_weight, up_weight, down_weight)
        )
        vec = lax.all_gather(vectors, "fsdp", axis=0, tiled=True)
        vec = lax.all_gather(vec, "dp", axis=1, tiled=True).astype(F32)
        bias = lax.all_gather(up_bias, ("dp", "fsdp"), axis=0, tiled=True)
        bias = bias.astype(F32).reshape(1, hidden)
    n_weight = len(any_in)
    n_grad = 8 if blocked else 1

    def grad_outs(shard, *more, extra=0):
        if not blocked:
            return [("a", shaped(shard.shape[0] * n_dp, shard.shape[1] * n_fsdp))]
        cols = shard.shape[1] + sum(item.shape[1] for item in more)
        shape = (links.rest, shard.shape[0] // 2, 2 * cols + extra)
        return 8 * [("a", shaped(*shape))]

    small = shaped(8 + -(-hidden // width // 8) * 8, width, dtype=F32)
    one, two = pltpu.SemaphoreType.DMA, pltpu.SemaphoreType.DMA((2,))
    flat = shaped(rows, width)
    lined = ("s", where)

    def room(mib):
        return mib if blocked else 2 * mib

    qkv, attended = call(
        partial(attend_kernel, links, n_weight),
        "attend",
        [("v", shaped(rows, 3 * width)), ("v", flat)],
        [pltpu.VMEM((width, 3 * width), BF16), one],
        [lined, ("s", lengths), ("v", inputs), ("v", vec)] + any_in,
        room(13),
    )
    if blocked:
        up_first, up_second, down_far = hold([up_first, up_second, down_far], [attended])
        own_down_stack = double_rest(links, jnp.concatenate([down_pair, down_far], axis=0))
        up_both = links.second(up_first)
        down_first, down_second = links.first(own_down_stack), links.second(own_down_stack)
        near_up = [own_up_stack, up_first, up_second, up_both]
        any_up = [("a", item) for item in spread_cores(links, near_up)]
        any_out = any_up
    activated, slope, first_norm, normed, factor = call(
        partial(up_kernel, links, n_weight),
        "up",
        [
            ("v", shaped(rows, hidden)),
            ("v", shaped(rows, hidden)),
            ("v", flat),
            ("v", flat),
            ("v", shaped(rows, LANES, dtype=F32)),
        ],
        [pltpu.VMEM((width, hidden), BF16), pltpu.VMEM((width, width), BF16)]
        + [pltpu.VMEM((rows, 512), F32)] * 2
        + [two],
        [lined, ("v", attended), ("v", inputs), ("v", vec), ("v", bias)] + any_up + any_out,
        room(17),
        after=[down_first] if blocked else [],
    )
    if blocked:
        down_both = links.second(down_first)
        down_second, down_both = hold([down_second, down_both], [activated])
        near_down = [own_down_stack, down_first, down_second, down_both]
        any_down = [("a", item) for item in spread_cores(links, near_down)]
    down = call(
        partial(down_kernel, links, n_weight, n_grad),
        "down",
        [
            ("v", flat),
            ("v", shaped(sent_count, prefix_widths.shape[0], width, dtype=F32)),
            ("v", flat),
            ("v", small),
        ]
        + grad_outs(down_weight),
        [pltpu.VMEM((hidden, width), BF16), pltpu.VMEM((hidden, width), BF16), two],
        [lined, ("s", lengths), ("s", exit_depth), ("s", prefix_widths)]
        + [("v", activated), ("v", first_norm), ("v", inputs), ("v", grad_in), ("v", vec)]
        + any_down,
        room(19),
    )
    layer_out, pooled, d_down, sums_down = down[:4]
    grad_down = down[4:]
    if blocked:
        sum_down = Collect(links, grad_down[:4], grad_down[4:])
        sum_down.add_cores()

    d_pre, sums_up, grad_up = call(
        partial(up_back_kernel, links, n_weight),
        "up_back",
        [("v", shaped(rows, hidden)), ("v", small), ("v", shaped(width, hidden))],
        [pltpu.VMEM((hidden, width), BF16), pltpu.VMEM((width, rows), BF16), one],
        [lined, ("v", d_down), ("v", slope), ("v", first_norm), ("v", sums_down)] + any_down,
        room(16),
        after=sum_down.halves if blocked else [],
    )
    d_attn, d_att, sums_out, *grad_out = call(
        partial(out_back_kernel, links, n_weight, n_grad),
        "out_back",
        [("v", flat), ("v", flat), ("v", small)]
        + (grad_outs(up_weight, out_weight) if blocked else grad_outs(out_weight)),
        [
            pltpu.VMEM((width, hidden), BF16),
            pltpu.VMEM((width, width), BF16),
            pltpu.VMEM((width, width), BF16),
            pltpu.SemaphoreType.DMA((4,)),
        ],
        [lined]
        + [("v", item) for item in (d_pre, d_down, normed, factor, attended, vec, sums_up, grad_up)]
        + any_up
        + any_out,
        room(17),
    )
    if blocked:
        sum_up = Collect(links, grad_out[:4], hold(grad_out[4:], sum_down.near))
        sum_up.add_cores()
        sum_down.add_chips()
        sum_down.halve()
    attend_back = call(
        partial(attend_back_kernel, links, n_grad),
        "attend_back",
        [("v", shaped(rows, 3 * width)), ("v", small)]
        + grad_outs(qkv_weight, extra=LANES),
        [
            pltpu.VMEM((width, rows), BF16),
            pltpu.VMEM((width, 3 * width), BF16),
            pltpu.VMEM((n_dp * n_fsdp, 16, LANES), F32),
            pltpu.VMEM((n_dp * n_fsdp, 16, LANES), BF16),
            two,
        ],
        [lined, ("s", lengths), ("v", qkv), ("v", d_att), ("v", inputs), ("v", sums_out)],
        room(17),
        after=sum_up.halves + [sum_down.far] if blocked else [],
    )
    d_qkv, sums_in = attend_back[:2]
    grad_in_blocks = attend_back[2:]
    if blocked:
        (sum_down.back,) = hold([sum_down.back], [sums_in])
        sum_down.add_half()
        sum_down.halve()
    (grad_tokens,) = call(
        partial(inputs_kernel, links, n_weight),
        "inputs",
        [("v", flat)],
        [pltpu.VMEM((width, 3 * width), BF16), one],
        [lined, ("v", d_qkv), ("v", d_attn)] + any_in,
        room(10),
        after=[sum_down.far] if blocked else [],
    )

    if blocked:
        passed = hold(grad_in_blocks[4:] + [sum_down.back] + sum_up.near, [grad_tokens])
        give, (sum_down.back, *sum_up.near) = passed[:4], passed[4:]
        sum_in = Collect(links, grad_in_blocks[:4], give)
        sum_in.add_cores()
        sum_up.near = hold(sum_up.near, sum_in.halves)
        sum_up.add_chips()
        sum_up.halve()
        *sum_in.near, sum_up.back = hold(sum_in.near + [sum_up.back], [])
        sum_in.add_chips()
        sum_in.direct()
        sum_up.back, sum_down.back = hold([sum_up.back, sum_down.back], sum_in.blocks)
        for item in (sum_up, sum_down):
            item.add_half()
            while item.total.shape[0] > 1:
                item.halve()
                item.add_half()
        wide = 2 * qkv_weight.shape[1]
        split, total = 2 * up_weight.shape[1], 2 * (up_weight.shape[1] + out_weight.shape[1])
        own_qkv, own_up, own_out, own_down, last = owned(
            links,
            where,
            [
                ([sum_in.total[0]] + sum_in.ahead, [(0, wide)], LANES),
                ([sum_up.total[0]], [(0, split), (split, total)], 0),
                ([sum_down.total[0]], [(0, 2 * down_weight.shape[1])], 0),
            ],
        )
        own_vec = last[: vectors.shape[0], : vectors.shape[1]]
        own_bias = last[vectors.shape[0], : up_bias.shape[0]]
    else:

        def scattered(grad):
            part = lax.psum_scatter(grad, "dp", scatter_dimension=0, tiled=True)
            part = lax.psum_scatter(part, "fsdp", scatter_dimension=1, tiled=True)
            return part.astype(F32)

        own_down, own_up, own_out, own_qkv = (
            scattered(item) for item in (grad_down[0], grad_up, grad_out[0], grad_in_blocks[0])
        )
        every = lax.psum(sums_in, ("dp", "fsdp"))
        dp, fsdp = lax.axis_index("dp"), lax.axis_index("fsdp")
        own_vec = lax.dynamic_slice(
            every, (fsdp * vectors.shape[0], dp * vectors.shape[1]), vectors.shape
        )
        own_bias = lax.dynamic_slice_in_dim(
            every[8:].reshape(-1), (dp * n_fsdp + fsdp) * up_bias.shape[0], up_bias.shape[0], 0
        )
    return (
        layer_out.reshape(tokens.shape),
        pooled,
        grad_tokens.reshape(tokens.shape),
        own_qkv,
        own_out,
        own_up,
        own_bias,
        own_down,
        own_vec,
    )


def solution(mesh):
    placed = (
        P(("dp", "fsdp"), None, None),
        P("dp", "fsdp"),
        P("dp", "fsdp"),
        P("dp", "fsdp"),
        P(("dp", "fsdp")),
        P("dp", "fsdp"),
        P("fsdp", "dp"),
        P(("dp", "fsdp")),
        P(("dp", "fsdp")),
        P(),
        P(("dp", "fsdp"), None, None),
    )
    return jax.shard_map(
        partial(local, mesh.shape["dp"], mesh.shape["fsdp"]),
        mesh=mesh,
        in_specs=placed,
        out_specs=(
            P(("dp", "fsdp"), None, None),
            P(("dp", "fsdp"), None, None),
            P(("dp", "fsdp"), None, None),
            P("dp", "fsdp"),
            P("dp", "fsdp"),
            P("dp", "fsdp"),
            P(("dp", "fsdp")),
            P("dp", "fsdp"),
            P("fsdp", "dp"),
        ),
        check_vma=False,
    )
```

```python
import itertools
from functools import partial

import jax
import jax.numpy as jnp
from jax import lax
from jax.experimental import pallas as pl
from jax.experimental.pallas import tpu as pltpu
from jax.sharding import PartitionSpec as P

HEAD_DIM = 64
EPS = 1e-05
MASKED = -1000000000.0
F32 = jnp.float32
BF16 = jnp.bfloat16
MIB = 1024 * 1024
LANES = 128
GROUP = 3


class Links:
    def __init__(self, n_dp, n_fsdp):
        self.n_dp, self.n_fsdp = n_dp, n_fsdp
        self.high = n_fsdp // 4
        self.rest = (n_dp // 2) * self.high

    def number(self, rest, y, x, core):
        z, high = divmod(rest, self.high)
        return (z * 2 + y) * self.n_fsdp + (high * 2 + x) * 2 + core

    def pairs(self, step):
        return [
            (self.number(*place), self.number(*step(*place)))
            for place in itertools.product(range(self.rest), range(2), range(2), range(2))
        ]

    def move(self, value, step):
        return lax.ppermute(value, ("dp", "fsdp"), self.pairs(step))

    def core(self, value):
        return self.move(value, lambda q, y, x, c: (q, y, x, 1 - c))

    def along_x(self, value):
        return self.move(value, lambda q, y, x, c: (q, y, 1 - x, c))

    def along_y(self, value):
        return self.move(value, lambda q, y, x, c: (q, 1 - y, x, c))

    def across(self, value):
        return self.move(value, lambda q, y, x, c: (q, 1 - y, 1 - x, c))

    def first(self, value):
        return self.move(value, lambda q, y, x, c: (q, 1 - y, x, c) if c else (q, y, 1 - x, c))

    def second(self, value):
        return self.move(value, lambda q, y, x, c: (q, y, 1 - x, c) if c else (q, 1 - y, x, c))

    def flip(self, value, bit):
        return self.move(value, lambda q, y, x, c: (q ^ bit, y, x, c))

    def ahead(self, value, far):
        return self.move(value, lambda q, y, x, c: ((q + far) % self.rest, y, x, c))

    def place(self):
        dp, fsdp = lax.axis_index("dp"), lax.axis_index("fsdp")
        rest = (dp // 2) * self.high + fsdp // 4
        return rest, dp % 2, (fsdp // 2) % 2, fsdp % 2


def double_rest(links, stack):
    while stack.shape[0] < links.rest:
        stack = jnp.concatenate([stack, links.ahead(stack, stack.shape[0])], axis=0)
    return stack


def spread_cores(links, near):
    return list(near) + [links.core(item) for item in near]


class Collect:
    def __init__(self, links, keep, give):
        self.links, self.keep = links, keep
        self.got = [links.core(item) for item in give]

    def add_cores(self):
        halves = [
            (keep.astype(F32) + got.astype(F32)).astype(BF16)
            for keep, got in zip(self.keep[:3], self.got[:3])
        ]
        self.halves = halves
        links = self.links
        self.near = [
            links.across(halves[0]),
            links.along_y(halves[1]),
            links.along_x(halves[2]),
        ]

    def add_chips(self):
        total = self.keep[3].astype(F32) + self.got[3].astype(F32)
        for item in self.near:
            total = total + item.astype(F32)
        self.total = total

    def direct(self):
        self.blocks = [self.total[far].astype(BF16) for far in range(1, self.links.rest)]
        self.ahead = [self.links.ahead(item, at + 1) for at, item in enumerate(self.blocks)]

    def halve(self):
        half = self.total.shape[0] // 2
        self.far = self.total[half:].astype(BF16)
        self.total = self.total[:half]
        self.back = self.links.ahead(self.far, half)

    def add_half(self):
        self.total = self.total + self.back.astype(F32)


class Blocks:
    def __init__(self, links, where):
        self.links = links
        self.rest, self.y, self.x, self.core = where[0], where[1], where[2], where[3]

    def device(self, other, flip_y, flip_x, far, sign):
        links = self.links
        core = jnp.bitwise_xor(self.core, other)
        rest = lax.rem(self.rest + (sign * far + links.rest), links.rest)
        x, y = jnp.bitwise_xor(self.x, flip_x), jnp.bitwise_xor(self.y, flip_y)
        dp = lax.div(rest, links.high) * 2 + y
        return dp, lax.rem(rest, links.high) * 2 + x, core

    def corner(self, rows, cols, *spot):
        dp, wide, core = self.device(*spot)
        return pl.multiple_of((dp * 2 + core) * rows, rows), pl.multiple_of(wide * cols, cols)


def load_weight(links, where, refs, first_col, cols, out, sem, steps=True):
    if len(refs) == 1:
        copies = [pltpu.make_async_copy(refs[0], out, sem)]
    else:
        blocks = Blocks(links, where)
        rows = refs[0].shape[1]
        copies = []
        for stack, far in itertools.product(range(8), range(links.rest)):
            other, high, low = stack // 4, (stack // 2) % 2, stack % 2
            if not steps:
                high, low = 1 - high, 1 - low
            else:
                core = jnp.bitwise_xor(blocks.core, other)
                high, low = jnp.where(core == 0, high, low), jnp.where(core == 0, low, high)
            row, col = blocks.corner(rows, cols, other, high, low, far, -1)
            copies.append(
                pltpu.make_async_copy(
                    refs[stack].at[far, :, pl.ds(first_col, cols)],
                    out.at[pl.ds(row, rows), pl.ds(col, cols)],
                    sem,
                )
            )
    for copy in copies:
        copy.start()
    return copies


def store_grad(links, where, grad, refs, first_col, cols, sem):
    if len(refs) == 1:
        copies = [pltpu.make_async_copy(grad, refs[0], sem)]
    else:
        blocks = Blocks(links, where)
        rows = refs[0].shape[1]
        copies = []
        for other, y, x, far in itertools.product(range(2), range(2), range(2), range(links.rest)):
            row, col = blocks.corner(rows, cols, other, y, x, far, 1)
            out = refs[4 * other + 3 - 2 * y - x].at[far]
            copies.append(
                pltpu.make_async_copy(
                    grad.at[pl.ds(row, rows), pl.ds(col, cols)],
                    out.at[:, pl.ds(first_col, cols)],
                    sem,
                )
            )
    for copy in copies:
        copy.start()
    return copies


def store_small(links, where, small, refs, first_col, sem):
    blocks = Blocks(links, where)
    copies = []
    for other, y, x, far in itertools.product(range(2), range(2), range(2), range(links.rest)):
        dp, wide, core = blocks.device(other, y, x, far, 1)
        target = refs[4 * other + 3 - 2 * y - x].at[far, pl.ds(0, 16), pl.ds(first_col, LANES)]
        source = small.at[dp * links.n_fsdp + wide * 2 + core]
        copies.append(pltpu.make_async_copy(source, target, sem))
    for copy in copies:
        copy.start()
    return copies


def wait_all(copies):
    for copy in copies:
        copy.wait()


def dot(left, right):
    return lax.dot_general(left, right, (((1,), (0,)), ((), ())), preferred_element_type=F32)


def dot_nt(left, right):
    return lax.dot_general(left, right, (((1,), (1,)), ((), ())), preferred_element_type=F32)


def dot_tn(left, right):
    return lax.dot_general(left, right, (((0,), (0,)), ((), ())), preferred_element_type=F32)


def normalize(hidden):
    centered = hidden - jnp.mean(hidden, axis=-1, keepdims=True)
    factor = lax.rsqrt(jnp.mean(centered * centered, axis=-1, keepdims=True) + EPS)
    return centered * factor, factor


def norm_back(scaled, normed, factor):
    return factor * (
        scaled
        - jnp.mean(scaled, axis=-1, keepdims=True)
        - normed * jnp.mean(scaled * normed, axis=-1, keepdims=True)
    )


def gelu_parts(value):
    bell = jnp.exp(-0.5 * value * value)
    weight = 0.5 + 0.5 * lax.erf(value * 0.7071067811865476)
    return value * weight, weight + value * (bell * 0.3989422804014327)


def piece_kernel(n_shards, where, *refs):
    mine, theirs = refs[:n_shards], refs[n_shards : 2 * n_shards]
    *extra, piece = refs[2 * n_shards :]
    core = where[3]
    half = mine[0].shape[0] // 2
    lines = []
    for keep, got in zip(mine, theirs):
        times = keep.shape[0] // 2 // half
        for at in range(times):
            row = pl.multiple_of(core * half * times + at * half, half)
            low, high = keep[pl.ds(row, half), :], got[pl.ds(row, half), :]
            lines += [jnp.where(core == 0, low, high), jnp.where(core == 0, high, low)]
    if extra:
        line = jnp.concatenate([item[...].astype(F32) for item in extra], axis=0)
        below = jnp.zeros((half - line.shape[0], line.shape[1]), F32)
        line = jnp.concatenate([line, below], axis=0)
        beside = jnp.zeros((line.shape[0], LANES - line.shape[1]), F32)
        lines.append(jnp.concatenate([line, beside], axis=1).astype(BF16))
    piece[...] = jnp.concatenate(lines, axis=1)


def small_kernel(links, where, *refs):
    stacks, vec_out, bias_out, held, sem = refs[:8], *refs[8:]
    blocks = Blocks(links, where)
    first_col = stacks[0].shape[2] - LANES
    copies = []
    for stack, far in itertools.product(range(8), range(links.rest)):
        dp, wide, core = blocks.device(stack // 4, 1 - (stack // 2) % 2, 1 - stack % 2, far, -1)
        copies.append(
            pltpu.make_async_copy(
                stacks[stack].at[far, pl.ds(0, 16), pl.ds(first_col, LANES)],
                held.at[dp * links.n_fsdp + wide * 2 + core],
                sem,
            )
        )
    for copy in copies:
        copy.start()
    wait_all(copies)
    rows, width = 8 // links.n_fsdp, vec_out.shape[1] // links.n_dp
    got = [held[at].astype(F32)[:, :width] for at in range(links.n_dp * links.n_fsdp)]
    for fsdp in range(links.n_fsdp):
        line = jnp.concatenate([got[dp * links.n_fsdp + fsdp] for dp in range(links.n_dp)], axis=1)
        vec_out[pl.ds(rows * fsdp, rows), :] = line[:rows]
    bias_out[...] = jnp.concatenate(got, axis=1)[rows : rows + 1]


def head_half(pair, half):
    lane = lax.broadcasted_iota(jnp.int32, pair.shape, 1)
    keep = (lane < HEAD_DIM) if half == 0 else (lane >= HEAD_DIM)
    return jnp.where(keep, pair, jnp.zeros_like(pair))


def group_spots(step, pairs, seq):
    spots = []
    for at in range(GROUP):
        number = step * GROUP + at
        sent, pair = lax.div(number, pairs), lax.rem(number, pairs)
        rows = pl.ds(pl.multiple_of(sent * seq, seq), seq)
        spots.append((sent, rows, pl.multiple_of(pair * LANES, LANES)))
    return spots


def join_halves(low, high):
    lane = lax.broadcasted_iota(jnp.int32, low.shape, 1)
    return jnp.where(lane < HEAD_DIM, low, high)


def attend_kernel(links, n_weight, where, lengths, tokens, vec, *refs):
    weight_refs = refs[:n_weight]
    qkv, attended, w_qkv, sem = refs[n_weight:]
    width = tokens.shape[1]
    seq = 256
    sents = tokens.shape[0] // seq
    wide = width * 3 * 2 // links.n_fsdp
    wait_all(load_weight(links, where, weight_refs, 0, wide, w_qkv, sem, steps=False))
    for tile in range(3 * width // 256):
        at = pl.ds(tile * 256, 256)
        product = dot(tokens[...], w_qkv[:, at])
        if tile * 256 < width:
            product = product + vec[0:1, at]
        elif tile * 256 >= 2 * width:
            product = product + vec[1:2, pl.ds(tile * 256 - 2 * width, 256)]
        qkv[:, at] = product.astype(BF16)

    pairs = width // LANES

    def attend(step, carry):
        spots = group_spots(step, pairs, seq)
        scores = []
        for sent, rows, col in spots:
            queries = qkv[rows, pl.ds(col, LANES)] * jnp.asarray(HEAD_DIM ** (-0.5), BF16)
            keys = qkv[rows, pl.ds(col + width, LANES)]
            keep = lax.broadcasted_iota(jnp.int32, (seq, seq), 1) < lengths[sent]
            for half in range(2):
                scores.append(jnp.where(keep, dot_nt(head_half(queries, half), keys), MASKED))
        tops = [jnp.max(item, axis=-1, keepdims=True) for item in scores]
        exponents = [jnp.exp(item - top) for item, top in zip(scores, tops)]
        scales = [1.0 / jnp.sum(item, axis=-1, keepdims=True) for item in exponents]
        probs = [(item * scale).astype(BF16) for item, scale in zip(exponents, scales)]
        for at, (sent, rows, col) in enumerate(spots):
            values = qkv[rows, pl.ds(col + 2 * width, LANES)]
            low, high = (dot(probs[2 * at + half], values) for half in range(2))
            attended[rows, pl.ds(col, LANES)] = join_halves(low, high).astype(BF16)
        return carry

    lax.fori_loop(0, sents * pairs // GROUP, attend, 0)


def up_kernel(links, n_weight, where, attended, tokens, vec, bias, *refs):
    up_refs = refs[:n_weight]
    out_refs = refs[n_weight : 2 * n_weight]
    activated, slope, first_norm, normed, factor = refs[2 * n_weight : 2 * n_weight + 5]
    w_up, w_out, even, odd, sems = refs[2 * n_weight + 5 :]
    width, hidden = w_up.shape
    tile = even.shape[1]
    count = hidden // tile
    wide = hidden * 2 // links.n_fsdp
    copies_out = load_weight(
        links, where, out_refs, wide, width * 2 // links.n_fsdp, w_out, sems.at[1]
    )
    copies = load_weight(links, where, up_refs, 0, wide, w_up, sems.at[0])
    wait_all(copies_out)
    for part in range(tokens.shape[0] // 256):
        rows = pl.ds(part * 256, 256)
        total = tokens[rows, :].astype(F32) + (dot(attended[rows, :], w_out[...]) + vec[2:3, :])
        unit, scale = normalize(total)
        normed[rows, :] = unit.astype(BF16)
        factor[rows, :] = jnp.broadcast_to(scale, (256, LANES))
        first_norm[rows, :] = (unit * vec[3:4, :] + vec[4:5, :]).astype(BF16)
    wait_all(copies)

    def place(step):
        return pl.ds(pl.multiple_of(step * tile, tile), tile)

    def fill(held, step):
        held[...] = dot(first_norm[...], w_up[:, place(step)])

    def drain(held, step):
        at = place(step)
        act, der = gelu_parts(held[...] + bias[:, at])
        activated[:, at] = act.astype(BF16)
        slope[:, at] = der.astype(BF16)

    fill(even, 0)

    def body(step, carry):
        fill(odd, 2 * step + 1)
        drain(even, 2 * step)
        fill(even, lax.rem(2 * step + 2, count))
        drain(odd, 2 * step + 1)
        return carry

    lax.fori_loop(0, count // 2, body, 0)


def down_kernel(links, n_weight, n_grad, where, lengths, depth, prefix, *refs):
    activated, first_norm, tokens, cotangent, vec = refs[:5]
    weight_refs = refs[5 : 5 + n_weight]
    layer_out, pooled, d_down, sums = refs[5 + n_weight : 9 + n_weight]
    grad_refs = refs[9 + n_weight : 9 + n_weight + n_grad]
    w_down, grad, sems = refs[9 + n_weight + n_grad :]
    hidden, width = w_down.shape
    seq = 256
    sents = tokens.shape[0] // seq
    cols = width * 2 // links.n_fsdp
    wait_all(load_weight(links, where, weight_refs, 0, cols, w_down, sems.at[0]))
    sums[...] = jnp.zeros_like(sums)
    columns = lax.broadcasted_iota(jnp.int32, (1, width), 1)
    for sent in range(sents):
        rows = pl.ds(sent * seq, seq)
        total = first_norm[rows, :].astype(F32) + (dot(activated[rows, :], w_down[...]) + vec[5:6, :])
        normed, factor = normalize(total)
        result = normed * vec[6:7, :] + vec[7:8, :]
        layer_out[rows, :] = result.astype(BF16)
        valid = lax.broadcasted_iota(jnp.int32, (seq, width), 0) < lengths[sent]
        source = jnp.where(depth[sent] == 1, result, tokens[rows, :].astype(F32))
        mean = jnp.sum(jnp.where(valid, source, 0.0), axis=0, keepdims=True)
        mean = mean / lengths[sent].astype(F32)
        for at in range(pooled.shape[1]):
            pooled[sent, pl.ds(at, 1), :] = mean * (columns < prefix[at]).astype(F32)
        grad_in = cotangent[rows, :].astype(F32)
        sums[6:7, :] += jnp.sum(grad_in * normed, axis=0, keepdims=True)
        sums[7:8, :] += jnp.sum(grad_in, axis=0, keepdims=True)
        back = norm_back(grad_in * vec[6:7, :], normed, factor)
        low = back.astype(BF16)
        d_down[rows, :] = low
        sums[5:6, :] += jnp.sum(low.astype(F32), axis=0, keepdims=True)

    for step in range(hidden // 768):
        at = pl.ds(step * 768, 768)
        grad[at, :] = dot_tn(activated[:, at], d_down[...]).astype(BF16)
    wait_all(store_grad(links, where, grad, grad_refs, 0, cols, sems.at[1]))


def up_back_kernel(links, n_weight, where, d_down, slope, first_norm, sums_in, *refs):
    weight_refs = refs[:n_weight]
    d_pre, sums, grad, w_down, turned, sem = refs[n_weight:]
    hidden, width = w_down.shape
    copies = load_weight(links, where, weight_refs, 0, width * 2 // links.n_fsdp, w_down, sem)
    sums[...] = sums_in[...]
    turned[...] = first_norm[...].T
    wait_all(copies)

    for step in range(hidden // 512):
        at = pl.ds(step * 512, 512)
        d_act = dot_nt(d_down[...], w_down[at, :])
        low = (d_act * slope[:, at].astype(F32)).astype(BF16)
        d_pre[:, at] = low
        line = jnp.sum(low.astype(F32), axis=0, keepdims=True)
        for part in range(2):
            row, col = divmod(step * 512 + part * 256, width)
            sums[pl.ds(8 + row, 1), pl.ds(col, 256)] = line[:, part * 256 : part * 256 + 256]
        grad[:, at] = dot(turned[...], low).astype(BF16)


def out_back_kernel(links, n_weight, n_grad, where, *refs):
    d_pre, d_down, normed, factor, attended, vec, sums_in, grad_up = refs[:8]
    up_refs = refs[8 : 8 + n_weight]
    out_refs = refs[8 + n_weight : 8 + 2 * n_weight]
    d_attn, d_att, sums = refs[8 + 2 * n_weight : 11 + 2 * n_weight]
    grad_refs = refs[11 + 2 * n_weight : 11 + 2 * n_weight + n_grad]
    w_up, w_out, grad_out, sems = refs[11 + 2 * n_weight + n_grad :]
    width, hidden = w_up.shape
    seq = 256
    wide = hidden * 2 // links.n_fsdp
    copies = load_weight(links, where, up_refs, 0, wide, w_up, sems.at[0])
    copies_out = load_weight(
        links, where, out_refs, wide, width * 2 // links.n_fsdp, w_out, sems.at[1]
    )
    if n_grad > 1:
        copies_up = store_grad(links, where, grad_up, grad_refs, 0, wide, sems.at[3])
    wait_all(copies)
    sums[...] = sums_in[...]
    for part in range(d_pre.shape[0] // seq):
        rows = pl.ds(part * seq, seq)
        d_first = dot_nt(d_pre[rows, :], w_up[...]) + d_down[rows, :].astype(F32)
        unit = normed[rows, :].astype(F32)
        sums[3:4, :] += jnp.sum(d_first * unit, axis=0, keepdims=True)
        sums[4:5, :] += jnp.sum(d_first, axis=0, keepdims=True)
        back = norm_back(d_first * vec[3:4, :], unit, factor[rows, 0:1])
        low = back.astype(BF16)
        d_attn[rows, :] = low
        sums[2:3, :] += jnp.sum(low.astype(F32), axis=0, keepdims=True)
    wait_all(copies_out)
    grad_out[...] = dot_tn(attended[...], d_attn[...]).astype(BF16)
    first = wide if n_grad > 1 else 0
    copies = store_grad(
        links, where, grad_out, grad_refs, first, width * 2 // links.n_fsdp, sems.at[2]
    )
    if n_grad > 1:
        copies += copies_up
    d_att[...] = dot_nt(d_attn[...], w_out[...]).astype(BF16)
    wait_all(copies)


def attend_back_kernel(links, n_grad, where, lengths, qkv, d_att, tokens, sums_in, *refs):
    d_qkv, sums = refs[:2]
    grad_refs = refs[2 : 2 + n_grad]
    turned, grad, held, small, sems = refs[2 + n_grad :]
    width = tokens.shape[1]
    seq = 256
    sents = tokens.shape[0] // seq
    pairs = width // LANES
    wide = width * 3 * 2 // links.n_fsdp
    turned[...] = tokens[...].T
    sums[...] = sums_in[...]
    key_scale = jnp.asarray(HEAD_DIM ** (-0.5), BF16)

    def body(step, carry):
        spots = group_spots(step, pairs, seq)
        loaded, scores, d_probs = [], [], []
        for sent, rows, col in spots:
            queries = qkv[rows, pl.ds(col, LANES)] * key_scale
            keys = qkv[rows, pl.ds(col + width, LANES)]
            values = qkv[rows, pl.ds(col + 2 * width, LANES)]
            d_out = d_att[rows, pl.ds(col, LANES)]
            loaded.append((queries, keys, d_out))
            keep = lax.broadcasted_iota(jnp.int32, (seq, seq), 0) < lengths[sent]
            for half in range(2):
                scores.append(jnp.where(keep, dot_nt(keys, head_half(queries, half)), MASKED))
                d_probs.append(dot_nt(values, head_half(d_out, half)))
        tops = [jnp.max(item, axis=0, keepdims=True) for item in scores]
        exponents = [jnp.exp(item - top) for item, top in zip(scores, tops)]
        scales = [1.0 / jnp.sum(item, axis=0, keepdims=True) for item in exponents]
        probs = [item * scale for item, scale in zip(exponents, scales)]
        row_dots = [jnp.sum(back * prob, axis=0, keepdims=True) for back, prob in zip(d_probs, probs)]
        d_scores = [
            (prob * (back - row_dot)).astype(BF16)
            for prob, back, row_dot in zip(probs, d_probs, row_dots)
        ]
        for at, (sent, rows, col) in enumerate(spots):
            queries, keys, d_out = loaded[at]
            mine = (2 * at, 2 * at + 1)
            d_value = join_halves(*(dot(probs[one].astype(BF16), d_out) for one in mine))
            d_key = join_halves(*(dot(d_scores[one], queries) for one in mine))
            d_query = join_halves(*(dot_tn(d_scores[one], keys) for one in mine))
            d_query = (d_query * (HEAD_DIM ** (-0.5))).astype(BF16)
            d_value = d_value.astype(BF16)
            d_qkv[rows, pl.ds(col, LANES)] = d_query
            d_qkv[rows, pl.ds(col + width, LANES)] = d_key.astype(BF16)
            d_qkv[rows, pl.ds(col + 2 * width, LANES)] = d_value
            sums[0:1, pl.ds(col, LANES)] += jnp.sum(d_query.astype(F32), axis=0, keepdims=True)
            sums[1:2, pl.ds(col, LANES)] += jnp.sum(d_value.astype(F32), axis=0, keepdims=True)
        return carry

    lax.fori_loop(0, sents * pairs // GROUP, body, 0)
    copies = []
    if n_grad > 1:
        held[...] = jnp.zeros_like(held)
        per_device = 8 // links.n_fsdp
        line_rows, line_cols = sums.shape[0] - 8, width // links.n_dp
        for dp, fsdp in itertools.product(range(links.n_dp), range(links.n_fsdp)):
            at = dp * links.n_fsdp + fsdp
            rows = pl.ds(fsdp * per_device, per_device)
            held[at, :per_device, :line_cols] = sums[rows, pl.ds(dp * line_cols, line_cols)]
            first = at * line_cols
            row, col = 8 + first // width, first % width
            held[at, per_device : per_device + 1, :line_cols] = sums[pl.ds(row, 1), pl.ds(col, line_cols)]
        small[...] = held[...].astype(BF16)
        copies = store_small(links, where, small, grad_refs, wide, sems.at[1])
    for step in range(3 * width // 256):
        at = pl.ds(step * 256, 256)
        grad[:, at] = dot(turned[...], d_qkv[:, at]).astype(BF16)
    wait_all(copies + store_grad(links, where, grad, grad_refs, 0, wide, sems.at[0]))


def inputs_kernel(links, n_weight, where, d_qkv, d_attn, *refs):
    weight_refs = refs[:n_weight]
    grad_tokens, mark, w_qkv, sem = refs[n_weight:]
    mark[...] = jnp.zeros_like(mark)
    width = d_attn.shape[1]
    wide = width * 3 * 2 // links.n_fsdp
    wait_all(load_weight(links, where, weight_refs, 0, wide, w_qkv, sem, steps=False))
    for part in range(d_qkv.shape[0] // 256):
        rows = pl.ds(part * 256, 256)
        grad_tokens[rows, :] = (
            dot_nt(d_qkv[rows, :], w_qkv[...]) + d_attn[rows, :].astype(F32)
        ).astype(BF16)


def columns_kernel(plan, where, *refs):
    refs = list(refs)
    mine = where[3] == 0
    sums = []
    for n_parts, spans, extra in plan:
        total = refs.pop(0)[...]
        for _ in range(n_parts - 1):
            total = total + refs.pop(0)[...].astype(F32)
        sums.append(total)
    for total, (_, spans, extra) in zip(sums, plan):
        for first, last in spans:
            middle = (first + last) // 2
            low, high = total[:, first:middle], total[:, middle:last]
            refs.pop(0)[...] = jnp.where(mine, low, high)
            refs.pop(0)[...] = jnp.where(mine, high, low)
        if extra:
            refs.pop(0)[...] = total[:8, -extra:]


def rows_kernel(turned, where, *refs):
    count = len(refs) // 3
    mine = where[3] == 0
    for at in range(count):
        keep, got, out = refs[at], refs[count + at], refs[2 * count + at]
        half = keep.shape[0]
        low, high = jnp.where(mine, keep[...], got[...]), jnp.where(mine, got[...], keep[...])
        if at in turned:
            out[...] = jnp.concatenate([low.T, high.T], axis=1)
        else:
            out[:half, :] = low
            out[half:, :] = high


SMEM_SPEC = pl.BlockSpec(memory_space=pltpu.SMEM)
VMEM_SPEC = pl.BlockSpec(memory_space=pltpu.VMEM)
ANY_SPEC = pl.BlockSpec(memory_space=pl.ANY)


def call(body, name, outs, scratch, args, vmem, after=(), through=()):
    spec = {"s": SMEM_SPEC, "v": VMEM_SPEC, "a": ANY_SPEC}
    extra = [("a", v) for v in list(through) + list(after)]
    handed = [("a", v) for v in through]
    n_args, n_outs = len(args), len(outs)

    def run(*refs):
        rest = refs[n_args + len(extra) :]
        body(*refs[:n_args], *rest[:n_outs], *rest[n_outs + len(handed) :])

    return list(
        pl.pallas_call(
            run,
            name=name,
            out_shape=[jax.ShapeDtypeStruct(v.shape, v.dtype) for _, v in list(outs) + handed],
            in_specs=[spec[place] for place, _ in list(args) + extra],
            out_specs=[spec[place] for place, _ in list(outs) + handed],
            scratch_shapes=scratch,
            input_output_aliases={n_args + at: n_outs + at for at in range(len(handed))},
            compiler_params=pltpu.CompilerParams(vmem_limit_bytes=vmem * MIB),
            cost_estimate=pl.CostEstimate(flops=1, bytes_accessed=1, transcendentals=0),
        )(*[value for _, value in list(args) + extra])
    )


def hold(arrays, after):
    return call(lambda: None, "hold", [], [], [], 1, after=after, through=arrays)


def owned(links, where, items, turned):
    outs, pairs = [], []
    for parts, spans, extra in items:
        rows = parts[0].shape[0]
        for first, last in spans:
            pairs.append(len(outs))
            outs += 2 * [("v", shaped(rows, (last - first) // 2, dtype=F32))]
        if extra:
            outs.append(("v", shaped(8, extra, dtype=F32)))
    pieces = call(
        partial(columns_kernel, [(len(parts), spans, extra) for parts, spans, extra in items]),
        "columns",
        outs,
        [],
        [("s", where)] + [("v", part) for parts, _, _ in items for part in parts],
        5,
    )
    keep = [pieces[at] for at in pairs]
    got = [links.core(pieces[at + 1]) for at in pairs]
    rows_out = call(
        partial(rows_kernel, turned),
        "rows",
        [
            ("v", shaped(*shape[:: -1 if at in turned else 1], dtype=F32))
            for at, shape in enumerate((2 * item.shape[0], item.shape[1]) for item in keep)
        ],
        [],
        [("s", where)] + [("v", item) for item in keep + got],
        4,
    )
    return rows_out + [item for at, item in enumerate(pieces) if at not in pairs and at - 1 not in pairs]


def shaped(*shape, dtype=BF16):
    return jax.ShapeDtypeStruct(shape, dtype)


def local(
    n_dp,
    n_fsdp,
    tokens,
    qkv_weight,
    out_weight,
    up_weight,
    up_bias,
    down_weight,
    vectors,
    lengths,
    exit_depth,
    prefix_widths,
    cotangent,
):
    sent_count, seq_len, width = tokens.shape
    rows = sent_count * seq_len
    hidden = up_weight.shape[1] * n_fsdp
    links = Links(n_dp, n_fsdp)
    where = jnp.stack(links.place()).astype(jnp.int32)
    inputs = tokens.reshape(rows, width)
    grad_in = cotangent.reshape(rows, width)
    blocked = qkv_weight.shape[0] % 32 == 0 and out_weight.shape[1] % 64 == 0

    if blocked:
        half = qkv_weight.shape[0] // 2
        parts = down_weight.shape[0] // 2 // half

        def chip_piece(name, shards, extra=(), after=()):
            wide = 2 * sum(item.size for item in shards) // (2 * half)
            theirs = [links.core(item) for item in shards]
            return call(
                partial(piece_kernel, len(shards)),
                name,
                [("v", shaped(half, wide + (LANES if extra else 0)))],
                [],
                [("s", where)] + [("v", item) for item in (*shards, *theirs, *extra)],
                3,
                after=after,
            )[0]

        small = jnp.concatenate([vectors, up_bias.reshape(1, -1)], axis=0)
        piece_in = chip_piece("in_piece", [qkv_weight], [small])
        far_in = [links.ahead(piece_in, far) for far in range(1, links.rest)]
        own_in = jnp.stack([piece_in] + far_in)
        piece_up = chip_piece(
            "up_piece", [up_weight, out_weight, down_weight], after=far_in[:1]
        )
        (piece_up,) = hold([piece_up], [own_in])
        pair = jnp.stack([piece_up, links.ahead(piece_up, 1)])
        split = 2 * (up_weight.shape[1] + out_weight.shape[1])
        up_pair = pair[:, :, :split]
        down_pair = jnp.concatenate(jnp.split(pair[:, :, split:], parts, axis=2), axis=1)
        own_up_stack = double_rest(links, up_pair)
        near_in = [links.across(own_in), links.along_y(own_in), links.along_x(own_in), own_in]
        (down_pair,) = hold([down_pair], [own_up_stack])
        down_far = links.ahead(down_pair, 2)
        up_first, up_second = links.first(own_up_stack), links.second(own_up_stack)
        any_in = [("a", item) for item in spread_cores(links, near_in)]
        vec, bias = call(
            partial(small_kernel, links),
            "small_values",
            [("v", shaped(8, width, dtype=F32)), ("v", shaped(1, hidden, dtype=F32))],
            [pltpu.VMEM((n_dp * n_fsdp, 16, LANES), BF16), pltpu.SemaphoreType.DMA],
            [("s", where)] + any_in,
            3,
            after=[own_up_stack],
        )
    else:

        def whole(shard):
            part = lax.all_gather(shard, "fsdp", axis=1, tiled=True)
            return lax.all_gather(part, "dp", axis=0, tiled=True)

        any_in, any_out, any_up, any_down = (
            [("a", whole(shard))] for shard in (qkv_weight, out_weight, up_weight, down_weight)
        )
        vec = lax.all_gather(vectors, "fsdp", axis=0, tiled=True)
        vec = lax.all_gather(vec, "dp", axis=1, tiled=True).astype(F32)
        bias = lax.all_gather(up_bias, ("dp", "fsdp"), axis=0, tiled=True)
        bias = bias.astype(F32).reshape(1, hidden)
    n_weight = len(any_in)
    n_grad = 8 if blocked else 1

    def grad_outs(shard, *more, extra=0):
        if not blocked:
            return [("a", shaped(shard.shape[0] * n_dp, shard.shape[1] * n_fsdp))]
        cols = shard.shape[1] + sum(item.shape[1] for item in more)
        shape = (links.rest, shard.shape[0] // 2, 2 * cols + extra)
        return 8 * [("a", shaped(*shape))]

    small = shaped(8 + -(-hidden // width // 8) * 8, width, dtype=F32)
    one, two = pltpu.SemaphoreType.DMA, pltpu.SemaphoreType.DMA((2,))
    flat = shaped(rows, width)
    lined = ("s", where)

    def room(mib):
        return mib if blocked else 2 * mib

    qkv, attended = call(
        partial(attend_kernel, links, n_weight),
        "attend",
        [("v", shaped(rows, 3 * width)), ("v", flat)],
        [pltpu.VMEM((width, 3 * width), BF16), one],
        [lined, ("s", lengths), ("v", inputs), ("v", vec)] + any_in,
        room(13),
    )
    if blocked:
        up_first, up_second, down_far = hold([up_first, up_second, down_far], [attended])
        own_down_stack = double_rest(links, jnp.concatenate([down_pair, down_far], axis=0))
        up_both = links.second(up_first)
        down_first, down_second = links.first(own_down_stack), links.second(own_down_stack)
        near_up = [own_up_stack, up_first, up_second, up_both]
        any_up = [("a", item) for item in spread_cores(links, near_up)]
        any_out = any_up
    activated, slope, first_norm, normed, factor = call(
        partial(up_kernel, links, n_weight),
        "up",
        [
            ("v", shaped(rows, hidden)),
            ("v", shaped(rows, hidden)),
            ("v", flat),
            ("v", flat),
            ("v", shaped(rows, LANES, dtype=F32)),
        ],
        [pltpu.VMEM((width, hidden), BF16), pltpu.VMEM((width, width), BF16)]
        + [pltpu.VMEM((rows, 512), F32)] * 2
        + [two],
        [lined, ("v", attended), ("v", inputs), ("v", vec), ("v", bias)] + any_up + any_out,
        room(17),
        after=[down_first] if blocked else [],
    )
    if blocked:
        down_both = links.second(down_first)
        down_second, down_both = hold([down_second, down_both], [activated])
        near_down = [own_down_stack, down_first, down_second, down_both]
        any_down = [("a", item) for item in spread_cores(links, near_down)]
    down = call(
        partial(down_kernel, links, n_weight, n_grad),
        "down",
        [
            ("v", flat),
            ("v", shaped(sent_count, prefix_widths.shape[0], width, dtype=F32)),
            ("v", flat),
            ("v", small),
        ]
        + grad_outs(down_weight),
        [pltpu.VMEM((hidden, width), BF16), pltpu.VMEM((hidden, width), BF16), two],
        [lined, ("s", lengths), ("s", exit_depth), ("s", prefix_widths)]
        + [("v", activated), ("v", first_norm), ("v", inputs), ("v", grad_in), ("v", vec)]
        + any_down,
        room(19),
    )
    layer_out, pooled, d_down, sums_down = down[:4]
    grad_down = down[4:]
    if blocked:
        sum_down = Collect(links, grad_down[:4], grad_down[4:])
        sum_down.add_cores()

    d_pre, sums_up, grad_up = call(
        partial(up_back_kernel, links, n_weight),
        "up_back",
        [("v", shaped(rows, hidden)), ("v", small), ("v", shaped(width, hidden))],
        [pltpu.VMEM((hidden, width), BF16), pltpu.VMEM((width, rows), BF16), one],
        [lined, ("v", d_down), ("v", slope), ("v", first_norm), ("v", sums_down)] + any_down,
        room(16),
        after=sum_down.halves if blocked else [],
    )
    d_attn, d_att, sums_out, *grad_out = call(
        partial(out_back_kernel, links, n_weight, n_grad),
        "out_back",
        [("v", flat), ("v", flat), ("v", small)]
        + (grad_outs(up_weight, out_weight) if blocked else grad_outs(out_weight)),
        [
            pltpu.VMEM((width, hidden), BF16),
            pltpu.VMEM((width, width), BF16),
            pltpu.VMEM((width, width), BF16),
            pltpu.SemaphoreType.DMA((4,)),
        ],
        [lined]
        + [("v", item) for item in (d_pre, d_down, normed, factor, attended, vec, sums_up, grad_up)]
        + any_up
        + any_out,
        room(17),
    )
    if blocked:
        sum_up = Collect(links, grad_out[:4], hold(grad_out[4:], sum_down.near))
        sum_up.add_cores()
        sum_down.add_chips()
        sum_down.halve()
    attend_back = call(
        partial(attend_back_kernel, links, n_grad),
        "attend_back",
        [("v", shaped(rows, 3 * width)), ("v", small)]
        + grad_outs(qkv_weight, extra=LANES),
        [
            pltpu.VMEM((width, rows), BF16),
            pltpu.VMEM((width, 3 * width), BF16),
            pltpu.VMEM((n_dp * n_fsdp, 16, LANES), F32),
            pltpu.VMEM((n_dp * n_fsdp, 16, LANES), BF16),
            two,
        ],
        [lined, ("s", lengths), ("v", qkv), ("v", d_att), ("v", inputs), ("v", sums_out)],
        room(17),
        after=sum_up.halves + [sum_down.far] if blocked else [],
    )
    d_qkv, sums_in = attend_back[:2]
    grad_in_blocks = attend_back[2:]
    if blocked:
        (sum_down.back,) = hold([sum_down.back], [sums_in])
        sum_down.add_half()
        sum_down.halve()
    grad_tokens, mark = call(
        partial(inputs_kernel, links, n_weight),
        "inputs",
        [("v", flat), ("v", shaped(8, LANES, dtype=F32))],
        [pltpu.VMEM((width, 3 * width), BF16), one],
        [lined, ("v", d_qkv), ("v", d_attn)] + any_in,
        room(10),
        after=[sum_down.far] if blocked else [],
    )

    if blocked:
        passed = hold(grad_in_blocks[4:] + [sum_down.back], [mark] + sum_up.near)
        give, (sum_down.back,) = passed[:4], passed[4:]
        sum_in = Collect(links, grad_in_blocks[:4], give)
        sum_in.add_cores()
        sum_up.near = hold(sum_up.near, sum_in.halves)
        sum_up.add_chips()
        sum_up.halve()
        *sum_in.near, sum_up.back = hold(sum_in.near + [sum_up.back], [])
        sum_in.add_chips()
        sum_in.direct()
        sum_up.back, sum_down.back = hold([sum_up.back, sum_down.back], sum_in.blocks)
        for item in (sum_up, sum_down):
            item.add_half()
            while item.total.shape[0] > 1:
                item.halve()
                item.add_half()
        wide = 2 * qkv_weight.shape[1]
        split, total = 2 * up_weight.shape[1], 2 * (up_weight.shape[1] + out_weight.shape[1])
        own_qkv, own_up, own_out, own_down, last = owned(
            links,
            where,
            [
                ([sum_in.total[0]] + sum_in.ahead, [(0, wide)], LANES),
                ([sum_up.total[0]], [(0, split), (split, total)], 0),
                ([sum_down.total[0]], [(0, 2 * down_weight.shape[1])], 0),
            ],
            turned=(3,),
        )
        own_down = own_down.T
        own_vec = last[: vectors.shape[0], : vectors.shape[1]]
        own_bias = last[vectors.shape[0], : up_bias.shape[0]]
    else:

        def scattered(grad):
            part = lax.psum_scatter(grad, "dp", scatter_dimension=0, tiled=True)
            part = lax.psum_scatter(part, "fsdp", scatter_dimension=1, tiled=True)
            return part.astype(F32)

        own_down, own_up, own_out, own_qkv = (
            scattered(item) for item in (grad_down[0], grad_up, grad_out[0], grad_in_blocks[0])
        )
        every = lax.psum(sums_in, ("dp", "fsdp"))
        dp, fsdp = lax.axis_index("dp"), lax.axis_index("fsdp")
        own_vec = lax.dynamic_slice(
            every, (fsdp * vectors.shape[0], dp * vectors.shape[1]), vectors.shape
        )
        own_bias = lax.dynamic_slice_in_dim(
            every[8:].reshape(-1), (dp * n_fsdp + fsdp) * up_bias.shape[0], up_bias.shape[0], 0
        )
    return (
        layer_out.reshape(tokens.shape),
        pooled,
        grad_tokens.reshape(tokens.shape),
        own_qkv,
        own_out,
        own_up,
        own_bias,
        own_down,
        own_vec,
    )


def solution(mesh):
    placed = (
        P(("dp", "fsdp"), None, None),
        P("dp", "fsdp"),
        P("dp", "fsdp"),
        P("dp", "fsdp"),
        P(("dp", "fsdp")),
        P("dp", "fsdp"),
        P("fsdp", "dp"),
        P(("dp", "fsdp")),
        P(("dp", "fsdp")),
        P(),
        P(("dp", "fsdp"), None, None),
    )
    return jax.shard_map(
        partial(local, mesh.shape["dp"], mesh.shape["fsdp"]),
        mesh=mesh,
        in_specs=placed,
        out_specs=(
            P(("dp", "fsdp"), None, None),
            P(("dp", "fsdp"), None, None),
            P(("dp", "fsdp"), None, None),
            P("dp", "fsdp"),
            P("dp", "fsdp"),
            P("dp", "fsdp"),
            P(("dp", "fsdp")),
            P("dp", "fsdp"),
            P("fsdp", "dp"),
        ),
        check_vma=False,
    )
```

```python
import itertools
from functools import partial

import jax
import jax.numpy as jnp
from jax import lax
from jax.experimental import pallas as pl
from jax.experimental.pallas import tpu as pltpu
from jax.sharding import PartitionSpec as P

HEAD_DIM = 64
EPS = 1e-05
MASKED = -1000000000.0
F32 = jnp.float32
BF16 = jnp.bfloat16
MIB = 1024 * 1024
LANES = 128
GROUP = 3


class Links:
    def __init__(self, n_dp, n_fsdp):
        self.n_dp, self.n_fsdp = n_dp, n_fsdp
        self.high = n_fsdp // 4
        self.rest = (n_dp // 2) * self.high

    def number(self, rest, y, x, core):
        z, high = divmod(rest, self.high)
        return (z * 2 + y) * self.n_fsdp + (high * 2 + x) * 2 + core

    def pairs(self, step):
        return [
            (self.number(*place), self.number(*step(*place)))
            for place in itertools.product(range(self.rest), range(2), range(2), range(2))
        ]

    def move(self, value, step):
        return lax.ppermute(value, ("dp", "fsdp"), self.pairs(step))

    def core(self, value):
        return self.move(value, lambda q, y, x, c: (q, y, x, 1 - c))

    def along_x(self, value):
        return self.move(value, lambda q, y, x, c: (q, y, 1 - x, c))

    def along_y(self, value):
        return self.move(value, lambda q, y, x, c: (q, 1 - y, x, c))

    def across(self, value):
        return self.move(value, lambda q, y, x, c: (q, 1 - y, 1 - x, c))

    def first(self, value):
        return self.move(value, lambda q, y, x, c: (q, 1 - y, x, c) if c else (q, y, 1 - x, c))

    def second(self, value):
        return self.move(value, lambda q, y, x, c: (q, y, 1 - x, c) if c else (q, 1 - y, x, c))

    def flip(self, value, bit):
        return self.move(value, lambda q, y, x, c: (q ^ bit, y, x, c))

    def ahead(self, value, far):
        return self.move(value, lambda q, y, x, c: ((q + far) % self.rest, y, x, c))

    def place(self):
        dp, fsdp = lax.axis_index("dp"), lax.axis_index("fsdp")
        rest = (dp // 2) * self.high + fsdp // 4
        return rest, dp % 2, (fsdp // 2) % 2, fsdp % 2


def double_rest(links, stack):
    while stack.shape[0] < links.rest:
        stack = jnp.concatenate([stack, links.ahead(stack, stack.shape[0])], axis=0)
    return stack


def spread_cores(links, near):
    return list(near) + [links.core(item) for item in near]


class Collect:
    def __init__(self, links, keep, give):
        self.links, self.keep = links, keep
        self.got = [links.core(item) for item in give]

    def add_cores(self):
        halves = [
            (keep.astype(F32) + got.astype(F32)).astype(BF16)
            for keep, got in zip(self.keep[:3], self.got[:3])
        ]
        self.halves = halves
        links = self.links
        self.near = [
            links.across(halves[0]),
            links.along_y(halves[1]),
            links.along_x(halves[2]),
        ]

    def add_chips(self):
        total = self.keep[3].astype(F32) + self.got[3].astype(F32)
        for item in self.near:
            total = total + item.astype(F32)
        self.total = total

    def direct(self):
        self.blocks = [self.total[far].astype(BF16) for far in range(1, self.links.rest)]
        self.ahead = [self.links.ahead(item, at + 1) for at, item in enumerate(self.blocks)]

    def halve(self):
        half = self.total.shape[0] // 2
        self.far = self.total[half:].astype(BF16)
        self.total = self.total[:half]
        self.back = self.links.ahead(self.far, half)

    def add_half(self):
        self.total = self.total + self.back.astype(F32)


class Blocks:
    def __init__(self, links, where):
        self.links = links
        self.rest, self.y, self.x, self.core = where[0], where[1], where[2], where[3]

    def device(self, other, flip_y, flip_x, far, sign):
        links = self.links
        core = jnp.bitwise_xor(self.core, other)
        rest = lax.rem(self.rest + (sign * far + links.rest), links.rest)
        x, y = jnp.bitwise_xor(self.x, flip_x), jnp.bitwise_xor(self.y, flip_y)
        dp = lax.div(rest, links.high) * 2 + y
        return dp, lax.rem(rest, links.high) * 2 + x, core

    def corner(self, rows, cols, *spot):
        dp, wide, core = self.device(*spot)
        return pl.multiple_of((dp * 2 + core) * rows, rows), pl.multiple_of(wide * cols, cols)


def load_weight(links, where, refs, first_col, cols, out, sem, steps=True):
    if len(refs) == 1:
        copies = [pltpu.make_async_copy(refs[0], out, sem)]
    else:
        blocks = Blocks(links, where)
        rows = refs[0].shape[1]
        copies = []
        for stack, far in itertools.product(range(8), range(links.rest)):
            other, high, low = stack // 4, (stack // 2) % 2, stack % 2
            if not steps:
                high, low = 1 - high, 1 - low
            else:
                core = jnp.bitwise_xor(blocks.core, other)
                high, low = jnp.where(core == 0, high, low), jnp.where(core == 0, low, high)
            row, col = blocks.corner(rows, cols, other, high, low, far, -1)
            copies.append(
                pltpu.make_async_copy(
                    refs[stack].at[far, :, pl.ds(first_col, cols)],
                    out.at[pl.ds(row, rows), pl.ds(col, cols)],
                    sem,
                )
            )
    for copy in copies:
        copy.start()
    return copies


def store_grad(links, where, grad, refs, first_col, cols, sem):
    if len(refs) == 1:
        copies = [pltpu.make_async_copy(grad, refs[0], sem)]
    else:
        blocks = Blocks(links, where)
        rows = refs[0].shape[1]
        copies = []
        for other, y, x, far in itertools.product(range(2), range(2), range(2), range(links.rest)):
            row, col = blocks.corner(rows, cols, other, y, x, far, 1)
            out = refs[4 * other + 3 - 2 * y - x].at[far]
            copies.append(
                pltpu.make_async_copy(
                    grad.at[pl.ds(row, rows), pl.ds(col, cols)],
                    out.at[:, pl.ds(first_col, cols)],
                    sem,
                )
            )
    for copy in copies:
        copy.start()
    return copies


def store_small(links, where, small, refs, first_col, sem):
    blocks = Blocks(links, where)
    copies = []
    for other, y, x, far in itertools.product(range(2), range(2), range(2), range(links.rest)):
        dp, wide, core = blocks.device(other, y, x, far, 1)
        target = refs[4 * other + 3 - 2 * y - x].at[far, pl.ds(0, 16), pl.ds(first_col, LANES)]
        source = small.at[dp * links.n_fsdp + wide * 2 + core]
        copies.append(pltpu.make_async_copy(source, target, sem))
    for copy in copies:
        copy.start()
    return copies


def wait_all(copies):
    for copy in copies:
        copy.wait()


def dot(left, right):
    return lax.dot_general(left, right, (((1,), (0,)), ((), ())), preferred_element_type=F32)


def dot_nt(left, right):
    return lax.dot_general(left, right, (((1,), (1,)), ((), ())), preferred_element_type=F32)


def dot_tn(left, right):
    return lax.dot_general(left, right, (((0,), (0,)), ((), ())), preferred_element_type=F32)


def normalize(hidden):
    centered = hidden - jnp.mean(hidden, axis=-1, keepdims=True)
    factor = lax.rsqrt(jnp.mean(centered * centered, axis=-1, keepdims=True) + EPS)
    return centered * factor, factor


def norm_back(scaled, normed, factor):
    return factor * (
        scaled
        - jnp.mean(scaled, axis=-1, keepdims=True)
        - normed * jnp.mean(scaled * normed, axis=-1, keepdims=True)
    )


def gelu_parts(value):
    bell = jnp.exp(-0.5 * value * value)
    weight = 0.5 + 0.5 * lax.erf(value * 0.7071067811865476)
    return value * weight, weight + value * (bell * 0.3989422804014327)


def piece_kernel(n_shards, where, *refs):
    mine, theirs = refs[:n_shards], refs[n_shards : 2 * n_shards]
    *extra, piece = refs[2 * n_shards :]
    core = where[3]
    half = mine[0].shape[0] // 2
    lines = []
    for keep, got in zip(mine, theirs):
        times = keep.shape[0] // 2 // half
        for at in range(times):
            row = pl.multiple_of(core * half * times + at * half, half)
            low, high = keep[pl.ds(row, half), :], got[pl.ds(row, half), :]
            lines += [jnp.where(core == 0, low, high), jnp.where(core == 0, high, low)]
    if extra:
        line = jnp.concatenate([item[...].astype(F32) for item in extra], axis=0)
        below = jnp.zeros((half - line.shape[0], line.shape[1]), F32)
        line = jnp.concatenate([line, below], axis=0)
        beside = jnp.zeros((line.shape[0], LANES - line.shape[1]), F32)
        lines.append(jnp.concatenate([line, beside], axis=1).astype(BF16))
    piece[...] = jnp.concatenate(lines, axis=1)


def small_kernel(links, where, *refs):
    stacks, vec_out, bias_out, held, sem = refs[:8], *refs[8:]
    blocks = Blocks(links, where)
    first_col = stacks[0].shape[2] - LANES
    copies = []
    for stack, far in itertools.product(range(8), range(links.rest)):
        dp, wide, core = blocks.device(stack // 4, 1 - (stack // 2) % 2, 1 - stack % 2, far, -1)
        copies.append(
            pltpu.make_async_copy(
                stacks[stack].at[far, pl.ds(0, 16), pl.ds(first_col, LANES)],
                held.at[dp * links.n_fsdp + wide * 2 + core],
                sem,
            )
        )
    for copy in copies:
        copy.start()
    wait_all(copies)
    rows, width = 8 // links.n_fsdp, vec_out.shape[1] // links.n_dp
    got = [held[at].astype(F32)[:, :width] for at in range(links.n_dp * links.n_fsdp)]
    for fsdp in range(links.n_fsdp):
        line = jnp.concatenate([got[dp * links.n_fsdp + fsdp] for dp in range(links.n_dp)], axis=1)
        vec_out[pl.ds(rows * fsdp, rows), :] = line[:rows]
    bias_out[...] = jnp.concatenate(got, axis=1)[rows : rows + 1]


def head_half(pair, half):
    lane = lax.broadcasted_iota(jnp.int32, pair.shape, 1)
    keep = (lane < HEAD_DIM) if half == 0 else (lane >= HEAD_DIM)
    return jnp.where(keep, pair, jnp.zeros_like(pair))


def group_spots(step, pairs, seq):
    spots = []
    for at in range(GROUP):
        number = step * GROUP + at
        sent, pair = lax.div(number, pairs), lax.rem(number, pairs)
        rows = pl.ds(pl.multiple_of(sent * seq, seq), seq)
        spots.append((sent, rows, pl.multiple_of(pair * LANES, LANES)))
    return spots


def join_halves(low, high):
    lane = lax.broadcasted_iota(jnp.int32, low.shape, 1)
    return jnp.where(lane < HEAD_DIM, low, high)


def attend_kernel(links, n_weight, where, lengths, tokens, vec, *refs):
    weight_refs = refs[:n_weight]
    qkv, attended, w_qkv, sem = refs[n_weight:]
    width = tokens.shape[1]
    seq = 256
    sents = tokens.shape[0] // seq
    wide = width * 3 * 2 // links.n_fsdp
    wait_all(load_weight(links, where, weight_refs, 0, wide, w_qkv, sem, steps=False))
    for tile in range(3 * width // 256):
        at = pl.ds(tile * 256, 256)
        product = dot(tokens[...], w_qkv[:, at])
        if tile * 256 < width:
            product = product + vec[0:1, at]
        elif tile * 256 >= 2 * width:
            product = product + vec[1:2, pl.ds(tile * 256 - 2 * width, 256)]
        qkv[:, at] = product.astype(BF16)

    pairs = width // LANES

    def attend(step, carry):
        spots = group_spots(step, pairs, seq)
        scores = []
        for sent, rows, col in spots:
            queries = qkv[rows, pl.ds(col, LANES)] * jnp.asarray(HEAD_DIM ** (-0.5), BF16)
            keys = qkv[rows, pl.ds(col + width, LANES)]
            keep = lax.broadcasted_iota(jnp.int32, (seq, seq), 1) < lengths[sent]
            for half in range(2):
                scores.append(jnp.where(keep, dot_nt(head_half(queries, half), keys), MASKED))
        tops = [jnp.max(item, axis=-1, keepdims=True) for item in scores]
        exponents = [jnp.exp(item - top) for item, top in zip(scores, tops)]
        scales = [1.0 / jnp.sum(item, axis=-1, keepdims=True) for item in exponents]
        probs = [(item * scale).astype(BF16) for item, scale in zip(exponents, scales)]
        for at, (sent, rows, col) in enumerate(spots):
            values = qkv[rows, pl.ds(col + 2 * width, LANES)]
            low, high = (dot(probs[2 * at + half], values) for half in range(2))
            attended[rows, pl.ds(col, LANES)] = join_halves(low, high).astype(BF16)
        return carry

    lax.fori_loop(0, sents * pairs // GROUP, attend, 0)


def up_kernel(links, n_weight, where, attended, tokens, vec, bias, *refs):
    up_refs = refs[:n_weight]
    out_refs = refs[n_weight : 2 * n_weight]
    activated, slope, first_norm, normed, factor = refs[2 * n_weight : 2 * n_weight + 5]
    w_up, w_out, even, odd, sems = refs[2 * n_weight + 5 :]
    width, hidden = w_up.shape
    tile = even.shape[1]
    count = hidden // tile
    wide = hidden * 2 // links.n_fsdp
    copies_out = load_weight(
        links, where, out_refs, wide, width * 2 // links.n_fsdp, w_out, sems.at[1]
    )
    copies = load_weight(links, where, up_refs, 0, wide, w_up, sems.at[0])
    wait_all(copies_out)
    for part in range(tokens.shape[0] // 256):
        rows = pl.ds(part * 256, 256)
        total = tokens[rows, :].astype(F32) + (dot(attended[rows, :], w_out[...]) + vec[2:3, :])
        unit, scale = normalize(total)
        normed[rows, :] = unit.astype(BF16)
        factor[rows, :] = jnp.broadcast_to(scale, (256, LANES))
        first_norm[rows, :] = (unit * vec[3:4, :] + vec[4:5, :]).astype(BF16)
    wait_all(copies)

    def place(step):
        return pl.ds(pl.multiple_of(step * tile, tile), tile)

    def fill(held, step):
        held[...] = dot(first_norm[...], w_up[:, place(step)])

    def drain(held, step):
        at = place(step)
        act, der = gelu_parts(held[...] + bias[:, at])
        activated[:, at] = act.astype(BF16)
        slope[:, at] = der.astype(BF16)

    fill(even, 0)

    def body(step, carry):
        fill(odd, 2 * step + 1)
        drain(even, 2 * step)
        fill(even, lax.rem(2 * step + 2, count))
        drain(odd, 2 * step + 1)
        return carry

    lax.fori_loop(0, count // 2, body, 0)


def down_kernel(links, n_weight, n_grad, where, lengths, depth, prefix, *refs):
    activated, first_norm, tokens, cotangent, vec = refs[:5]
    weight_refs = refs[5 : 5 + n_weight]
    layer_out, pooled, d_down, sums = refs[5 + n_weight : 9 + n_weight]
    grad_refs = refs[9 + n_weight : 9 + n_weight + n_grad]
    w_down, grad, sems = refs[9 + n_weight + n_grad :]
    hidden, width = w_down.shape
    seq = 256
    sents = tokens.shape[0] // seq
    cols = width * 2 // links.n_fsdp
    wait_all(load_weight(links, where, weight_refs, 0, cols, w_down, sems.at[0]))
    sums[...] = jnp.zeros_like(sums)
    columns = lax.broadcasted_iota(jnp.int32, (1, width), 1)
    for sent in range(sents):
        rows = pl.ds(sent * seq, seq)
        total = first_norm[rows, :].astype(F32) + (dot(activated[rows, :], w_down[...]) + vec[5:6, :])
        normed, factor = normalize(total)
        result = normed * vec[6:7, :] + vec[7:8, :]
        layer_out[rows, :] = result.astype(BF16)
        valid = lax.broadcasted_iota(jnp.int32, (seq, width), 0) < lengths[sent]
        source = jnp.where(depth[sent] == 1, result, tokens[rows, :].astype(F32))
        mean = jnp.sum(jnp.where(valid, source, 0.0), axis=0, keepdims=True)
        mean = mean / lengths[sent].astype(F32)
        for at in range(pooled.shape[1]):
            pooled[sent, pl.ds(at, 1), :] = mean * (columns < prefix[at]).astype(F32)
        grad_in = cotangent[rows, :].astype(F32)
        sums[6:7, :] += jnp.sum(grad_in * normed, axis=0, keepdims=True)
        sums[7:8, :] += jnp.sum(grad_in, axis=0, keepdims=True)
        back = norm_back(grad_in * vec[6:7, :], normed, factor)
        low = back.astype(BF16)
        d_down[rows, :] = low
        sums[5:6, :] += jnp.sum(low.astype(F32), axis=0, keepdims=True)

    for step in range(hidden // 768):
        at = pl.ds(step * 768, 768)
        grad[at, :] = dot_tn(activated[:, at], d_down[...]).astype(BF16)
    wait_all(store_grad(links, where, grad, grad_refs, 0, cols, sems.at[1]))


def up_back_kernel(links, n_weight, where, d_down, slope, first_norm, sums_in, *refs):
    weight_refs = refs[:n_weight]
    d_pre, sums, grad, w_down, turned, sem = refs[n_weight:]
    hidden, width = w_down.shape
    copies = load_weight(links, where, weight_refs, 0, width * 2 // links.n_fsdp, w_down, sem)
    sums[...] = sums_in[...]
    turned[...] = first_norm[...].T
    wait_all(copies)

    for step in range(hidden // 512):
        at = pl.ds(step * 512, 512)
        d_act = dot_nt(d_down[...], w_down[at, :])
        low = (d_act * slope[:, at].astype(F32)).astype(BF16)
        d_pre[:, at] = low
        line = jnp.sum(low.astype(F32), axis=0, keepdims=True)
        for part in range(2):
            row, col = divmod(step * 512 + part * 256, width)
            sums[pl.ds(8 + row, 1), pl.ds(col, 256)] = line[:, part * 256 : part * 256 + 256]
        grad[:, at] = dot(turned[...], low).astype(BF16)


def out_back_kernel(links, n_weight, n_grad, where, *refs):
    d_pre, d_down, normed, factor, attended, vec, sums_in, grad_up = refs[:8]
    up_refs = refs[8 : 8 + n_weight]
    out_refs = refs[8 + n_weight : 8 + 2 * n_weight]
    d_attn, d_att, sums = refs[8 + 2 * n_weight : 11 + 2 * n_weight]
    grad_refs = refs[11 + 2 * n_weight : 11 + 2 * n_weight + n_grad]
    w_up, w_out, grad_out, sems = refs[11 + 2 * n_weight + n_grad :]
    width, hidden = w_up.shape
    seq = 256
    wide = hidden * 2 // links.n_fsdp
    copies = load_weight(links, where, up_refs, 0, wide, w_up, sems.at[0])
    copies_out = load_weight(
        links, where, out_refs, wide, width * 2 // links.n_fsdp, w_out, sems.at[1]
    )
    if n_grad > 1:
        copies_up = store_grad(links, where, grad_up, grad_refs, 0, wide, sems.at[3])
    wait_all(copies)
    sums[...] = sums_in[...]
    for part in range(d_pre.shape[0] // seq):
        rows = pl.ds(part * seq, seq)
        d_first = dot_nt(d_pre[rows, :], w_up[...]) + d_down[rows, :].astype(F32)
        unit = normed[rows, :].astype(F32)
        sums[3:4, :] += jnp.sum(d_first * unit, axis=0, keepdims=True)
        sums[4:5, :] += jnp.sum(d_first, axis=0, keepdims=True)
        back = norm_back(d_first * vec[3:4, :], unit, factor[rows, 0:1])
        low = back.astype(BF16)
        d_attn[rows, :] = low
        sums[2:3, :] += jnp.sum(low.astype(F32), axis=0, keepdims=True)
    wait_all(copies_out)
    grad_out[...] = dot_tn(attended[...], d_attn[...]).astype(BF16)
    first = wide if n_grad > 1 else 0
    copies = store_grad(
        links, where, grad_out, grad_refs, first, width * 2 // links.n_fsdp, sems.at[2]
    )
    if n_grad > 1:
        copies += copies_up
    d_att[...] = dot_nt(d_attn[...], w_out[...]).astype(BF16)
    wait_all(copies)


def attend_back_kernel(links, n_grad, where, lengths, qkv, d_att, tokens, sums_in, *refs):
    d_qkv, sums = refs[:2]
    grad_refs = refs[2 : 2 + n_grad]
    turned, grad, held, small, sems = refs[2 + n_grad :]
    width = tokens.shape[1]
    seq = 256
    sents = tokens.shape[0] // seq
    pairs = width // LANES
    wide = width * 3 * 2 // links.n_fsdp
    turned[...] = tokens[...].T
    sums[...] = sums_in[...]
    key_scale = jnp.asarray(HEAD_DIM ** (-0.5), BF16)

    def body(step, carry):
        spots = group_spots(step, pairs, seq)
        loaded, scores, d_probs = [], [], []
        for sent, rows, col in spots:
            queries = qkv[rows, pl.ds(col, LANES)] * key_scale
            keys = qkv[rows, pl.ds(col + width, LANES)]
            values = qkv[rows, pl.ds(col + 2 * width, LANES)]
            d_out = d_att[rows, pl.ds(col, LANES)]
            loaded.append((queries, keys, d_out))
            keep = lax.broadcasted_iota(jnp.int32, (seq, seq), 0) < lengths[sent]
            for half in range(2):
                scores.append(jnp.where(keep, dot_nt(keys, head_half(queries, half)), MASKED))
                d_probs.append(dot_nt(values, head_half(d_out, half)))
        tops = [jnp.max(item, axis=0, keepdims=True) for item in scores]
        exponents = [jnp.exp(item - top) for item, top in zip(scores, tops)]
        scales = [1.0 / jnp.sum(item, axis=0, keepdims=True) for item in exponents]
        probs = [item * scale for item, scale in zip(exponents, scales)]
        row_dots = [jnp.sum(back * prob, axis=0, keepdims=True) for back, prob in zip(d_probs, probs)]
        d_scores = [
            (prob * (back - row_dot)).astype(BF16)
            for prob, back, row_dot in zip(probs, d_probs, row_dots)
        ]
        for at, (sent, rows, col) in enumerate(spots):
            queries, keys, d_out = loaded[at]
            mine = (2 * at, 2 * at + 1)
            d_value = join_halves(*(dot(probs[one].astype(BF16), d_out) for one in mine))
            d_key = join_halves(*(dot(d_scores[one], queries) for one in mine))
            d_query = join_halves(*(dot_tn(d_scores[one], keys) for one in mine))
            d_query = (d_query * (HEAD_DIM ** (-0.5))).astype(BF16)
            d_value = d_value.astype(BF16)
            d_qkv[rows, pl.ds(col, LANES)] = d_query
            d_qkv[rows, pl.ds(col + width, LANES)] = d_key.astype(BF16)
            d_qkv[rows, pl.ds(col + 2 * width, LANES)] = d_value
            sums[0:1, pl.ds(col, LANES)] += jnp.sum(d_query.astype(F32), axis=0, keepdims=True)
            sums[1:2, pl.ds(col, LANES)] += jnp.sum(d_value.astype(F32), axis=0, keepdims=True)
        return carry

    lax.fori_loop(0, sents * pairs // GROUP, body, 0)
    copies = []
    if n_grad > 1:
        held[...] = jnp.zeros_like(held)
        per_device = 8 // links.n_fsdp
        line_rows, line_cols = sums.shape[0] - 8, width // links.n_dp
        for dp, fsdp in itertools.product(range(links.n_dp), range(links.n_fsdp)):
            at = dp * links.n_fsdp + fsdp
            rows = pl.ds(fsdp * per_device, per_device)
            held[at, :per_device, :line_cols] = sums[rows, pl.ds(dp * line_cols, line_cols)]
            first = at * line_cols
            row, col = 8 + first // width, first % width
            held[at, per_device : per_device + 1, :line_cols] = sums[pl.ds(row, 1), pl.ds(col, line_cols)]
        small[...] = held[...].astype(BF16)
        copies = store_small(links, where, small, grad_refs, wide, sems.at[1])
    for step in range(3 * width // 256):
        at = pl.ds(step * 256, 256)
        grad[:, at] = dot(turned[...], d_qkv[:, at]).astype(BF16)
    wait_all(copies + store_grad(links, where, grad, grad_refs, 0, wide, sems.at[0]))


def inputs_kernel(links, n_weight, where, d_qkv, d_attn, *refs):
    weight_refs = refs[:n_weight]
    grad_tokens, mark, w_qkv, sem = refs[n_weight:]
    mark[...] = jnp.zeros_like(mark)
    width = d_attn.shape[1]
    wide = width * 3 * 2 // links.n_fsdp
    wait_all(load_weight(links, where, weight_refs, 0, wide, w_qkv, sem, steps=False))
    for part in range(d_qkv.shape[0] // 256):
        rows = pl.ds(part * 256, 256)
        grad_tokens[rows, :] = (
            dot_nt(d_qkv[rows, :], w_qkv[...]) + d_attn[rows, :].astype(F32)
        ).astype(BF16)


def columns_kernel(plan, where, *refs):
    refs = list(refs)
    mine = where[3] == 0
    sums = []
    for n_parts, spans, extra in plan:
        total = refs.pop(0)[...]
        for _ in range(n_parts - 1):
            total = total + refs.pop(0)[...].astype(F32)
        sums.append(total)
    for total, (_, spans, extra) in zip(sums, plan):
        for first, last in spans:
            middle = (first + last) // 2
            low, high = total[:, first:middle], total[:, middle:last]
            refs.pop(0)[...] = jnp.where(mine, low, high)
            refs.pop(0)[...] = jnp.where(mine, high, low)
        if extra:
            refs.pop(0)[...] = total[:8, -extra:]


def rows_kernel(turned, where, *refs):
    count = len(refs) // 3
    mine = where[3] == 0
    for at in range(count):
        keep, got, out = refs[at], refs[count + at], refs[2 * count + at]
        half = keep.shape[0]
        low, high = jnp.where(mine, keep[...], got[...]), jnp.where(mine, got[...], keep[...])
        if at in turned:
            out[...] = jnp.concatenate([low.T, high.T], axis=1)
        else:
            out[:half, :] = low
            out[half:, :] = high


SMEM_SPEC = pl.BlockSpec(memory_space=pltpu.SMEM)
VMEM_SPEC = pl.BlockSpec(memory_space=pltpu.VMEM)
ANY_SPEC = pl.BlockSpec(memory_space=pl.ANY)


def call(body, name, outs, scratch, args, vmem, after=(), through=()):
    spec = {"s": SMEM_SPEC, "v": VMEM_SPEC, "a": ANY_SPEC}
    extra = [("a", v) for v in list(through) + list(after)]
    handed = [("a", v) for v in through]
    n_args, n_outs = len(args), len(outs)

    def run(*refs):
        rest = refs[n_args + len(extra) :]
        body(*refs[:n_args], *rest[:n_outs], *rest[n_outs + len(handed) :])

    return list(
        pl.pallas_call(
            run,
            name=name,
            out_shape=[jax.ShapeDtypeStruct(v.shape, v.dtype) for _, v in list(outs) + handed],
            in_specs=[spec[place] for place, _ in list(args) + extra],
            out_specs=[spec[place] for place, _ in list(outs) + handed],
            scratch_shapes=scratch,
            input_output_aliases={n_args + at: n_outs + at for at in range(len(handed))},
            compiler_params=pltpu.CompilerParams(vmem_limit_bytes=vmem * MIB),
            cost_estimate=pl.CostEstimate(flops=1, bytes_accessed=1, transcendentals=0),
        )(*[value for _, value in list(args) + extra])
    )


def hold(arrays, after):
    return call(lambda: None, "hold", [], [], [], 1, after=after, through=arrays)


def owned(links, where, items, turned):
    outs, pairs = [], []
    for parts, spans, extra in items:
        rows = parts[0].shape[0]
        for first, last in spans:
            pairs.append(len(outs))
            outs += 2 * [("v", shaped(rows, (last - first) // 2, dtype=F32))]
        if extra:
            outs.append(("v", shaped(8, extra, dtype=F32)))
    pieces = call(
        partial(columns_kernel, [(len(parts), spans, extra) for parts, spans, extra in items]),
        "columns",
        outs,
        [],
        [("s", where)] + [("v", part) for parts, _, _ in items for part in parts],
        5,
    )
    keep = [pieces[at] for at in pairs]
    got = [links.core(pieces[at + 1]) for at in pairs]
    rows_out = call(
        partial(rows_kernel, turned),
        "rows",
        [
            ("v", shaped(*shape[:: -1 if at in turned else 1], dtype=F32))
            for at, shape in enumerate((2 * item.shape[0], item.shape[1]) for item in keep)
        ],
        [],
        [("s", where)] + [("v", item) for item in keep + got],
        4,
    )
    return rows_out + [item for at, item in enumerate(pieces) if at not in pairs and at - 1 not in pairs]


def shaped(*shape, dtype=BF16):
    return jax.ShapeDtypeStruct(shape, dtype)


def local(
    n_dp,
    n_fsdp,
    tokens,
    qkv_weight,
    out_weight,
    up_weight,
    up_bias,
    down_weight,
    vectors,
    lengths,
    exit_depth,
    prefix_widths,
    cotangent,
):
    sent_count, seq_len, width = tokens.shape
    rows = sent_count * seq_len
    hidden = up_weight.shape[1] * n_fsdp
    links = Links(n_dp, n_fsdp)
    where = jnp.stack(links.place()).astype(jnp.int32)
    inputs = tokens.reshape(rows, width)
    grad_in = cotangent.reshape(rows, width)
    blocked = qkv_weight.shape[0] % 32 == 0 and out_weight.shape[1] % 64 == 0

    if blocked:
        half = qkv_weight.shape[0] // 2
        parts = down_weight.shape[0] // 2 // half

        def chip_piece(name, shards, extra=(), after=()):
            wide = 2 * sum(item.size for item in shards) // (2 * half)
            theirs = [links.core(item) for item in shards]
            return call(
                partial(piece_kernel, len(shards)),
                name,
                [("v", shaped(half, wide + (LANES if extra else 0)))],
                [],
                [("s", where)] + [("v", item) for item in (*shards, *theirs, *extra)],
                3,
                after=after,
            )[0]

        small = jnp.concatenate([vectors, up_bias.reshape(1, -1)], axis=0)
        piece_in = chip_piece("in_piece", [qkv_weight], [small])
        far_in = [links.ahead(piece_in, far) for far in range(1, links.rest)]
        own_in = jnp.stack([piece_in] + far_in)
        piece_up = chip_piece(
            "up_piece", [up_weight, out_weight, down_weight], after=far_in[:1]
        )
        (piece_up,) = hold([piece_up], [own_in])
        pair = jnp.stack([piece_up, links.ahead(piece_up, 1)])
        split = 2 * (up_weight.shape[1] + out_weight.shape[1])
        up_pair = pair[:, :, :split]
        down_pair = jnp.concatenate(jnp.split(pair[:, :, split:], parts, axis=2), axis=1)
        own_up_stack = double_rest(links, up_pair)
        near_in = [links.across(own_in), links.along_y(own_in), links.along_x(own_in), own_in]
        (down_pair,) = hold([down_pair], [own_up_stack])
        down_far = links.ahead(down_pair, 2)
        up_first, up_second = links.first(own_up_stack), links.second(own_up_stack)
        any_in = [("a", item) for item in spread_cores(links, near_in)]
        vec, bias = call(
            partial(small_kernel, links),
            "small_values",
            [("v", shaped(8, width, dtype=F32)), ("v", shaped(1, hidden, dtype=F32))],
            [pltpu.VMEM((n_dp * n_fsdp, 16, LANES), BF16), pltpu.SemaphoreType.DMA],
            [("s", where)] + any_in,
            3,
            after=[own_up_stack],
        )
    else:

        def whole(shard):
            part = lax.all_gather(shard, "fsdp", axis=1, tiled=True)
            return lax.all_gather(part, "dp", axis=0, tiled=True)

        any_in, any_out, any_up, any_down = (
            [("a", whole(shard))] for shard in (qkv_weight, out_weight, up_weight, down_weight)
        )
        vec = lax.all_gather(vectors, "fsdp", axis=0, tiled=True)
        vec = lax.all_gather(vec, "dp", axis=1, tiled=True).astype(F32)
        bias = lax.all_gather(up_bias, ("dp", "fsdp"), axis=0, tiled=True)
        bias = bias.astype(F32).reshape(1, hidden)
    n_weight = len(any_in)
    n_grad = 8 if blocked else 1

    def grad_outs(shard, *more, extra=0):
        if not blocked:
            return [("a", shaped(shard.shape[0] * n_dp, shard.shape[1] * n_fsdp))]
        cols = shard.shape[1] + sum(item.shape[1] for item in more)
        shape = (links.rest, shard.shape[0] // 2, 2 * cols + extra)
        return 8 * [("a", shaped(*shape))]

    small = shaped(8 + -(-hidden // width // 8) * 8, width, dtype=F32)
    one, two = pltpu.SemaphoreType.DMA, pltpu.SemaphoreType.DMA((2,))
    flat = shaped(rows, width)
    lined = ("s", where)

    def room(mib):
        return mib if blocked else 2 * mib

    qkv, attended = call(
        partial(attend_kernel, links, n_weight),
        "attend",
        [("v", shaped(rows, 3 * width)), ("v", flat)],
        [pltpu.VMEM((width, 3 * width), BF16), one],
        [lined, ("s", lengths), ("v", inputs), ("v", vec)] + any_in,
        room(13),
    )
    if blocked:
        up_first, up_second, down_far = hold([up_first, up_second, down_far], [attended])
        own_down_stack = double_rest(links, jnp.concatenate([down_pair, down_far], axis=0))
        up_both = links.second(up_first)
        down_first, down_second = links.first(own_down_stack), links.second(own_down_stack)
        near_up = [own_up_stack, up_first, up_second, up_both]
        any_up = [("a", item) for item in spread_cores(links, near_up)]
        any_out = any_up
    activated, slope, first_norm, normed, factor = call(
        partial(up_kernel, links, n_weight),
        "up",
        [
            ("v", shaped(rows, hidden)),
            ("v", shaped(rows, hidden)),
            ("v", flat),
            ("v", flat),
            ("v", shaped(rows, LANES, dtype=F32)),
        ],
        [pltpu.VMEM((width, hidden), BF16), pltpu.VMEM((width, width), BF16)]
        + [pltpu.VMEM((rows, 512), F32)] * 2
        + [two],
        [lined, ("v", attended), ("v", inputs), ("v", vec), ("v", bias)] + any_up + any_out,
        room(17),
        after=[down_first] if blocked else [],
    )
    if blocked:
        down_both = links.second(down_first)
        down_second, down_both = hold([down_second, down_both], [activated])
        near_down = [own_down_stack, down_first, down_second, down_both]
        any_down = [("a", item) for item in spread_cores(links, near_down)]
    down = call(
        partial(down_kernel, links, n_weight, n_grad),
        "down",
        [
            ("v", flat),
            ("v", shaped(sent_count, prefix_widths.shape[0], width, dtype=F32)),
            ("v", flat),
            ("v", small),
        ]
        + grad_outs(down_weight),
        [pltpu.VMEM((hidden, width), BF16), pltpu.VMEM((hidden, width), BF16), two],
        [lined, ("s", lengths), ("s", exit_depth), ("s", prefix_widths)]
        + [("v", activated), ("v", first_norm), ("v", inputs), ("v", grad_in), ("v", vec)]
        + any_down,
        room(19),
    )
    layer_out, pooled, d_down, sums_down = down[:4]
    grad_down = down[4:]
    if blocked:
        sum_down = Collect(links, grad_down[:4], grad_down[4:])
        sum_down.add_cores()

    d_pre, sums_up, grad_up = call(
        partial(up_back_kernel, links, n_weight),
        "up_back",
        [("v", shaped(rows, hidden)), ("v", small), ("v", shaped(width, hidden))],
        [pltpu.VMEM((hidden, width), BF16), pltpu.VMEM((width, rows), BF16), one],
        [lined, ("v", d_down), ("v", slope), ("v", first_norm), ("v", sums_down)] + any_down,
        room(16),
        after=sum_down.halves if blocked else [],
    )
    d_attn, d_att, sums_out, *grad_out = call(
        partial(out_back_kernel, links, n_weight, n_grad),
        "out_back",
        [("v", flat), ("v", flat), ("v", small)]
        + (grad_outs(up_weight, out_weight) if blocked else grad_outs(out_weight)),
        [
            pltpu.VMEM((width, hidden), BF16),
            pltpu.VMEM((width, width), BF16),
            pltpu.VMEM((width, width), BF16),
            pltpu.SemaphoreType.DMA((4,)),
        ],
        [lined]
        + [("v", item) for item in (d_pre, d_down, normed, factor, attended, vec, sums_up, grad_up)]
        + any_up
        + any_out,
        room(17),
    )
    if blocked:
        sum_up = Collect(links, grad_out[:4], hold(grad_out[4:], sum_down.near))
        sum_up.add_cores()
        sum_down.add_chips()
        sum_down.halve()
    attend_back = call(
        partial(attend_back_kernel, links, n_grad),
        "attend_back",
        [("v", shaped(rows, 3 * width)), ("v", small)]
        + grad_outs(qkv_weight, extra=LANES),
        [
            pltpu.VMEM((width, rows), BF16),
            pltpu.VMEM((width, 3 * width), BF16),
            pltpu.VMEM((n_dp * n_fsdp, 16, LANES), F32),
            pltpu.VMEM((n_dp * n_fsdp, 16, LANES), BF16),
            two,
        ],
        [lined, ("s", lengths), ("v", qkv), ("v", d_att), ("v", inputs), ("v", sums_out)],
        room(17),
        after=sum_up.halves + [sum_down.far] if blocked else [],
    )
    d_qkv, sums_in = attend_back[:2]
    grad_in_blocks = attend_back[2:]
    if blocked:
        (sum_down.back,) = hold([sum_down.back], [sums_in])
        sum_down.add_half()
        sum_down.halve()
    grad_tokens, mark = call(
        partial(inputs_kernel, links, n_weight),
        "inputs",
        [("v", flat), ("v", shaped(8, LANES, dtype=F32))],
        [pltpu.VMEM((width, 3 * width), BF16), one],
        [lined, ("v", d_qkv), ("v", d_attn)] + any_in,
        room(10),
        after=[sum_down.far] if blocked else [],
    )

    if blocked:
        sum_up.add_chips()
        sum_up.halve()
        passed = hold(grad_in_blocks[4:] + [sum_down.back], [mark, sum_up.far])
        give, (sum_down.back,) = passed[:4], passed[4:]
        sum_in = Collect(links, grad_in_blocks[:4], give)
        sum_in.add_cores()
        (sum_up.back,) = hold([sum_up.back], sum_in.halves)
        sum_up.add_half()
        sum_up.halve()
        *sum_in.near, sum_up.back = hold(sum_in.near + [sum_up.back], [])
        sum_in.add_chips()
        sum_in.direct()
        sum_up.back, sum_down.back = hold([sum_up.back, sum_down.back], sum_in.blocks)
        for item in (sum_up, sum_down):
            item.add_half()
            while item.total.shape[0] > 1:
                item.halve()
                item.add_half()
        wide = 2 * qkv_weight.shape[1]
        split, total = 2 * up_weight.shape[1], 2 * (up_weight.shape[1] + out_weight.shape[1])
        own_qkv, own_up, own_out, own_down, last = owned(
            links,
            where,
            [
                ([sum_in.total[0]] + sum_in.ahead, [(0, wide)], LANES),
                ([sum_up.total[0]], [(0, split), (split, total)], 0),
                ([sum_down.total[0]], [(0, 2 * down_weight.shape[1])], 0),
            ],
            turned=(3,),
        )
        own_down = own_down.T
        own_vec = last[: vectors.shape[0], : vectors.shape[1]]
        own_bias = last[vectors.shape[0], : up_bias.shape[0]]
    else:

        def scattered(grad):
            part = lax.psum_scatter(grad, "dp", scatter_dimension=0, tiled=True)
            part = lax.psum_scatter(part, "fsdp", scatter_dimension=1, tiled=True)
            return part.astype(F32)

        own_down, own_up, own_out, own_qkv = (
            scattered(item) for item in (grad_down[0], grad_up, grad_out[0], grad_in_blocks[0])
        )
        every = lax.psum(sums_in, ("dp", "fsdp"))
        dp, fsdp = lax.axis_index("dp"), lax.axis_index("fsdp")
        own_vec = lax.dynamic_slice(
            every, (fsdp * vectors.shape[0], dp * vectors.shape[1]), vectors.shape
        )
        own_bias = lax.dynamic_slice_in_dim(
            every[8:].reshape(-1), (dp * n_fsdp + fsdp) * up_bias.shape[0], up_bias.shape[0], 0
        )
    return (
        layer_out.reshape(tokens.shape),
        pooled,
        grad_tokens.reshape(tokens.shape),
        own_qkv,
        own_out,
        own_up,
        own_bias,
        own_down,
        own_vec,
    )


def solution(mesh):
    placed = (
        P(("dp", "fsdp"), None, None),
        P("dp", "fsdp"),
        P("dp", "fsdp"),
        P("dp", "fsdp"),
        P(("dp", "fsdp")),
        P("dp", "fsdp"),
        P("fsdp", "dp"),
        P(("dp", "fsdp")),
        P(("dp", "fsdp")),
        P(),
        P(("dp", "fsdp"), None, None),
    )
    return jax.shard_map(
        partial(local, mesh.shape["dp"], mesh.shape["fsdp"]),
        mesh=mesh,
        in_specs=placed,
        out_specs=(
            P(("dp", "fsdp"), None, None),
            P(("dp", "fsdp"), None, None),
            P(("dp", "fsdp"), None, None),
            P("dp", "fsdp"),
            P("dp", "fsdp"),
            P("dp", "fsdp"),
            P(("dp", "fsdp")),
            P("dp", "fsdp"),
            P("fsdp", "dp"),
        ),
        check_vma=False,
    )
```

```python
import itertools
from functools import partial

import jax
import jax.numpy as jnp
from jax import lax
from jax.experimental import pallas as pl
from jax.experimental.pallas import tpu as pltpu
from jax.sharding import PartitionSpec as P

HEAD_DIM = 64
EPS = 1e-05
MASKED = -1000000000.0
F32 = jnp.float32
BF16 = jnp.bfloat16
MIB = 1024 * 1024
LANES = 128
GROUP = 3


class Links:
    def __init__(self, n_dp, n_fsdp):
        self.n_dp, self.n_fsdp = n_dp, n_fsdp
        self.high = n_fsdp // 4
        self.rest = (n_dp // 2) * self.high

    def number(self, rest, y, x, core):
        z, high = divmod(rest, self.high)
        return (z * 2 + y) * self.n_fsdp + (high * 2 + x) * 2 + core

    def pairs(self, step):
        return [
            (self.number(*place), self.number(*step(*place)))
            for place in itertools.product(range(self.rest), range(2), range(2), range(2))
        ]

    def move(self, value, step):
        return lax.ppermute(value, ("dp", "fsdp"), self.pairs(step))

    def core(self, value):
        return self.move(value, lambda q, y, x, c: (q, y, x, 1 - c))

    def along_x(self, value):
        return self.move(value, lambda q, y, x, c: (q, y, 1 - x, c))

    def along_y(self, value):
        return self.move(value, lambda q, y, x, c: (q, 1 - y, x, c))

    def across(self, value):
        return self.move(value, lambda q, y, x, c: (q, 1 - y, 1 - x, c))

    def first(self, value):
        return self.move(value, lambda q, y, x, c: (q, 1 - y, x, c) if c else (q, y, 1 - x, c))

    def second(self, value):
        return self.move(value, lambda q, y, x, c: (q, y, 1 - x, c) if c else (q, 1 - y, x, c))

    def flip(self, value, bit):
        return self.move(value, lambda q, y, x, c: (q ^ bit, y, x, c))

    def ahead(self, value, far):
        return self.move(value, lambda q, y, x, c: ((q + far) % self.rest, y, x, c))

    def place(self):
        dp, fsdp = lax.axis_index("dp"), lax.axis_index("fsdp")
        rest = (dp // 2) * self.high + fsdp // 4
        return rest, dp % 2, (fsdp // 2) % 2, fsdp % 2


def double_rest(links, stack):
    while stack.shape[0] < links.rest:
        stack = jnp.concatenate([stack, links.ahead(stack, stack.shape[0])], axis=0)
    return stack


def spread_cores(links, near):
    return list(near) + [links.core(item) for item in near]


class Collect:
    def __init__(self, links, keep, give):
        self.links, self.keep = links, keep
        self.got = [links.core(item) for item in give]

    def add_cores(self):
        halves = [
            (keep.astype(F32) + got.astype(F32)).astype(BF16)
            for keep, got in zip(self.keep[:3], self.got[:3])
        ]
        self.halves = halves
        links = self.links
        self.near = [
            links.across(halves[0]),
            links.along_y(halves[1]),
            links.along_x(halves[2]),
        ]

    def add_chips(self):
        total = self.keep[3].astype(F32) + self.got[3].astype(F32)
        for item in self.near:
            total = total + item.astype(F32)
        self.total = total

    def direct(self):
        self.blocks = [self.total[far].astype(BF16) for far in range(1, self.links.rest)]
        self.ahead = [self.links.ahead(item, at + 1) for at, item in enumerate(self.blocks)]

    def halve(self):
        half = self.total.shape[0] // 2
        self.far = self.total[half:].astype(BF16)
        self.total = self.total[:half]
        self.back = self.links.ahead(self.far, half)

    def add_half(self):
        self.total = self.total + self.back.astype(F32)


class Blocks:
    def __init__(self, links, where):
        self.links = links
        self.rest, self.y, self.x, self.core = where[0], where[1], where[2], where[3]

    def device(self, other, flip_y, flip_x, far, sign):
        links = self.links
        core = jnp.bitwise_xor(self.core, other)
        rest = lax.rem(self.rest + (sign * far + links.rest), links.rest)
        x, y = jnp.bitwise_xor(self.x, flip_x), jnp.bitwise_xor(self.y, flip_y)
        dp = lax.div(rest, links.high) * 2 + y
        return dp, lax.rem(rest, links.high) * 2 + x, core

    def corner(self, rows, cols, *spot):
        dp, wide, core = self.device(*spot)
        return pl.multiple_of((dp * 2 + core) * rows, rows), pl.multiple_of(wide * cols, cols)


def load_weight(links, where, refs, first_col, cols, out, sem, steps=True):
    if len(refs) == 1:
        copies = [pltpu.make_async_copy(refs[0], out, sem)]
    else:
        blocks = Blocks(links, where)
        rows = refs[0].shape[1]
        copies = []
        for stack, far in itertools.product(range(8), range(links.rest)):
            other, high, low = stack // 4, (stack // 2) % 2, stack % 2
            if not steps:
                high, low = 1 - high, 1 - low
            else:
                core = jnp.bitwise_xor(blocks.core, other)
                high, low = jnp.where(core == 0, high, low), jnp.where(core == 0, low, high)
            row, col = blocks.corner(rows, cols, other, high, low, far, -1)
            copies.append(
                pltpu.make_async_copy(
                    refs[stack].at[far, :, pl.ds(first_col, cols)],
                    out.at[pl.ds(row, rows), pl.ds(col, cols)],
                    sem,
                )
            )
    for copy in copies:
        copy.start()
    return copies


def store_grad(links, where, grad, refs, first_col, cols, sem):
    if len(refs) == 1:
        copies = [pltpu.make_async_copy(grad, refs[0], sem)]
    else:
        blocks = Blocks(links, where)
        rows = refs[0].shape[1]
        copies = []
        for other, y, x, far in itertools.product(range(2), range(2), range(2), range(links.rest)):
            row, col = blocks.corner(rows, cols, other, y, x, far, 1)
            out = refs[4 * other + 3 - 2 * y - x].at[far]
            copies.append(
                pltpu.make_async_copy(
                    grad.at[pl.ds(row, rows), pl.ds(col, cols)],
                    out.at[:, pl.ds(first_col, cols)],
                    sem,
                )
            )
    for copy in copies:
        copy.start()
    return copies


def store_tall(links, where, grad, small, refs, cols, sems):
    blocks = Blocks(links, where)
    rows = grad.shape[0] // (2 * links.n_dp)
    tiles = cols // LANES
    copies = []
    for other, y, x, far in itertools.product(range(2), range(2), range(2), range(links.rest)):
        dp, wide, core = blocks.device(other, y, x, far, 1)
        row, col = blocks.corner(rows, cols, other, y, x, far, 1)
        out = refs[4 * other + 3 - 2 * y - x].at[far]
        source = small.at[dp * links.n_fsdp + wide * 2 + core]
        copies.append(pltpu.make_async_copy(source, out.at[pl.ds(tiles * rows, 16)], sems.at[1]))
        for tile in range(tiles):
            at = pl.ds(pl.multiple_of(col + tile * LANES, LANES), LANES)
            source = grad.at[pl.ds(row, rows), at]
            target = out.at[pl.ds(tile * rows, rows)]
            copies.append(pltpu.make_async_copy(source, target, sems.at[0]))
    for copy in copies:
        copy.start()
    return copies


def wait_all(copies):
    for copy in copies:
        copy.wait()


def dot(left, right):
    return lax.dot_general(left, right, (((1,), (0,)), ((), ())), preferred_element_type=F32)


def dot_nt(left, right):
    return lax.dot_general(left, right, (((1,), (1,)), ((), ())), preferred_element_type=F32)


def dot_tn(left, right):
    return lax.dot_general(left, right, (((0,), (0,)), ((), ())), preferred_element_type=F32)


def normalize(hidden):
    centered = hidden - jnp.mean(hidden, axis=-1, keepdims=True)
    factor = lax.rsqrt(jnp.mean(centered * centered, axis=-1, keepdims=True) + EPS)
    return centered * factor, factor


def norm_back(scaled, normed, factor):
    return factor * (
        scaled
        - jnp.mean(scaled, axis=-1, keepdims=True)
        - normed * jnp.mean(scaled * normed, axis=-1, keepdims=True)
    )


def gelu_parts(value):
    bell = jnp.exp(-0.5 * value * value)
    weight = 0.5 + 0.5 * lax.erf(value * 0.7071067811865476)
    return value * weight, weight + value * (bell * 0.3989422804014327)


def piece_kernel(n_shards, where, *refs):
    mine, theirs = refs[:n_shards], refs[n_shards : 2 * n_shards]
    *extra, piece = refs[2 * n_shards :]
    core = where[3]
    half = mine[0].shape[0] // 2
    lines = []
    for keep, got in zip(mine, theirs):
        times = keep.shape[0] // 2 // half
        for at in range(times):
            row = pl.multiple_of(core * half * times + at * half, half)
            low, high = keep[pl.ds(row, half), :], got[pl.ds(row, half), :]
            lines += [jnp.where(core == 0, low, high), jnp.where(core == 0, high, low)]
    if extra:
        line = jnp.concatenate([item[...].astype(F32) for item in extra], axis=0)
        below = jnp.zeros((half - line.shape[0], line.shape[1]), F32)
        line = jnp.concatenate([line, below], axis=0)
        beside = jnp.zeros((line.shape[0], LANES - line.shape[1]), F32)
        lines.append(jnp.concatenate([line, beside], axis=1).astype(BF16))
    piece[...] = jnp.concatenate(lines, axis=1)


def small_kernel(links, where, *refs):
    stacks, vec_out, bias_out, held, sem = refs[:8], *refs[8:]
    blocks = Blocks(links, where)
    first_col = stacks[0].shape[2] - LANES
    copies = []
    for stack, far in itertools.product(range(8), range(links.rest)):
        dp, wide, core = blocks.device(stack // 4, 1 - (stack // 2) % 2, 1 - stack % 2, far, -1)
        copies.append(
            pltpu.make_async_copy(
                stacks[stack].at[far, pl.ds(0, 16), pl.ds(first_col, LANES)],
                held.at[dp * links.n_fsdp + wide * 2 + core],
                sem,
            )
        )
    for copy in copies:
        copy.start()
    wait_all(copies)
    rows, width = 8 // links.n_fsdp, vec_out.shape[1] // links.n_dp
    got = [held[at].astype(F32)[:, :width] for at in range(links.n_dp * links.n_fsdp)]
    for fsdp in range(links.n_fsdp):
        line = jnp.concatenate([got[dp * links.n_fsdp + fsdp] for dp in range(links.n_dp)], axis=1)
        vec_out[pl.ds(rows * fsdp, rows), :] = line[:rows]
    bias_out[...] = jnp.concatenate(got, axis=1)[rows : rows + 1]


def head_half(pair, half):
    lane = lax.broadcasted_iota(jnp.int32, pair.shape, 1)
    keep = (lane < HEAD_DIM) if half == 0 else (lane >= HEAD_DIM)
    return jnp.where(keep, pair, jnp.zeros_like(pair))


def group_spots(step, pairs, seq):
    spots = []
    for at in range(GROUP):
        number = step * GROUP + at
        sent, pair = lax.div(number, pairs), lax.rem(number, pairs)
        rows = pl.ds(pl.multiple_of(sent * seq, seq), seq)
        spots.append((sent, rows, pl.multiple_of(pair * LANES, LANES)))
    return spots


def join_halves(low, high):
    lane = lax.broadcasted_iota(jnp.int32, low.shape, 1)
    return jnp.where(lane < HEAD_DIM, low, high)


def attend_kernel(links, n_weight, where, lengths, tokens, vec, *refs):
    weight_refs = refs[:n_weight]
    qkv, attended, w_qkv, sem = refs[n_weight:]
    width = tokens.shape[1]
    seq = 256
    sents = tokens.shape[0] // seq
    wide = width * 3 * 2 // links.n_fsdp
    wait_all(load_weight(links, where, weight_refs, 0, wide, w_qkv, sem, steps=False))
    for tile in range(3 * width // 256):
        at = pl.ds(tile * 256, 256)
        product = dot(tokens[...], w_qkv[:, at])
        if tile * 256 < width:
            product = product + vec[0:1, at]
        elif tile * 256 >= 2 * width:
            product = product + vec[1:2, pl.ds(tile * 256 - 2 * width, 256)]
        qkv[:, at] = product.astype(BF16)

    pairs = width // LANES

    def attend(step, carry):
        spots = group_spots(step, pairs, seq)
        scores = []
        for sent, rows, col in spots:
            queries = qkv[rows, pl.ds(col, LANES)] * jnp.asarray(HEAD_DIM ** (-0.5), BF16)
            keys = qkv[rows, pl.ds(col + width, LANES)]
            keep = lax.broadcasted_iota(jnp.int32, (seq, seq), 1) < lengths[sent]
            for half in range(2):
                scores.append(jnp.where(keep, dot_nt(head_half(queries, half), keys), MASKED))
        tops = [jnp.max(item, axis=-1, keepdims=True) for item in scores]
        exponents = [jnp.exp(item - top) for item, top in zip(scores, tops)]
        scales = [1.0 / jnp.sum(item, axis=-1, keepdims=True) for item in exponents]
        probs = [(item * scale).astype(BF16) for item, scale in zip(exponents, scales)]
        for at, (sent, rows, col) in enumerate(spots):
            values = qkv[rows, pl.ds(col + 2 * width, LANES)]
            low, high = (dot(probs[2 * at + half], values) for half in range(2))
            attended[rows, pl.ds(col, LANES)] = join_halves(low, high).astype(BF16)
        return carry

    lax.fori_loop(0, sents * pairs // GROUP, attend, 0)


def up_kernel(links, n_weight, where, attended, tokens, vec, bias, *refs):
    up_refs = refs[:n_weight]
    out_refs = refs[n_weight : 2 * n_weight]
    activated, slope, first_norm, normed, factor = refs[2 * n_weight : 2 * n_weight + 5]
    w_up, w_out, even, odd, sems = refs[2 * n_weight + 5 :]
    width, hidden = w_up.shape
    tile = even.shape[1]
    count = hidden // tile
    wide = hidden * 2 // links.n_fsdp
    copies_out = load_weight(
        links, where, out_refs, wide, width * 2 // links.n_fsdp, w_out, sems.at[1]
    )
    copies = load_weight(links, where, up_refs, 0, wide, w_up, sems.at[0])
    wait_all(copies_out)
    for part in range(tokens.shape[0] // 256):
        rows = pl.ds(part * 256, 256)
        total = tokens[rows, :].astype(F32) + (dot(attended[rows, :], w_out[...]) + vec[2:3, :])
        unit, scale = normalize(total)
        normed[rows, :] = unit.astype(BF16)
        factor[rows, :] = jnp.broadcast_to(scale, (256, LANES))
        first_norm[rows, :] = (unit * vec[3:4, :] + vec[4:5, :]).astype(BF16)
    wait_all(copies)

    def place(step):
        return pl.ds(pl.multiple_of(step * tile, tile), tile)

    def fill(held, step):
        held[...] = dot(first_norm[...], w_up[:, place(step)])

    def drain(held, step):
        at = place(step)
        act, der = gelu_parts(held[...] + bias[:, at])
        activated[:, at] = act.astype(BF16)
        slope[:, at] = der.astype(BF16)

    fill(even, 0)

    def body(step, carry):
        fill(odd, 2 * step + 1)
        drain(even, 2 * step)
        fill(even, lax.rem(2 * step + 2, count))
        drain(odd, 2 * step + 1)
        return carry

    lax.fori_loop(0, count // 2, body, 0)


def down_kernel(links, n_weight, n_grad, where, lengths, depth, prefix, *refs):
    activated, first_norm, tokens, cotangent, vec = refs[:5]
    weight_refs = refs[5 : 5 + n_weight]
    layer_out, pooled, d_down, sums = refs[5 + n_weight : 9 + n_weight]
    grad_refs = refs[9 + n_weight : 9 + n_weight + n_grad]
    w_down, grad, sems = refs[9 + n_weight + n_grad :]
    hidden, width = w_down.shape
    seq = 256
    sents = tokens.shape[0] // seq
    cols = width * 2 // links.n_fsdp
    wait_all(load_weight(links, where, weight_refs, 0, cols, w_down, sems.at[0]))
    sums[...] = jnp.zeros_like(sums)
    columns = lax.broadcasted_iota(jnp.int32, (1, width), 1)
    for sent in range(sents):
        rows = pl.ds(sent * seq, seq)
        total = first_norm[rows, :].astype(F32) + (dot(activated[rows, :], w_down[...]) + vec[5:6, :])
        normed, factor = normalize(total)
        result = normed * vec[6:7, :] + vec[7:8, :]
        layer_out[rows, :] = result.astype(BF16)
        valid = lax.broadcasted_iota(jnp.int32, (seq, width), 0) < lengths[sent]
        source = jnp.where(depth[sent] == 1, result, tokens[rows, :].astype(F32))
        mean = jnp.sum(jnp.where(valid, source, 0.0), axis=0, keepdims=True)
        mean = mean / lengths[sent].astype(F32)
        for at in range(pooled.shape[1]):
            pooled[sent, pl.ds(at, 1), :] = mean * (columns < prefix[at]).astype(F32)
        grad_in = cotangent[rows, :].astype(F32)
        sums[6:7, :] += jnp.sum(grad_in * normed, axis=0, keepdims=True)
        sums[7:8, :] += jnp.sum(grad_in, axis=0, keepdims=True)
        back = norm_back(grad_in * vec[6:7, :], normed, factor)
        low = back.astype(BF16)
        d_down[rows, :] = low
        sums[5:6, :] += jnp.sum(low.astype(F32), axis=0, keepdims=True)

    for step in range(hidden // 768):
        at = pl.ds(step * 768, 768)
        grad[at, :] = dot_tn(activated[:, at], d_down[...]).astype(BF16)
    wait_all(store_grad(links, where, grad, grad_refs, 0, cols, sems.at[1]))


def up_back_kernel(links, n_weight, where, d_down, slope, first_norm, sums_in, *refs):
    weight_refs = refs[:n_weight]
    d_pre, sums, grad, w_down, turned, sem = refs[n_weight:]
    hidden, width = w_down.shape
    copies = load_weight(links, where, weight_refs, 0, width * 2 // links.n_fsdp, w_down, sem)
    sums[...] = sums_in[...]
    turned[...] = first_norm[...].T
    wait_all(copies)

    for step in range(hidden // 512):
        at = pl.ds(step * 512, 512)
        d_act = dot_nt(d_down[...], w_down[at, :])
        low = (d_act * slope[:, at].astype(F32)).astype(BF16)
        d_pre[:, at] = low
        line = jnp.sum(low.astype(F32), axis=0, keepdims=True)
        for part in range(2):
            row, col = divmod(step * 512 + part * 256, width)
            sums[pl.ds(8 + row, 1), pl.ds(col, 256)] = line[:, part * 256 : part * 256 + 256]
        grad[:, at] = dot(turned[...], low).astype(BF16)


def out_back_kernel(links, n_weight, n_grad, where, *refs):
    d_pre, d_down, normed, factor, attended, vec, sums_in, grad_up = refs[:8]
    up_refs = refs[8 : 8 + n_weight]
    out_refs = refs[8 + n_weight : 8 + 2 * n_weight]
    d_attn, d_att, sums = refs[8 + 2 * n_weight : 11 + 2 * n_weight]
    grad_refs = refs[11 + 2 * n_weight : 11 + 2 * n_weight + n_grad]
    w_up, w_out, grad_out, sems = refs[11 + 2 * n_weight + n_grad :]
    width, hidden = w_up.shape
    seq = 256
    wide = hidden * 2 // links.n_fsdp
    copies = load_weight(links, where, up_refs, 0, wide, w_up, sems.at[0])
    copies_out = load_weight(
        links, where, out_refs, wide, width * 2 // links.n_fsdp, w_out, sems.at[1]
    )
    if n_grad > 1:
        copies_up = store_grad(links, where, grad_up, grad_refs, 0, wide, sems.at[3])
    wait_all(copies)
    sums[...] = sums_in[...]
    for part in range(d_pre.shape[0] // seq):
        rows = pl.ds(part * seq, seq)
        d_first = dot_nt(d_pre[rows, :], w_up[...]) + d_down[rows, :].astype(F32)
        unit = normed[rows, :].astype(F32)
        sums[3:4, :] += jnp.sum(d_first * unit, axis=0, keepdims=True)
        sums[4:5, :] += jnp.sum(d_first, axis=0, keepdims=True)
        back = norm_back(d_first * vec[3:4, :], unit, factor[rows, 0:1])
        low = back.astype(BF16)
        d_attn[rows, :] = low
        sums[2:3, :] += jnp.sum(low.astype(F32), axis=0, keepdims=True)
    wait_all(copies_out)
    grad_out[...] = dot_tn(attended[...], d_attn[...]).astype(BF16)
    first = wide if n_grad > 1 else 0
    copies = store_grad(
        links, where, grad_out, grad_refs, first, width * 2 // links.n_fsdp, sems.at[2]
    )
    if n_grad > 1:
        copies += copies_up
    d_att[...] = dot_nt(d_attn[...], w_out[...]).astype(BF16)
    wait_all(copies)


def attend_back_kernel(links, n_grad, where, lengths, qkv, d_att, tokens, sums_in, *refs):
    d_qkv, sums = refs[:2]
    grad_refs = refs[2 : 2 + n_grad]
    turned, grad, held, small, sems = refs[2 + n_grad :]
    width = tokens.shape[1]
    seq = 256
    sents = tokens.shape[0] // seq
    pairs = width // LANES
    wide = width * 3 * 2 // links.n_fsdp
    turned[...] = tokens[...].T
    sums[...] = sums_in[...]
    key_scale = jnp.asarray(HEAD_DIM ** (-0.5), BF16)

    def body(step, carry):
        spots = group_spots(step, pairs, seq)
        loaded, scores, d_probs = [], [], []
        for sent, rows, col in spots:
            queries = qkv[rows, pl.ds(col, LANES)] * key_scale
            keys = qkv[rows, pl.ds(col + width, LANES)]
            values = qkv[rows, pl.ds(col + 2 * width, LANES)]
            d_out = d_att[rows, pl.ds(col, LANES)]
            loaded.append((queries, keys, d_out))
            keep = lax.broadcasted_iota(jnp.int32, (seq, seq), 0) < lengths[sent]
            for half in range(2):
                scores.append(jnp.where(keep, dot_nt(keys, head_half(queries, half)), MASKED))
                d_probs.append(dot_nt(values, head_half(d_out, half)))
        tops = [jnp.max(item, axis=0, keepdims=True) for item in scores]
        exponents = [jnp.exp(item - top) for item, top in zip(scores, tops)]
        scales = [1.0 / jnp.sum(item, axis=0, keepdims=True) for item in exponents]
        probs = [item * scale for item, scale in zip(exponents, scales)]
        row_dots = [jnp.sum(back * prob, axis=0, keepdims=True) for back, prob in zip(d_probs, probs)]
        d_scores = [
            (prob * (back - row_dot)).astype(BF16)
            for prob, back, row_dot in zip(probs, d_probs, row_dots)
        ]
        for at, (sent, rows, col) in enumerate(spots):
            queries, keys, d_out = loaded[at]
            mine = (2 * at, 2 * at + 1)
            d_value = join_halves(*(dot(probs[one].astype(BF16), d_out) for one in mine))
            d_key = join_halves(*(dot(d_scores[one], queries) for one in mine))
            d_query = join_halves(*(dot_tn(d_scores[one], keys) for one in mine))
            d_query = (d_query * (HEAD_DIM ** (-0.5))).astype(BF16)
            d_value = d_value.astype(BF16)
            d_qkv[rows, pl.ds(col, LANES)] = d_query
            d_qkv[rows, pl.ds(col + width, LANES)] = d_key.astype(BF16)
            d_qkv[rows, pl.ds(col + 2 * width, LANES)] = d_value
            sums[0:1, pl.ds(col, LANES)] += jnp.sum(d_query.astype(F32), axis=0, keepdims=True)
            sums[1:2, pl.ds(col, LANES)] += jnp.sum(d_value.astype(F32), axis=0, keepdims=True)
        return carry

    lax.fori_loop(0, sents * pairs // GROUP, body, 0)
    if n_grad > 1:
        held[...] = jnp.zeros_like(held)
        per_device = 8 // links.n_fsdp
        line_rows, line_cols = sums.shape[0] - 8, width // links.n_dp
        for dp, fsdp in itertools.product(range(links.n_dp), range(links.n_fsdp)):
            at = dp * links.n_fsdp + fsdp
            rows = pl.ds(fsdp * per_device, per_device)
            held[at, :per_device, :line_cols] = sums[rows, pl.ds(dp * line_cols, line_cols)]
            first = at * line_cols
            row, col = 8 + first // width, first % width
            held[at, per_device : per_device + 1, :line_cols] = sums[pl.ds(row, 1), pl.ds(col, line_cols)]
        small[...] = held[...].astype(BF16)
    for step in range(3 * width // 256):
        at = pl.ds(step * 256, 256)
        grad[:, at] = dot(turned[...], d_qkv[:, at]).astype(BF16)
    if n_grad > 1:
        wait_all(store_tall(links, where, grad, small, grad_refs, wide, sems))
    else:
        wait_all(store_grad(links, where, grad, grad_refs, 0, wide, sems.at[0]))


def inputs_kernel(links, n_weight, where, d_qkv, d_attn, *refs):
    weight_refs = refs[:n_weight]
    grad_tokens, mark, w_qkv, sem = refs[n_weight:]
    mark[...] = jnp.zeros_like(mark)
    width = d_attn.shape[1]
    wide = width * 3 * 2 // links.n_fsdp
    wait_all(load_weight(links, where, weight_refs, 0, wide, w_qkv, sem, steps=False))
    for part in range(d_qkv.shape[0] // 256):
        rows = pl.ds(part * 256, 256)
        grad_tokens[rows, :] = (
            dot_nt(d_qkv[rows, :], w_qkv[...]) + d_attn[rows, :].astype(F32)
        ).astype(BF16)


def columns_kernel(plan, where, *refs):
    refs = list(refs)
    mine = where[3] == 0
    sums = []
    for n_parts, spans, extra in plan:
        total = refs.pop(0)[...]
        for _ in range(n_parts - 1):
            total = total + refs.pop(0)[...].astype(F32)
        if extra:
            tiles = spans[-1][1] // LANES
            rows = (total.shape[0] - extra) // tiles
            parts = [total[at * rows : (at + 1) * rows] for at in range(tiles)]
            sums.append((jnp.concatenate(parts, axis=1), total[tiles * rows : tiles * rows + 8]))
        else:
            sums.append((total, None))
    for (total, last_rows), (_, spans, extra) in zip(sums, plan):
        for first, last in spans:
            middle = (first + last) // 2
            low, high = total[:, first:middle], total[:, middle:last]
            refs.pop(0)[...] = jnp.where(mine, low, high)
            refs.pop(0)[...] = jnp.where(mine, high, low)
        if extra:
            refs.pop(0)[...] = last_rows


def rows_kernel(turned, where, *refs):
    count = len(refs) // 3
    mine = where[3] == 0
    for at in range(count):
        keep, got, out = refs[at], refs[count + at], refs[2 * count + at]
        half = keep.shape[0]
        low, high = jnp.where(mine, keep[...], got[...]), jnp.where(mine, got[...], keep[...])
        if at in turned:
            out[...] = jnp.concatenate([low.T, high.T], axis=1)
        else:
            out[:half, :] = low
            out[half:, :] = high


SMEM_SPEC = pl.BlockSpec(memory_space=pltpu.SMEM)
VMEM_SPEC = pl.BlockSpec(memory_space=pltpu.VMEM)
ANY_SPEC = pl.BlockSpec(memory_space=pl.ANY)


def call(body, name, outs, scratch, args, vmem, after=(), through=()):
    spec = {"s": SMEM_SPEC, "v": VMEM_SPEC, "a": ANY_SPEC}
    extra = [("a", v) for v in list(through) + list(after)]
    handed = [("a", v) for v in through]
    n_args, n_outs = len(args), len(outs)

    def run(*refs):
        rest = refs[n_args + len(extra) :]
        body(*refs[:n_args], *rest[:n_outs], *rest[n_outs + len(handed) :])

    return list(
        pl.pallas_call(
            run,
            name=name,
            out_shape=[jax.ShapeDtypeStruct(v.shape, v.dtype) for _, v in list(outs) + handed],
            in_specs=[spec[place] for place, _ in list(args) + extra],
            out_specs=[spec[place] for place, _ in list(outs) + handed],
            scratch_shapes=scratch,
            input_output_aliases={n_args + at: n_outs + at for at in range(len(handed))},
            compiler_params=pltpu.CompilerParams(vmem_limit_bytes=vmem * MIB),
            cost_estimate=pl.CostEstimate(flops=1, bytes_accessed=1, transcendentals=0),
        )(*[value for _, value in list(args) + extra])
    )


def hold(arrays, after):
    return call(lambda: None, "hold", [], [], [], 1, after=after, through=arrays)


def owned(links, where, items, turned):
    outs, pairs = [], []
    for parts, spans, extra in items:
        rows = parts[0].shape[0]
        if extra:
            rows = (rows - extra) * LANES // spans[-1][1]
        for first, last in spans:
            pairs.append(len(outs))
            outs += 2 * [("v", shaped(rows, (last - first) // 2, dtype=F32))]
        if extra:
            outs.append(("v", shaped(8, LANES, dtype=F32)))
    pieces = call(
        partial(columns_kernel, [(len(parts), spans, extra) for parts, spans, extra in items]),
        "columns",
        outs,
        [],
        [("s", where)] + [("v", part) for parts, _, _ in items for part in parts],
        5,
    )
    keep = [pieces[at] for at in pairs]
    got = [links.core(pieces[at + 1]) for at in pairs]
    rows_out = call(
        partial(rows_kernel, turned),
        "rows",
        [
            ("v", shaped(*shape[:: -1 if at in turned else 1], dtype=F32))
            for at, shape in enumerate((2 * item.shape[0], item.shape[1]) for item in keep)
        ],
        [],
        [("s", where)] + [("v", item) for item in keep + got],
        4,
    )
    return rows_out + [item for at, item in enumerate(pieces) if at not in pairs and at - 1 not in pairs]


def shaped(*shape, dtype=BF16):
    return jax.ShapeDtypeStruct(shape, dtype)


def local(
    n_dp,
    n_fsdp,
    tokens,
    qkv_weight,
    out_weight,
    up_weight,
    up_bias,
    down_weight,
    vectors,
    lengths,
    exit_depth,
    prefix_widths,
    cotangent,
):
    sent_count, seq_len, width = tokens.shape
    rows = sent_count * seq_len
    hidden = up_weight.shape[1] * n_fsdp
    links = Links(n_dp, n_fsdp)
    where = jnp.stack(links.place()).astype(jnp.int32)
    inputs = tokens.reshape(rows, width)
    grad_in = cotangent.reshape(rows, width)
    blocked = qkv_weight.shape[0] % 32 == 0 and out_weight.shape[1] % 64 == 0

    if blocked:
        half = qkv_weight.shape[0] // 2
        parts = down_weight.shape[0] // 2 // half

        def chip_piece(name, shards, extra=(), after=()):
            wide = 2 * sum(item.size for item in shards) // (2 * half)
            theirs = [links.core(item) for item in shards]
            return call(
                partial(piece_kernel, len(shards)),
                name,
                [("v", shaped(half, wide + (LANES if extra else 0)))],
                [],
                [("s", where)] + [("v", item) for item in (*shards, *theirs, *extra)],
                3,
                after=after,
            )[0]

        small = jnp.concatenate([vectors, up_bias.reshape(1, -1)], axis=0)
        piece_in = chip_piece("in_piece", [qkv_weight], [small])
        far_in = [links.ahead(piece_in, far) for far in range(1, links.rest)]
        own_in = jnp.stack([piece_in] + far_in)
        piece_up = chip_piece(
            "up_piece", [up_weight, out_weight, down_weight], after=far_in[:1]
        )
        (piece_up,) = hold([piece_up], [own_in])
        pair = jnp.stack([piece_up, links.ahead(piece_up, 1)])
        split = 2 * (up_weight.shape[1] + out_weight.shape[1])
        up_pair = pair[:, :, :split]
        down_pair = jnp.concatenate(jnp.split(pair[:, :, split:], parts, axis=2), axis=1)
        own_up_stack = double_rest(links, up_pair)
        near_in = [links.across(own_in), links.along_y(own_in), links.along_x(own_in), own_in]
        (down_pair,) = hold([down_pair], [own_up_stack])
        down_far = links.ahead(down_pair, 2)
        up_first, up_second = links.first(own_up_stack), links.second(own_up_stack)
        any_in = [("a", item) for item in spread_cores(links, near_in)]
        vec, bias = call(
            partial(small_kernel, links),
            "small_values",
            [("v", shaped(8, width, dtype=F32)), ("v", shaped(1, hidden, dtype=F32))],
            [pltpu.VMEM((n_dp * n_fsdp, 16, LANES), BF16), pltpu.SemaphoreType.DMA],
            [("s", where)] + any_in,
            3,
            after=[own_up_stack],
        )
    else:

        def whole(shard):
            part = lax.all_gather(shard, "fsdp", axis=1, tiled=True)
            return lax.all_gather(part, "dp", axis=0, tiled=True)

        any_in, any_out, any_up, any_down = (
            [("a", whole(shard))] for shard in (qkv_weight, out_weight, up_weight, down_weight)
        )
        vec = lax.all_gather(vectors, "fsdp", axis=0, tiled=True)
        vec = lax.all_gather(vec, "dp", axis=1, tiled=True).astype(F32)
        bias = lax.all_gather(up_bias, ("dp", "fsdp"), axis=0, tiled=True)
        bias = bias.astype(F32).reshape(1, hidden)
    n_weight = len(any_in)
    n_grad = 8 if blocked else 1

    def grad_outs(shard, *more, tall=False):
        if not blocked:
            return [("a", shaped(shard.shape[0] * n_dp, shard.shape[1] * n_fsdp))]
        cols = shard.shape[1] + sum(item.shape[1] for item in more)
        shape = (links.rest, shard.shape[0] // 2, 2 * cols)
        if tall:
            shape = (links.rest, shape[1] * shape[2] // LANES + 16, LANES)
        return 8 * [("a", shaped(*shape))]

    small = shaped(8 + -(-hidden // width // 8) * 8, width, dtype=F32)
    one, two = pltpu.SemaphoreType.DMA, pltpu.SemaphoreType.DMA((2,))
    flat = shaped(rows, width)
    lined = ("s", where)

    def room(mib):
        return mib if blocked else 2 * mib

    qkv, attended = call(
        partial(attend_kernel, links, n_weight),
        "attend",
        [("v", shaped(rows, 3 * width)), ("v", flat)],
        [pltpu.VMEM((width, 3 * width), BF16), one],
        [lined, ("s", lengths), ("v", inputs), ("v", vec)] + any_in,
        room(13),
    )
    if blocked:
        up_first, up_second, down_far = hold([up_first, up_second, down_far], [attended])
        own_down_stack = double_rest(links, jnp.concatenate([down_pair, down_far], axis=0))
        up_both = links.second(up_first)
        down_first, down_second = links.first(own_down_stack), links.second(own_down_stack)
        near_up = [own_up_stack, up_first, up_second, up_both]
        any_up = [("a", item) for item in spread_cores(links, near_up)]
        any_out = any_up
    activated, slope, first_norm, normed, factor = call(
        partial(up_kernel, links, n_weight),
        "up",
        [
            ("v", shaped(rows, hidden)),
            ("v", shaped(rows, hidden)),
            ("v", flat),
            ("v", flat),
            ("v", shaped(rows, LANES, dtype=F32)),
        ],
        [pltpu.VMEM((width, hidden), BF16), pltpu.VMEM((width, width), BF16)]
        + [pltpu.VMEM((rows, 512), F32)] * 2
        + [two],
        [lined, ("v", attended), ("v", inputs), ("v", vec), ("v", bias)] + any_up + any_out,
        room(17),
        after=[down_first] if blocked else [],
    )
    if blocked:
        down_both = links.second(down_first)
        down_second, down_both = hold([down_second, down_both], [activated])
        near_down = [own_down_stack, down_first, down_second, down_both]
        any_down = [("a", item) for item in spread_cores(links, near_down)]
    down = call(
        partial(down_kernel, links, n_weight, n_grad),
        "down",
        [
            ("v", flat),
            ("v", shaped(sent_count, prefix_widths.shape[0], width, dtype=F32)),
            ("v", flat),
            ("v", small),
        ]
        + grad_outs(down_weight),
        [pltpu.VMEM((hidden, width), BF16), pltpu.VMEM((hidden, width), BF16), two],
        [lined, ("s", lengths), ("s", exit_depth), ("s", prefix_widths)]
        + [("v", activated), ("v", first_norm), ("v", inputs), ("v", grad_in), ("v", vec)]
        + any_down,
        room(19),
    )
    layer_out, pooled, d_down, sums_down = down[:4]
    grad_down = down[4:]
    if blocked:
        sum_down = Collect(links, grad_down[:4], grad_down[4:])
        sum_down.add_cores()

    d_pre, sums_up, grad_up = call(
        partial(up_back_kernel, links, n_weight),
        "up_back",
        [("v", shaped(rows, hidden)), ("v", small), ("v", shaped(width, hidden))],
        [pltpu.VMEM((hidden, width), BF16), pltpu.VMEM((width, rows), BF16), one],
        [lined, ("v", d_down), ("v", slope), ("v", first_norm), ("v", sums_down)] + any_down,
        room(16),
        after=sum_down.halves if blocked else [],
    )
    d_attn, d_att, sums_out, *grad_out = call(
        partial(out_back_kernel, links, n_weight, n_grad),
        "out_back",
        [("v", flat), ("v", flat), ("v", small)]
        + (grad_outs(up_weight, out_weight) if blocked else grad_outs(out_weight)),
        [
            pltpu.VMEM((width, hidden), BF16),
            pltpu.VMEM((width, width), BF16),
            pltpu.VMEM((width, width), BF16),
            pltpu.SemaphoreType.DMA((4,)),
        ],
        [lined]
        + [("v", item) for item in (d_pre, d_down, normed, factor, attended, vec, sums_up, grad_up)]
        + any_up
        + any_out,
        room(17),
    )
    if blocked:
        sum_up = Collect(links, grad_out[:4], hold(grad_out[4:], sum_down.near))
        sum_up.add_cores()
        sum_down.add_chips()
        sum_down.halve()
    attend_back = call(
        partial(attend_back_kernel, links, n_grad),
        "attend_back",
        [("v", shaped(rows, 3 * width)), ("v", small)]
        + grad_outs(qkv_weight, tall=True),
        [
            pltpu.VMEM((width, rows), BF16),
            pltpu.VMEM((width, 3 * width), BF16),
            pltpu.VMEM((n_dp * n_fsdp, 16, LANES), F32),
            pltpu.VMEM((n_dp * n_fsdp, 16, LANES), BF16),
            two,
        ],
        [lined, ("s", lengths), ("v", qkv), ("v", d_att), ("v", inputs), ("v", sums_out)],
        room(17),
        after=sum_up.halves + [sum_down.far] if blocked else [],
    )
    d_qkv, sums_in = attend_back[:2]
    grad_in_blocks = attend_back[2:]
    if blocked:
        (sum_down.back,) = hold([sum_down.back], [sums_in])
        sum_down.add_half()
        sum_down.halve()
    grad_tokens, mark = call(
        partial(inputs_kernel, links, n_weight),
        "inputs",
        [("v", flat), ("v", shaped(8, LANES, dtype=F32))],
        [pltpu.VMEM((width, 3 * width), BF16), one],
        [lined, ("v", d_qkv), ("v", d_attn)] + any_in,
        room(10),
        after=[sum_down.far] if blocked else [],
    )

    if blocked:
        sum_up.add_chips()
        sum_up.halve()
        passed = hold(grad_in_blocks[4:] + [sum_down.back], [mark, sum_up.far])
        give, (sum_down.back,) = passed[:4], passed[4:]
        sum_in = Collect(links, grad_in_blocks[:4], give)
        sum_in.add_cores()
        (sum_up.back,) = hold([sum_up.back], sum_in.halves)
        sum_up.add_half()
        sum_up.halve()
        *sum_in.near, sum_up.back = hold(sum_in.near + [sum_up.back], [])
        sum_in.add_chips()
        sum_in.direct()
        sum_up.back, sum_down.back = hold([sum_up.back, sum_down.back], sum_in.blocks)
        for item in (sum_up, sum_down):
            item.add_half()
            while item.total.shape[0] > 1:
                item.halve()
                item.add_half()
        wide = 2 * qkv_weight.shape[1]
        split, total = 2 * up_weight.shape[1], 2 * (up_weight.shape[1] + out_weight.shape[1])
        own_qkv, own_up, own_out, own_down, last = owned(
            links,
            where,
            [
                ([sum_in.total[0]] + sum_in.ahead, [(0, wide)], 16),
                ([sum_up.total[0]], [(0, split), (split, total)], 0),
                ([sum_down.total[0]], [(0, 2 * down_weight.shape[1])], 0),
            ],
            turned=(3,),
        )
        own_down = own_down.T
        own_vec = last[: vectors.shape[0], : vectors.shape[1]]
        own_bias = last[vectors.shape[0], : up_bias.shape[0]]
    else:

        def scattered(grad):
            part = lax.psum_scatter(grad, "dp", scatter_dimension=0, tiled=True)
            part = lax.psum_scatter(part, "fsdp", scatter_dimension=1, tiled=True)
            return part.astype(F32)

        own_down, own_up, own_out, own_qkv = (
            scattered(item) for item in (grad_down[0], grad_up, grad_out[0], grad_in_blocks[0])
        )
        every = lax.psum(sums_in, ("dp", "fsdp"))
        dp, fsdp = lax.axis_index("dp"), lax.axis_index("fsdp")
        own_vec = lax.dynamic_slice(
            every, (fsdp * vectors.shape[0], dp * vectors.shape[1]), vectors.shape
        )
        own_bias = lax.dynamic_slice_in_dim(
            every[8:].reshape(-1), (dp * n_fsdp + fsdp) * up_bias.shape[0], up_bias.shape[0], 0
        )
    return (
        layer_out.reshape(tokens.shape),
        pooled,
        grad_tokens.reshape(tokens.shape),
        own_qkv,
        own_out,
        own_up,
        own_bias,
        own_down,
        own_vec,
    )


def solution(mesh):
    placed = (
        P(("dp", "fsdp"), None, None),
        P("dp", "fsdp"),
        P("dp", "fsdp"),
        P("dp", "fsdp"),
        P(("dp", "fsdp")),
        P("dp", "fsdp"),
        P("fsdp", "dp"),
        P(("dp", "fsdp")),
        P(("dp", "fsdp")),
        P(),
        P(("dp", "fsdp"), None, None),
    )
    return jax.shard_map(
        partial(local, mesh.shape["dp"], mesh.shape["fsdp"]),
        mesh=mesh,
        in_specs=placed,
        out_specs=(
            P(("dp", "fsdp"), None, None),
            P(("dp", "fsdp"), None, None),
            P(("dp", "fsdp"), None, None),
            P("dp", "fsdp"),
            P("dp", "fsdp"),
            P("dp", "fsdp"),
            P(("dp", "fsdp")),
            P("dp", "fsdp"),
            P("fsdp", "dp"),
        ),
        check_vma=False,
    )
```
